128 devices in a mesh: group: 4 (over y_lo, core), rep: 32 (over x, z, y_hi).
Axes of the slice: x: 4, y: 4 (y_hi: 2, y_lo: 2; y = y_hi * 2 + y_lo), z: 4, core: 2. Of those that a mesh axis runs over, the one named last changes fastest.
Arguments:
- tokens: bfloat16 [32, 1024, 768], P('rep', 'group'), may hold values from -6 to 6
- segments: int32 [32, 1024], P('rep', 'group'), may hold values from 0 to 4, as said below
- cotangent: bfloat16 [32, 1024, 768], P('rep', 'group'), may hold values from -6 to 6
- gain_in: bfloat16 [768], P('group'), may hold values from 0.5 to 1.5
- w_in: bfloat16 [768, 3352], P('group'), may hold values from -0.25 to 0.25
- kernel: bfloat16 [4, 1792], P(None, 'group'), may hold values from -3 to 3
- conv_bias: bfloat16 [1792], P('group'), may hold values from -1.5 to 1.5
- dt_bias: bfloat16 [24], P('group'), may hold values from -5 to -3
- a_log: bfloat16 [24], P('group'), may hold values from -6 to 0
- skip_gain: bfloat16 [24], P('group'), may hold values from 0.5 to 1.5
- gain_out: bfloat16 [1536], P('group'), may hold values from 0.5 to 1.5
- w_out: bfloat16 [1536, 768], P('group'), may hold values from -0.2 to 0.2
Outputs:
- layer_out: bfloat16 [32, 1024, 768], P('rep', 'group')
- grad_tokens: float32 [32, 1024, 768], P('rep', 'group')
- grad_gain_in: float32 [768], P('group')
- grad_w_in: float32 [768, 3352], P('group')
- grad_kernel: float32 [4, 1792], P(None, 'group')
- grad_conv_bias: float32 [1792], P('group')
- grad_dt_bias: float32 [24], P('group')
- grad_a_log: float32 [24], P('group')
- grad_skip_gain: float32 [24], P('group')
- grad_gain_out: float32 [1536], P('group')
- grad_w_out: float32 [1536, 768], P('group')
The draws below stay inside these ranges and needn't reach their ends.
Inputs may be any that keep to these rules, and one draw needn't show every extreme that they name: `segments`: along each sequence the numbers never fall.
All inputs are finite; a program needn't handle non-finite values.
Results may differ from the reference program's by a relative error of at most 0.024.
Values may be sent and summed in bfloat16 or wider, within the bound.
No kernel may reach another device: no remote copies, remote signals or barrier semaphores. Data moves between devices by JAX's collectives and lax.ppermute only.
A program may use at most 192 MiB of HBM per device.

```python
from functools import partial
import jax
import jax.numpy as jnp
from jax import lax

D = 768
NH = 24
HP = 64
NS = 128
KC = 4
DI = 1536
CW = 1792
PROJ = 3352
SPAN = 128
TOK_DEV = 256
LENGTH = 1024
SEQS = 32


def draw_segments(key, part):
    key = jax.random.fold_in(key, 7)
    keys = jax.random.split(key, 4)
    half_dev = TOK_DEV // 2
    start_doc = jax.random.randint(keys[0], (SEQS, 1), 2, half_dev + 1)
    early_cut = jax.random.randint(keys[1], (SEQS, 1), 1, start_doc)
    end_doc = LENGTH - jax.random.randint(keys[2], (SEQS, 1), 2, half_dev + 1)
    late_cut = jax.random.randint(keys[3], (SEQS, 1), end_doc + 1, LENGTH)
    positions = jnp.arange(LENGTH, dtype=jnp.int32)[None, :]
    labels = (positions >= early_cut).astype(jnp.int32) + (positions >= start_doc).astype(jnp.int32)
    labels = labels + (positions >= end_doc).astype(jnp.int32) + (positions >= late_cut).astype(jnp.int32)
    return labels.astype(jnp.int32)


def normal_part(key, shape, scale, limit):
    return jax.random.truncated_normal(key, -limit, limit, shape, jnp.float32) * scale


def draw_tokens(key, part):
    key = jax.random.fold_in(key, 11)
    values = normal_part(key, (SEQS, LENGTH, D), 1.0, 6.0)
    return values.astype(jnp.bfloat16)


def draw_cotangent(key, part):
    key = jax.random.fold_in(key, 13)
    values = normal_part(key, (SEQS, LENGTH, D), 1.0, 6.0)
    return values.astype(jnp.bfloat16)


def draw_w_in(key, part):
    key = jax.random.fold_in(key, 17)
    scale = 1.0 / D ** 0.5
    values = normal_part(key, (D, PROJ), scale, 6.0)
    return jnp.clip(values, -0.25, 0.25).astype(jnp.bfloat16)


def draw_w_out(key, part):
    key = jax.random.fold_in(key, 19)
    scale = 1.0 / DI ** 0.5
    values = normal_part(key, (DI, D), scale, 6.0)
    return jnp.clip(values, -0.19921875, 0.19921875).astype(jnp.bfloat16)


def draw_kernel(key, part):
    key = jax.random.fold_in(key, 23)
    values = normal_part(key, (KC, CW), 0.5, 6.0)
    return values.astype(jnp.bfloat16)


def draw_conv_bias(key, part):
    key = jax.random.fold_in(key, 29)
    values = normal_part(key, (CW,), 0.5, 3.0)
    return values.astype(jnp.bfloat16)


def steps_of(key, extent, cuts, low, largest):
    def one(axis_at, parts):
        draws = jax.random.uniform(jax.random.fold_in(jax.random.fold_in(key, 6), axis_at), (parts,), jnp.float32, low / len(cuts), largest / len(cuts))
        return jnp.repeat(jnp.exp(draws), extent[axis_at] // parts).reshape((-1,) + (1,) * (len(extent) - axis_at - 1))

    loudness = one(*cuts[0])
    for cut in cuts[1:]:
        loudness = loudness * one(*cut)
    return loudness


def setup_inputs(seed: int = 0) -> dict:
    seeds = jax.random.split(jax.random.key(seed), 13)
    return {
        "tokens": draw_tokens(jax.random.fold_in(seeds[12], 71), 0),
        "segments": draw_segments(jax.random.fold_in(seeds[12], 71), 0),
        "cotangent": draw_cotangent(jax.random.fold_in(seeds[12], 71), 0),
        "gain_in": jnp.clip(1.0 + 0.1 * jax.random.normal(seeds[3], (D,), jnp.float32), 0.5, 1.5).astype(jnp.bfloat16),
        "w_in": draw_w_in(jax.random.fold_in(seeds[12], 71), 0),
        "kernel": draw_kernel(jax.random.fold_in(seeds[12], 71), 0),
        "conv_bias": draw_conv_bias(jax.random.fold_in(seeds[12], 71), 0),
        "dt_bias": jnp.clip(-5.0 + 2.0 * jax.random.uniform(seeds[7], (NH,), jnp.float32) ** steps_of(seeds[7], (NH,), ((0, 4),), -0.2, 0.2), -5.0, -3.0).astype(jnp.bfloat16),
        "a_log": jnp.clip(-6.0 + 6.0 * jax.random.uniform(seeds[8], (NH,), jnp.float32) ** steps_of(seeds[8], (NH,), ((0, 4),), -0.2, 0.2), -6.0, 0.0).astype(jnp.bfloat16),
        "skip_gain": jnp.clip(0.5 + 1.0 * jax.random.uniform(seeds[9], (NH,), jnp.float32) ** steps_of(seeds[9], (NH,), ((0, 4),), -0.2, 0.2), 0.5, 1.5).astype(jnp.bfloat16),
        "gain_out": jnp.clip(1.0 + 0.1 * jax.random.normal(seeds[10], (DI,), jnp.float32), 0.5, 1.5).astype(jnp.bfloat16),
        "w_out": draw_w_out(jax.random.fold_in(seeds[12], 71), 0),
    }


epsilon = 1e-05
highest = lax.Precision.HIGHEST

@jax.custom_vjp
def low(v):
    return lax.optimization_barrier(v.astype(jnp.bfloat16)).astype(jnp.float32)

@jax.custom_vjp
def low_back(v):
    return v

def low_keep(v):
    return (low(v), None)

def low_pass(kept, grad):
    return (grad,)

def back_keep(v):
    return (v, None)

def back_low(kept, grad):
    return (low(grad),)
low.defvjp(low_keep, low_pass)
low_back.defvjp(back_keep, back_low)

def norm_rows(values, gain_values):
    return values * lax.rsqrt(lax.optimization_barrier(jnp.mean(values * values, axis=-1, keepdims=True)) + epsilon) * gain_values

def conv_silu(extended, extended_ids, kernel_values, bias_values, row_count):
    tap_count = kernel_values.shape[0]
    current = extended_ids[tap_count - 1:]
    summed = jnp.zeros((row_count, extended.shape[1]), extended.dtype) + bias_values[None, :]
    for offset in range(tap_count):
        window = lax.slice_in_dim(extended, offset, offset + row_count, axis=0)
        same_doc = (lax.slice_in_dim(extended_ids, offset, offset + row_count, axis=0) == current).astype(extended.dtype)
        summed = summed + window * kernel_values[offset][None, :] * same_doc[:, None]
    return jax.nn.silu(summed)

def ssd_block(rate_values, carried_in, block_items):
    state_now, prior_id = carried_in
    heads_x, b_rows, c_rows, step_rows, block_ids = block_items
    cumulated = jnp.cumsum(step_rows * rate_values[None, :], axis=0)
    block_len = block_ids.shape[0]
    positions = jnp.arange(block_len)
    allowed = (block_ids[:, None] == block_ids[None, :]) & (positions[:, None] >= positions[None, :])
    spread = jnp.minimum(cumulated[:, None, :] - cumulated[None, :, :], 0.0)
    decays = jnp.where(allowed[:, :, None], jnp.exp(spread), 0.0)
    scores = jnp.einsum('tn,sn->ts', c_rows, b_rows, precision=highest)
    mixing = decays * scores[:, :, None] * step_rows[None, :, :]
    inner_part = jnp.einsum('tsh,shp->thp', mixing, heads_x, precision=highest)
    linked = (block_ids == prior_id).astype(state_now.dtype)
    carried = jnp.exp(cumulated) * linked[:, None]
    outer_part = jnp.einsum('tn,hpn->thp', c_rows, state_now, precision=highest) * carried[:, :, None]
    last_id = block_ids[block_len - 1]
    tail_weights = jnp.where((block_ids == last_id)[:, None], jnp.exp(cumulated[block_len - 1][None, :] - cumulated), 0.0) * step_rows
    fresh_state = jnp.einsum('sh,shp,sn->hpn', tail_weights, heads_x, b_rows, precision=highest)
    state_next = carried[block_len - 1][:, None, None] * state_now + fresh_state
    return ((state_next, last_id), inner_part + outer_part)

def layer(inputs_f, gain_in, w_in, kernel, conv_bias, dt_bias, a_log, skip_gain, gain_out, w_out, seg_ids):
    seq_len = inputs_f.shape[0]
    normed = low(norm_rows(inputs_f, gain_in))
    projected = low(low_back(jnp.dot(normed, w_in, precision=highest, preferred_element_type=jnp.float32)))
    gate_rows = projected[:, :DI]
    extended = jnp.concatenate([jnp.zeros((KC - 1, CW), inputs_f.dtype), projected[:, DI:DI + CW]], axis=0)
    extended_ids = jnp.concatenate([jnp.full((KC - 1,), -1, jnp.int32), seg_ids.astype(jnp.int32)])
    conv_rows = conv_silu(extended, extended_ids, kernel, conv_bias, seq_len)
    heads_x = conv_rows[:, :DI].reshape(seq_len, NH, HP)
    b_rows = conv_rows[:, DI:DI + NS]
    c_rows = conv_rows[:, DI + NS:]
    step_rows = jax.nn.softplus(projected[:, DI + CW:] + dt_bias[None, :])
    rate_values = -jnp.exp(a_log)
    blocks = seq_len // SPAN
    pieces = (heads_x.reshape(blocks, SPAN, NH, HP), b_rows.reshape(blocks, SPAN, NS), c_rows.reshape(blocks, SPAN, NS), step_rows.reshape(blocks, SPAN, NH), seg_ids.astype(jnp.int32).reshape(blocks, SPAN))
    initial = (jnp.zeros((NH, HP, NS), inputs_f.dtype), jnp.array(-1, jnp.int32))
    _, outputs = lax.scan(jax.checkpoint(partial(ssd_block, rate_values)), initial, pieces)
    total_y = outputs.reshape(seq_len, NH, HP) + skip_gain[None, :, None] * heads_x
    gated = total_y.reshape(seq_len, DI) * jax.nn.silu(gate_rows)
    normed_out = low(norm_rows(gated, gain_out))
    return inputs_f + jnp.dot(normed_out, w_out, precision=highest, preferred_element_type=jnp.float32)

def reference(tokens, segments, cotangent, gain_in, w_in, kernel, conv_bias, dt_bias, a_log, skip_gain, gain_out, w_out):
    weights = tuple((weight_arg.astype(jnp.float32) for weight_arg in (gain_in, w_in, kernel, conv_bias, dt_bias, a_log, skip_gain, gain_out, w_out)))

    def one_sequence(totals, sequence_items):
        token_rows, seg_ids, cot_rows = sequence_items

        def forward(inputs_f, *params):
            return layer(inputs_f, *params, seg_ids)
        result, pullback = jax.vjp(forward, token_rows.astype(jnp.float32), *weights)
        gradients = pullback(cot_rows.astype(jnp.float32))
        new_totals = tuple((running + gradient for running, gradient in zip(totals, gradients[1:])))
        return (new_totals, (result.astype(jnp.bfloat16), gradients[0]))
    zeros_init = tuple((jnp.zeros_like(weight_arg) for weight_arg in weights))
    totals, (layer_out, grad_tokens) = lax.scan(one_sequence, zeros_init, (tokens, segments, cotangent))
    return (layer_out, grad_tokens) + totals
```

```python
import jax
import jax.numpy as jnp
import numpy as np
from jax import lax
from jax.experimental import pallas as pl
from jax.experimental.pallas import tpu as pltpu
from jax.sharding import PartitionSpec as P

D = 768
NH = 24
HP = 64
NS = 128
DI = 1536
CW = 1792
SPAN = 128
ROWS = 256
HL = 6
XW = HL * HP
CL = XW + 2 * NS
PW = XW + CL + 128
CHUNK = 288
epsilon = 1e-05
f32 = jnp.float32
bf16 = jnp.bfloat16
NN = ((1,), (0,))
NT = ((1,), (1,))
TN = ((0,), (0,))
vmem_bytes = 56 * 1024 * 1024


def mm(a, b, dims):
    return lax.dot_general(
        a.astype(bf16), b.astype(bf16), (dims, ((), ())), preferred_element_type=f32
    )


def mm_exact(a, b, dims):
    return lax.dot_general(
        a, b, (dims, ((), ())), preferred_element_type=f32, precision=lax.Precision.HIGHEST
    )


def to_columns(rows):
    short = SPAN - rows.shape[0]
    return jnp.concatenate([rows, jnp.zeros((short, SPAN), f32)], axis=0).T


def softplus(v):
    return jnp.maximum(v, 0.0) + jnp.log1p(jnp.exp(-jnp.abs(v)))


def over_lanes(column):
    return jnp.broadcast_to(column, (SPAN, SPAN))


def span_decays(dt_rows, rate, pos_rows):
    row_at = lax.broadcasted_iota(jnp.int32, (SPAN, SPAN), 0)
    lane_at = lax.broadcasted_iota(jnp.int32, (SPAN, SPAN), 1)
    pos = to_columns(pos_rows)
    step = softplus(dt_rows)
    cum = mm_exact((row_at >= lane_at).astype(f32), step * rate, NN)
    cum_t = cum.T
    step_t = step.T
    allowed = (over_lanes(pos[:, 0:1]) == pos_rows[0:1, :]) & (row_at >= lane_at)
    low = lane_at < HP
    cums = [over_lanes(cum[:, h : h + 1]) for h in range(HL)]
    linked = pos[:, 4:5]
    tail = pos[:, 5:6]
    carried, tails = [], []
    for p in range(HL // 2):
        both = jnp.where(low, cums[2 * p], cums[2 * p + 1])
        steps = jnp.where(
            low, over_lanes(step[:, 2 * p : 2 * p + 1]), over_lanes(step[:, 2 * p + 1 : 2 * p + 2])
        )
        carried.append(jnp.exp(both) * linked)
        tails.append(jnp.exp(both[SPAN - 1 :, :] - both) * tail * steps)

    def decay(h):
        return jnp.where(allowed, jnp.exp(jnp.minimum(cums[h] - cum_t[h : h + 1, :], 0.0)), 0.0)

    return pos, step, step_t, cum, decay, carried, tails, low


def pick(index, sources, target):
    for d, source in enumerate(sources):

        @pl.when(index == d)
        def _(source=source):
            target[...] = source[...]


def put(index, targets, value):
    for d, target in enumerate(targets):

        @pl.when(index == d)
        def _(target=target):
            target[...] = value


def forward_kernel(
    me, t0, t1, t2, t3, c0, c1, c2, c3, w0, w1, w2, w3,
    pos, gain_in, taps, bias, dtb, rate, skip, gain_out, w_out,
    w_full, normed, proj, v_out, states, y_out, dno_out, stats, o0, o1, o2, o3,
    tok, cot, state, ext,
):
    i = pl.program_id(0)
    g = me[0]

    @pl.when(i == 0)
    def _():
        for d, part in enumerate((w0, w1, w2, w3)):
            w_full[pl.ds(pl.multiple_of((g ^ d) * 192, 64), 192), :] = part[...]
        state[...] = jnp.zeros_like(state)
        ext[0:8, :] = jnp.zeros((8, CL), f32)

    pick(g ^ i, (t0, t1, t2, t3), tok)
    pick(g ^ i, (c0, c1, c2, c3), cot)
    x = tok[...].astype(f32)
    rms = lax.rsqrt(jnp.mean(x * x, axis=-1, keepdims=True) + epsilon)
    low_rows = (x * rms * gain_in[...]).astype(bf16)
    normed[...] = low_rows
    proj[...] = mm(low_rows, w_full[...], NN).astype(bf16)
    dno_out[...] = mm(cot[...], w_out[...], NT)
    ext[8 : 8 + ROWS, :] = proj[:, XW : XW + CL].astype(f32)
    weighted = []
    for s in range(ROWS // SPAN):
        at = s * SPAN
        rows = slice(at, at + SPAN)
        dt_rows = proj[rows, XW + CL :].astype(f32) + dtb[...]
        pos_rows = pos[s]
        cols, step, step_t, cum, decay, carried, tails, low = span_decays(
            dt_rows, rate[...], pos_rows
        )
        v = bias[...] + taps[3:4, :] * ext[8 + at : 8 + at + SPAN, :]
        for lag in range(1, 4):
            window = ext[8 + at - lag : 8 + at - lag + SPAN, :]
            v = v + (taps[3 - lag : 4 - lag, :] * cols[:, lag : lag + 1]) * window
        v_out[rows, :] = v
        conv = v * jax.nn.sigmoid(v)
        b_rows, c_rows = conv[:, XW : XW + NS], conv[:, XW + NS :]
        scores = mm(c_rows, b_rows, NT)
        states[s] = state[...]
        from_state = mm(c_rows, state[...], NN)
        ys, ends, decays_end = [], [], []
        for p in range(HL // 2):
            lanes = slice(p * SPAN, (p + 1) * SPAN)
            xp = conv[:, lanes]
            mixing = [
                decay(h) * scores * step_t[h : h + 1, :] for h in (2 * p, 2 * p + 1)
            ]
            inner = mm(
                jnp.concatenate(mixing, axis=1),
                jnp.concatenate([jnp.where(low, xp, 0.0), jnp.where(low, 0.0, xp)], axis=0),
                NN,
            )
            ys.append(inner + carried[p] * from_state[:, lanes] + skip[:, lanes] * xp)
            ends.append(tails[p] * xp)
            decays_end.append(carried[p][SPAN - 1 :, :])
        y = jnp.concatenate(ys, axis=1)
        y_out[rows, :] = y
        state[...] = jnp.concatenate(decays_end, axis=1) * state[...] + mm(
            b_rows, jnp.concatenate(ends, axis=1), TN
        )
        gate = proj[rows, :XW].astype(f32)
        gated = y * (gate * jax.nn.sigmoid(gate))
        scaled = gated * gain_out[...]
        weighted.append(scaled.astype(bf16))
        squares = jnp.sum(gated * gated, axis=-1, keepdims=True)
        products = jnp.sum(scaled * dno_out[rows, :], axis=-1, keepdims=True)
        lane_at = lax.broadcasted_iota(jnp.int32, (SPAN, SPAN), 1)
        both = jnp.where(lane_at == 0, squares, jnp.where(lane_at == 1, products, 0.0))
        stats[s] = both.T[0:8, :]
    ext[0:8, :] = ext[ROWS : ROWS + 8, :]
    branch = mm(jnp.concatenate(weighted, axis=0), w_out[...], NN)
    put(g ^ i, (o0, o1, o2, o3), branch.astype(bf16))


def split_sum(rows, ones):
    high = rows.astype(bf16)
    rest = rows - high.astype(f32)
    return mm(high, ones, NN) + mm(rest, ones, NN)


def backward_kernel(
    me, c0, c1, c2, c3, w_full, normed, proj, v_in, states, y_in, dno_in, stats,
    pos, taps, dtb, rate, skip, gain_out, ones,
    bundle, n0, n1, n2, n3,
    cot, d_state, ext, d_proj, normed_out, acc_in, acc_dt, acc_out, acc_small, small,
):
    i = pl.num_programs(0) - 1 - pl.program_id(0)
    g = me[0]

    @pl.when(pl.program_id(0) == 0)
    def _():
        for ref in (d_state, acc_in, acc_dt, acc_out, acc_small, small):
            ref[...] = jnp.zeros_like(ref)
        ext[ROWS:, :] = jnp.zeros((8, CL), f32)

    pick(g ^ i, (c0, c1, c2, c3), cot)
    row_at = lax.broadcasted_iota(jnp.int32, (SPAN, SPAN), 0)
    lane_at = lax.broadcasted_iota(jnp.int32, (SPAN, SPAN), 1)
    later = (row_at <= lane_at).astype(f32)

    def add(row, value):
        width = value.shape[1]
        acc_small[row : row + 1, :width] += value

    def down(value):
        return jnp.sum(value, axis=0, keepdims=True)

    for s in reversed(range(ROWS // SPAN)):
        at = s * SPAN
        rows = slice(at, at + SPAN)
        sums = to_columns(stats[s])
        rms = lax.rsqrt(sums[:, 0:1] * (1.0 / DI) + epsilon)
        mean = rms * rms * rms * sums[:, 1:2] * (1.0 / DI)
        gate = proj[rows, :XW].astype(f32)
        sig = jax.nn.sigmoid(gate)
        silu = gate * sig
        y = y_in[rows, :]
        gated = y * silu
        scaled = gated * rms
        normed_out[rows, :] = (scaled * gain_out[...]).astype(bf16)
        dno = dno_in[rows, :]
        add(0, down(dno * scaled))
        d_gated = rms * gain_out[...] * dno - gated * mean
        dy = d_gated * silu
        d_proj[rows, :XW] = (d_gated * y * (sig * (1.0 + gate * (1.0 - sig)))).astype(bf16)

        dt_rows = proj[rows, XW + CL :].astype(f32) + dtb[...]
        cols, step, step_t, cum, decay, carried, tails, low = span_decays(
            dt_rows, rate[...], pos[s]
        )
        v = v_in[rows, :]
        sig_v = jax.nn.sigmoid(v)
        conv = v * sig_v
        x, b_rows, c_rows = conv[:, :XW], conv[:, XW : XW + NS], conv[:, XW + NS :]
        add(1, down(dy * x))
        state = states[s]
        state_grad = d_state[...]
        scores = mm(c_rows, b_rows, NT)
        from_state = mm(c_rows, state, NN)
        from_grad = mm(b_rows, state_grad, NN)
        carried_all = jnp.concatenate(carried, axis=1)
        tails_all = jnp.concatenate(tails, axis=1)
        dy_carried = dy * carried_all
        x_tail = x * tails_all
        d_scores = jnp.zeros((SPAN, SPAN), f32)
        row_sums = jnp.zeros((SPAN, SPAN), f32)
        col_sums, dxs = [], []
        for p in range(HL // 2):
            lanes = slice(p * SPAN, (p + 1) * SPAN)
            xp, dyp = x[:, lanes], dy[:, lanes]
            halves = jnp.concatenate([jnp.where(low, dyp, 0.0), jnp.where(low, 0.0, dyp)], axis=0)
            d_mixing = mm(halves, xp, NT)
            mixing = []
            for k in range(2):
                h = 2 * p + k
                kept = decay(h)
                kept_step = kept * step_t[h : h + 1, :]
                mixing.append(kept_step * scores)
                d_mix = d_mixing[k * SPAN : (k + 1) * SPAN, :]
                d_scores = d_scores + d_mix * kept_step
                plain = d_mix * kept * scores
                col_sums.append(down(plain))
                row_sum = jnp.sum(plain * step_t[h : h + 1, :], axis=1, keepdims=True)
                row_sums = jnp.where(lane_at == h, row_sum, row_sums)
            inner = mm(jnp.concatenate(mixing, axis=0), halves, TN)
            dxs.append(inner + skip[:, lanes] * dyp + tails[p] * from_grad[:, lanes])
        dx = jnp.concatenate(dxs, axis=1)
        d_c = mm(d_scores, b_rows, NN) + mm(dy_carried, state, NT)
        d_b = mm(d_scores, c_rows, TN) + mm(x_tail, state_grad, NT)

        end_decay = carried_all[SPAN - 1 :, :]
        through = end_decay * down(state * state_grad)
        last = lax.broadcasted_iota(jnp.int32, (SPAN, XW), 0) == SPAN - 1
        from_start = split_sum(
            dy_carried * from_state + jnp.where(last, through, 0.0), ones[...]
        )
        to_end = split_sum(x * from_grad, ones[...])
        end_plain = jnp.exp(cum[SPAN - 1 :, :] - cum) * cols[:, 5:6]
        to_end_kept = to_end * end_plain
        to_end_step = to_end_kept * step
        col_sum = to_columns(jnp.concatenate(col_sums, axis=0))
        d_cum = row_sums - col_sum * step + from_start - to_end_step
        d_cum = d_cum + jnp.where(row_at == SPAN - 1, down(to_end_step), 0.0)
        d_log = mm_exact(later, d_cum, NN)
        d_step = col_sum + to_end_kept + rate[...] * d_log
        d_dt = d_step * jax.nn.sigmoid(dt_rows)
        add(2, down(d_dt))
        add(3, down(d_log * step) * rate[...])
        d_proj[rows, XW + CL :] = d_dt.astype(bf16)
        d_state[...] = end_decay * state_grad + mm(c_rows, dy_carried, TN)

        dv = jnp.concatenate([dx, d_b, d_c], axis=1) * (sig_v * (1.0 + v * (1.0 - sig_v)))
        ext[rows, :] = dv
        add(4, down(dv))
        conv_in = proj[rows, XW : XW + CL].astype(f32)
        add(8, down(dv * conv_in))
        d_conv = taps[3:4, :] * dv
        for lag in range(1, 4):
            window = ext[at + lag : at + lag + SPAN, :] * cols[:, 5 + lag : 6 + lag]
            d_conv = d_conv + taps[3 - lag : 4 - lag, :] * window
            add(8 - lag, down(window * conv_in))
        d_proj[rows, XW : XW + CL] = d_conv.astype(bf16)

    ext[ROWS:, :] = ext[0:8, :]
    d_normed = mm(d_proj[...], w_full[...], NT)
    put(g ^ i, (n0, n1, n2, n3), d_normed.astype(bf16))
    add(9, down(d_normed * normed[...].astype(f32)))
    acc_in[...] += mm(normed[...], d_proj[:, : XW + CL], TN)
    acc_dt[...] += mm(d_proj[:, XW + CL :], normed[...], TN)[0:8, :]
    acc_out[...] += mm(normed_out[...], cot[...], TN)

    @pl.when(i == 0)
    def _():
        for k in range(4):
            for tile in range(8):
                for q in range(4):
                    bundle[4 * tile + q, 48 * k : 48 * k + 48, :] = acc_in[
                        192 * k + 48 * q : 192 * k + 48 * q + 48, 128 * tile : 128 * tile + 128
                    ].astype(bf16)
            for h in range(HL):
                at = 16 * k + 2 * h
                small[at : at + 1, :] = acc_dt[h : h + 1, 192 * k : 192 * k + 128]
                small[at + 1 : at + 2, 0:64] = acc_dt[h : h + 1, 192 * k + 128 : 192 * k + 192]
        for piece in range(160):
            place = 192 + 16 * (piece % 5)
            if piece < 144:
                tile, q = piece // 24, piece % 24
                value = acc_out[16 * q : 16 * q + 16, 128 * tile : 128 * tile + 128].astype(bf16)
            else:
                value = jnp.zeros((16, 128), bf16)
            bundle[piece // 5, place : place + 16, :] = value

        def lay(start, row, tiles):
            for t in range(tiles):
                small[start + t : start + t + 1, :] = acc_small[
                    row : row + 1, 128 * t : 128 * t + 128
                ]

        for j in range(4):
            lay(64 + 5 * j, 5 + j, 5)
        lay(84, 4, 5)
        lay(89, 9, 6)
        lay(95, 0, 3)
        lay(98, 1, 3)
        lay(101, 2, 1)
        lay(102, 3, 1)
        for r in range(32):
            bundle[r, 272:288, :] = jnp.concatenate(
                [small[4 * r : 4 * r + 4, :], jnp.zeros((12, 128), f32)], axis=0
            ).astype(bf16)


def assemble_kernel(me, parts, grad_in, grad_out, small):
    g = me[0]
    for q in range(4):
        rows = slice(48 * q, 48 * q + 48)
        for tile in range(8):
            r = 4 * tile + q
            pieces = [parts[r, 48 * d : 48 * d + 48, :].astype(f32) for d in range(4)]
            if tile < 6:
                start = (tile // 3) * DI + (tile % 3) * 128
                for d in range(4):
                    column = pl.multiple_of(start + (g ^ d) * XW, 128)
                    grad_in[rows, pl.ds(column, 128)] = pieces[d]
            else:
                column = 2 * DI + (tile - 6) * 128
                grad_in[rows, column : column + 128] = (pieces[0] + pieces[1]) + (
                    pieces[2] + pieces[3]
                )
    grad_in[:, 2 * DI + 256 :] = jnp.zeros((192, NH), f32)
    for piece in range(144):
        tile, q = piece // 24, piece % 24
        place = 192 + 16 * (piece % 5)
        grad_out[16 * q : 16 * q + 16, 128 * tile : 128 * tile + 128] = parts[
            piece // 5, place : place + 16, :
        ].astype(f32)
    for r in range(32):
        values = parts[r, 272:288, :].astype(f32)
        for d in range(4):
            small[d, 4 * r : 4 * r + 4, :] = values[4 * d : 4 * d + 4, :]


def whole(shape):
    zeros = (0,) * len(shape)
    return pl.BlockSpec(shape, lambda i: zeros)


def blocked(shape, place):
    zeros = (0,) * (len(shape) - 1)
    return pl.BlockSpec(shape, lambda i: (place(i),) + zeros)


scalar_spec = pl.BlockSpec(memory_space=pltpu.SMEM)
params = pltpu.CompilerParams(
    vmem_limit_bytes=vmem_bytes, dimension_semantics=("arbitrary",)
)


def among(value, d):
    return lax.ppermute(value, "group", [(i, i ^ d) for i in range(4)])


def local(
    tokens, segments, cotangent, gain_in, w_in, kernel, conv_bias, dt_bias, a_log, skip_gain,
    gain_out, w_out,
):
    reps = lax.axis_size("rep")
    g = lax.axis_index("group")
    me = g.astype(jnp.int32).reshape(1)
    tok = tokens.reshape(ROWS, D)
    cot = cotangent.reshape(ROWS, D)

    t2 = among(tok, 2)
    t1 = among(tok, 1)
    columns = []
    for k in range(4):
        columns.append(
            jnp.concatenate(
                [
                    w_in[:, k * XW : (k + 1) * XW],
                    w_in[:, DI + k * XW : DI + (k + 1) * XW],
                    w_in[:, 2 * DI : DI + CW],
                    w_in[:, DI + CW + k * HL : DI + CW + (k + 1) * HL],
                    jnp.zeros((192, 128 - HL), bf16),
                ],
                axis=1,
            )
        )
    stacked = jnp.stack(columns)

    def share(d):
        return lax.dynamic_index_in_dim(stacked, g ^ d, 0, keepdims=False)

    def across(value, d):
        pairs = [(i * reps + r, (i ^ d) * reps + (r ^ 1)) for r in range(reps) for i in range(4)]
        return lax.ppermute(value, ("group", "rep"), pairs)

    w2, w3 = across(share(2), 2), across(share(3), 3)
    w1 = among(share(1), 1)
    w0 = share(0)
    c2 = among(cot, 2)
    c1 = among(cot, 1)
    t3 = among(t2, 1)
    c3 = among(c2, 1)

    packed = jnp.concatenate(
        [
            kernel.astype(f32).reshape(-1),
            conv_bias.astype(f32),
            gain_in.astype(f32),
            segments.reshape(-1).astype(f32),
        ]
    )
    gathered = lax.all_gather(packed, "group")
    taps_all = jnp.moveaxis(gathered[:, :CW].reshape(4, 4, 448), 0, 1).reshape(4, CW)
    both_all = jnp.concatenate([taps_all, gathered[:, CW : CW + 448].reshape(1, CW)], axis=0)
    both = jnp.concatenate(
        [lax.dynamic_slice_in_dim(both_all, g * XW, XW, axis=1), both_all[:, DI:]], axis=1
    )
    taps = jnp.concatenate([both[:4], jnp.zeros((4, CL), f32)], axis=0)
    bias = both[4:5]
    gain_in_all = gathered[:, CW + 448 : CW + 640].reshape(1, D)
    seg = gathered[:, CW + 640 :].reshape(-1)
    length = seg.shape[0]
    spans = length // SPAN
    before = jnp.concatenate([jnp.full((3,), -1.0, f32), seg])
    after = jnp.concatenate([seg, jnp.full((3,), -2.0, f32)])
    seg_rows = seg.reshape(spans, SPAN)
    ends = seg_rows[:, SPAN - 1 :]
    starts = jnp.concatenate([jnp.full((1, 1), -1.0, f32), ends[:-1]], axis=0)
    features = [seg_rows]
    features += [
        (before[3 - lag : 3 - lag + length] == seg).astype(f32).reshape(spans, SPAN)
        for lag in range(1, 4)
    ]
    features += [(seg_rows == starts).astype(f32), (seg_rows == ends).astype(f32)]
    features += [
        (after[lag : lag + length] == seg).astype(f32).reshape(spans, SPAN) for lag in range(1, 4)
    ]
    features += [jnp.zeros((spans, SPAN), f32)] * 7
    pos = jnp.stack(features, axis=1)

    dtb = jnp.pad(dt_bias.astype(f32), (0, 128 - HL)).reshape(1, 128)
    rate = jnp.pad(-jnp.exp(a_log.astype(f32)), (0, 128 - HL)).reshape(1, 128)
    skip = jnp.repeat(skip_gain.astype(f32), HP).reshape(1, XW)
    gain_o = gain_out.astype(f32).reshape(1, XW)

    blocks = 4
    part = whole((ROWS, D))

    def up(i):
        return i

    out_shapes = (
        jax.ShapeDtypeStruct((D, PW), bf16),
        jax.ShapeDtypeStruct((length, D), bf16),
        jax.ShapeDtypeStruct((length, PW), bf16),
        jax.ShapeDtypeStruct((length, CL), f32),
        jax.ShapeDtypeStruct((spans, NS, XW), f32),
        jax.ShapeDtypeStruct((length, XW), f32),
        jax.ShapeDtypeStruct((length, XW), f32),
        jax.ShapeDtypeStruct((spans, 8, SPAN), f32),
    ) + (jax.ShapeDtypeStruct((ROWS, D), bf16),) * 4
    (w_full, normed, proj, v_rows, states, y_rows, dno, stats, o0, o1, o2, o3) = pl.pallas_call(
        forward_kernel,
        grid=(blocks,),
        in_specs=[scalar_spec]
        + [part] * 8
        + [whole((192, PW))] * 4
        + [blocked((2, 16, SPAN), up)]
        + [
            whole((1, D)), whole((8, CL)), whole((1, CL)), whole((1, 128)), whole((1, 128)),
            whole((1, XW)), whole((1, XW)), whole((XW, D)),
        ],
        out_specs=[
            whole((D, PW)),
            blocked((ROWS, D), up),
            blocked((ROWS, PW), up),
            blocked((ROWS, CL), up),
            blocked((2, NS, XW), up),
            blocked((ROWS, XW), up),
            blocked((ROWS, XW), up),
            blocked((2, 8, SPAN), up),
        ]
        + [part] * 4,
        out_shape=out_shapes,
        scratch_shapes=[
            pltpu.VMEM((ROWS, D), bf16),
            pltpu.VMEM((ROWS, D), bf16),
            pltpu.VMEM((NS, XW), f32),
            pltpu.VMEM((ROWS + 8, CL), f32),
        ],
        compiler_params=params,
        name="forward",
    )(
        me, tok, t1, t2, t3, cot, c1, c2, c3, w0, w1, w2, w3,
        pos, gain_in_all, taps, bias, dtb, rate, skip, gain_o, w_out,
    )

    stats = lax.psum(stats, "group")
    branches = [o0, among(o1, 1), among(o2, 2), among(o3, 3)]

    def down(i):
        return blocks - 1 - i

    ones = jnp.asarray(np.arange(XW)[:, None] // HP == np.arange(128)[None, :], bf16)
    bundle, n0, n1, n2, n3 = pl.pallas_call(
        backward_kernel,
        grid=(blocks,),
        in_specs=[scalar_spec]
        + [part] * 4
        + [
            whole((D, PW)),
            blocked((ROWS, D), down),
            blocked((ROWS, PW), down),
            blocked((ROWS, CL), down),
            blocked((2, NS, XW), down),
            blocked((ROWS, XW), down),
            blocked((ROWS, XW), down),
            blocked((2, 8, SPAN), down),
            blocked((2, 16, SPAN), down),
            whole((8, CL)), whole((1, 128)), whole((1, 128)), whole((1, XW)), whole((1, XW)),
            whole((XW, 128)),
        ],
        out_specs=[whole((32, CHUNK, 128))] + [part] * 4,
        out_shape=(jax.ShapeDtypeStruct((32, CHUNK, 128), bf16),)
        + (jax.ShapeDtypeStruct((ROWS, D), bf16),) * 4,
        scratch_shapes=[
            pltpu.VMEM((ROWS, D), bf16),
            pltpu.VMEM((NS, XW), f32),
            pltpu.VMEM((ROWS + 8, CL), f32),
            pltpu.VMEM((ROWS, PW), bf16),
            pltpu.VMEM((ROWS, XW), bf16),
            pltpu.VMEM((D, XW + CL), f32),
            pltpu.VMEM((8, D), f32),
            pltpu.VMEM((XW, D), f32),
            pltpu.VMEM((16, D), f32),
            pltpu.VMEM((128, 128), f32),
        ],
        compiler_params=params,
        name="backward",
    )(
        me, cot, c1, c2, c3, w_full, normed, proj, v_rows, states, y_rows, dno, stats,
        pos, taps, dtb, rate, skip, gain_o, ones,
    )

    d_parts = [n0, among(n1, 1), among(n2, 2), among(n3, 3)]
    x = tok.astype(f32)
    squares = lax.dynamic_slice_in_dim(stats[:, 0, :].reshape(-1), g * ROWS, ROWS, axis=0)
    rms_out = lax.rsqrt(squares * (1.0 / DI) + epsilon)[:, None]
    branch = sum(value.astype(f32) for value in branches)
    layer_out = (x + rms_out * branch).astype(bf16).reshape(tokens.shape)
    d_normed = sum(value.astype(f32) for value in d_parts)
    rms_in = lax.rsqrt(jnp.mean(x * x, axis=-1, keepdims=True) + epsilon)
    scaled = d_normed * gain_in_all
    grad_tokens = (
        cot.astype(f32)
        + rms_in * scaled
        - x * (rms_in * rms_in * rms_in * jnp.mean(x * scaled, axis=-1, keepdims=True))
    ).reshape(tokens.shape)

    received = lax.all_to_all(bundle, "rep", 0, 0, tiled=True)
    reduced = jnp.sum(received.astype(f32), axis=0).astype(bf16)
    for_members = reduced[:192].reshape(4, 48, 128)
    small_part = reduced[272:276]
    pieces, smalls = [], []
    for d in range(4):
        piece = lax.dynamic_index_in_dim(for_members, g ^ d, 0, keepdims=False)
        both = jnp.concatenate([piece, small_part], axis=0)
        both = both if d == 0 else among(both, d)
        pieces.append(both[:48])
        smalls.append(both[48:])
    payload = jnp.concatenate(pieces + [reduced[192:272]] + smalls, axis=0)
    parts = lax.all_to_all(
        jnp.broadcast_to(payload[None], (reps, CHUNK, 128)), "rep", 0, 0, tiled=True
    )
    grad_w_in, grad_w_out, small = pl.pallas_call(
        assemble_kernel,
        in_specs=[scalar_spec, pl.BlockSpec(memory_space=pltpu.VMEM)],
        out_specs=[pl.BlockSpec(memory_space=pltpu.VMEM)] * 3,
        out_shape=(
            jax.ShapeDtypeStruct((192, 3352), f32),
            jax.ShapeDtypeStruct((XW, D), f32),
            jax.ShapeDtypeStruct((4, 128, 128), f32),
        ),
        compiler_params=pltpu.CompilerParams(vmem_limit_bytes=vmem_bytes),
        name="assemble",
    )(me, parts)
    own = small[0]
    ordered = small[jnp.arange(4) ^ g]
    mine = lax.dynamic_slice_in_dim(ordered, g * 16, 16, axis=1)[:, : 2 * HL]
    dt_grad = mine.reshape(NH, 256)[:, :192].T
    grad_w_in = lax.dynamic_update_slice(grad_w_in, dt_grad, (0, DI + CW))
    conv = ordered[:, 64:89].reshape(4, 5, CL)
    conv_x = jnp.moveaxis(conv[:, :, :XW], 0, 1).reshape(5, DI)
    conv_all = jnp.concatenate([conv_x, jnp.sum(conv[:, :, XW:], axis=0)], axis=1)
    conv_mine = lax.dynamic_slice_in_dim(conv_all, g * 448, 448, axis=1)
    gain_in_sum = jnp.sum(small[:, 89:95], axis=0).reshape(-1) / gain_in_all[0]
    grad_gain_in = lax.dynamic_slice_in_dim(gain_in_sum, g * 192, 192, axis=0)
    grad_gain_out = own[95:98].reshape(-1)
    grad_skip = jnp.sum(own[98:101].reshape(HL, HP), axis=1)
    return (
        layer_out,
        grad_tokens,
        grad_gain_in,
        grad_w_in,
        conv_mine[:4],
        conv_mine[4],
        own[101, :HL],
        own[102, :HL],
        grad_skip,
        grad_gain_out,
        grad_w_out,
    )


def solution(mesh):
    sequences = P("rep", "group", None)
    vector = P("group")
    matrix = P("group", None)
    return jax.shard_map(
        local,
        mesh=mesh,
        in_specs=(
            sequences, P("rep", "group"), sequences, vector, matrix, P(None, "group"),
            vector, vector, vector, vector, vector, matrix,
        ),
        out_specs=(
            sequences, sequences, vector, matrix, P(None, "group"), vector, vector, vector,
            vector, vector, matrix,
        ),
        check_vma=False,
    )
```

```python
import jax
import jax.numpy as jnp
import numpy as np
from jax import lax
from jax.experimental import pallas as pl
from jax.experimental.pallas import tpu as pltpu
from jax.sharding import PartitionSpec as P

D = 768
NH = 24
HP = 64
NS = 128
DI = 1536
CW = 1792
SPAN = 128
ROWS = 256
HL = 6
XW = HL * HP
CL = XW + 2 * NS
PW = XW + CL + 128
epsilon = 1e-05
f32 = jnp.float32
bf16 = jnp.bfloat16
NN = ((1,), (0,))
NT = ((1,), (1,))
TN = ((0,), (0,))
vmem_bytes = 56 * 1024 * 1024


def mm(a, b, dims):
    return lax.dot_general(
        a.astype(bf16), b.astype(bf16), (dims, ((), ())), preferred_element_type=f32
    )


def mm_exact(a, b, dims):
    return lax.dot_general(
        a, b, (dims, ((), ())), preferred_element_type=f32, precision=lax.Precision.HIGHEST
    )


def to_columns(rows):
    short = SPAN - rows.shape[0]
    return jnp.concatenate([rows, jnp.zeros((short, SPAN), f32)], axis=0).T


def softplus(v):
    return jnp.maximum(v, 0.0) + jnp.log1p(jnp.exp(-jnp.abs(v)))


def over_lanes(column):
    return jnp.broadcast_to(column, (SPAN, SPAN))


def span_decays(dt_rows, rate, pos_rows):
    row_at = lax.broadcasted_iota(jnp.int32, (SPAN, SPAN), 0)
    lane_at = lax.broadcasted_iota(jnp.int32, (SPAN, SPAN), 1)
    pos = to_columns(pos_rows)
    step = softplus(dt_rows)
    cum = mm_exact((row_at >= lane_at).astype(f32), step * rate, NN)
    cum_t = cum.T
    step_t = step.T
    allowed = (over_lanes(pos[:, 0:1]) == pos_rows[0:1, :]) & (row_at >= lane_at)
    low = lane_at < HP
    cums = [over_lanes(cum[:, h : h + 1]) for h in range(HL)]
    linked = pos[:, 4:5]
    tail = pos[:, 5:6]
    carried, tails = [], []
    for p in range(HL // 2):
        both = jnp.where(low, cums[2 * p], cums[2 * p + 1])
        steps = jnp.where(
            low, over_lanes(step[:, 2 * p : 2 * p + 1]), over_lanes(step[:, 2 * p + 1 : 2 * p + 2])
        )
        carried.append(jnp.exp(both) * linked)
        tails.append(jnp.exp(both[SPAN - 1 :, :] - both) * tail * steps)

    def decay(h):
        return jnp.where(allowed, jnp.exp(jnp.minimum(cums[h] - cum_t[h : h + 1, :], 0.0)), 0.0)

    return pos, step, step_t, cum, decay, carried, tails, low


def pick(index, sources, target):
    for d, source in enumerate(sources):

        @pl.when(index == d)
        def _(source=source):
            target[...] = source[...]


def put(index, own, pair, across, value):
    low, high = pair.at[0:ROWS, :], pair.at[ROWS : 2 * ROWS, :]
    for d, target in enumerate((own, low, across, high)):

        @pl.when(index == d)
        def _(target=target):
            target[...] = value


def columns_kernel(me, w_in, tok, taps, bias, gain_in, seg, w0, w1, w2, w3, out, rows):
    g = me[0]
    for d, send in enumerate((w0, w1, w2, w3)):
        start = (g ^ d) * XW
        send[:, :XW] = w_in[:, pl.ds(pl.multiple_of(start, 128), XW)]
        send[:, XW : 2 * XW] = w_in[:, pl.ds(pl.multiple_of(DI + start, 128), XW)]
        send[:, 2 * XW : XW + CL] = w_in[:, 2 * DI : DI + CW]
        send[:, XW + CL :] = jnp.concatenate(
            [w_in[:, DI + CW :], jnp.zeros((192, 128 - NH), bf16)], axis=1
        )
    out[0:ROWS, :] = tok[...]
    rows[...] = jnp.zeros_like(rows)
    rows[0:4, 0:448] = taps[...].astype(f32)
    rows[4:5, 0:448] = bias[...].astype(f32).reshape(1, 448)
    rows[5:6, 0:192] = gain_in[...].astype(f32).reshape(1, 192)
    rows[6:7, 0:ROWS] = seg[...].astype(f32)
    out[ROWS : ROWS + 16, :] = rows[...].astype(bf16)


def gather_short(g, parts, taps, gain_in, pos, wide, seg):
    for d, part in enumerate(parts):
        rows = part[ROWS : ROWS + 16, :].astype(f32)
        for k in range(4):

            @pl.when((g ^ d) == k)
            def _(k=k, rows=rows):
                wide[0:5, 448 * k : 448 * k + 448] = rows[0:5, 0:448]
                gain_in[:, 192 * k : 192 * k + 192] = rows[5:6, 0:192]
                seg[2 * k : 2 * k + 1, :] = rows[6:7, 0:128]
                seg[2 * k + 1 : 2 * k + 2, :] = rows[6:7, 128:256]

    taps[...] = jnp.zeros_like(taps)
    taps[0:5, 0:XW] = wide[0:5, pl.ds(pl.multiple_of(g * XW, 128), XW)]
    taps[0:5, XW:] = wide[0:5, DI:]
    ids = seg[...]
    row_at = lax.broadcasted_iota(jnp.int32, (8, 128), 0)
    lane_at = lax.broadcasted_iota(jnp.int32, (8, 128), 1)
    one = jnp.full((1, 128), -1.0, f32)
    earlier = jnp.concatenate([one, ids[0:7]], axis=0)
    later = jnp.concatenate([ids[1:8], one], axis=0)
    ends = jnp.broadcast_to(ids[:, 127:128], (8, 128))
    starts = jnp.broadcast_to(earlier[:, 127:128], (8, 128))
    features = [ids]
    for lag in range(1, 4):
        shifted = jnp.where(
            lane_at >= lag, pltpu.roll(ids, lag, 1), pltpu.roll(earlier, lag, 1)
        )
        features.append((shifted == ids).astype(f32))
    features += [(ids == starts).astype(f32), (ids == ends).astype(f32)]
    for lag in range(1, 4):
        shifted = jnp.where(
            lane_at < 128 - lag, pltpu.roll(ids, 128 - lag, 1), pltpu.roll(later, 128 - lag, 1)
        )
        features.append((shifted == ids).astype(f32))
    pos[...] = jnp.zeros_like(pos)
    for j, feature in enumerate(features):
        for n in range(8):
            pos[n, j : j + 1, :] = feature[n : n + 1, :]


def forward_kernel(
    me, t0, t1, t2, t3, w0, w1, w2, w3, dtb, rate, skip,
    w_full, normed, proj, v_out, states, y_out, pos, taps, gain_in,
    tok, state, ext, wide, seg,
):
    i = pl.program_id(0)
    g = me[0]

    @pl.when(i == 0)
    def _():
        row_at = lax.broadcasted_iota(jnp.int32, (128, 128), 0)
        lane_at = lax.broadcasted_iota(jnp.int32, (128, 128), 1)
        chosen = ((row_at == lane_at + g * HL) & (lane_at < HL)).astype(bf16)
        for d, part in enumerate((w0, w1, w2, w3)):
            rows = pl.ds(pl.multiple_of((g ^ d) * 192, 64), 192)
            w_full[rows, : XW + CL] = part[:, : XW + CL]
            w_full[rows, XW + CL :] = mm(part[:, XW + CL :], chosen, NN).astype(bf16)
        state[...] = jnp.zeros_like(state)
        ext[0:8, :] = jnp.zeros((8, CL), f32)
        gather_short(g, (t0, t1, t2, t3), taps, gain_in, pos, wide, seg)

    for d, source in enumerate((t0, t1, t2, t3)):

        @pl.when((g ^ i) == d)
        def _(source=source):
            tok[...] = source[0:ROWS, :]

    x = tok[...].astype(f32)
    rms = lax.rsqrt(jnp.mean(x * x, axis=-1, keepdims=True) + epsilon)
    low_rows = (x * rms * gain_in[...]).astype(bf16)
    normed[...] = low_rows
    proj[...] = mm(low_rows, w_full[...], NN).astype(bf16)
    ext[8 : 8 + ROWS, :] = proj[:, XW : XW + CL].astype(f32)
    for s in range(ROWS // SPAN):
        at = s * SPAN
        rows = slice(at, at + SPAN)
        dt_rows = proj[rows, XW + CL :].astype(f32) + dtb[...]
        pos_rows = pos[2 * i + s]
        cols, step, step_t, cum, decay, carried, tails, low = span_decays(
            dt_rows, rate[...], pos_rows
        )
        v = taps[4:5, :] + taps[3:4, :] * ext[8 + at : 8 + at + SPAN, :]
        for lag in range(1, 4):
            window = ext[8 + at - lag : 8 + at - lag + SPAN, :]
            v = v + (taps[3 - lag : 4 - lag, :] * cols[:, lag : lag + 1]) * window
        v_out[rows, :] = v
        conv = v * jax.nn.sigmoid(v)
        b_rows, c_rows = conv[:, XW : XW + NS], conv[:, XW + NS :]
        scores = mm(c_rows, b_rows, NT)
        states[s] = state[...]
        from_state = mm(c_rows, state[...], NN)
        ys, ends, decays_end = [], [], []
        for p in range(HL // 2):
            lanes = slice(p * SPAN, (p + 1) * SPAN)
            xp = conv[:, lanes]
            mixing = [
                decay(h) * scores * step_t[h : h + 1, :] for h in (2 * p, 2 * p + 1)
            ]
            inner = mm(
                jnp.concatenate(mixing, axis=1),
                jnp.concatenate([jnp.where(low, xp, 0.0), jnp.where(low, 0.0, xp)], axis=0),
                NN,
            )
            ys.append(inner + carried[p] * from_state[:, lanes] + skip[:, lanes] * xp)
            ends.append(tails[p] * xp)
            decays_end.append(carried[p][SPAN - 1 :, :])
        y_out[rows, :] = jnp.concatenate(ys, axis=1)
        state[...] = jnp.concatenate(decays_end, axis=1) * state[...] + mm(
            b_rows, jnp.concatenate(ends, axis=1), TN
        )
    ext[0:8, :] = ext[ROWS : ROWS + 8, :]


def sums_kernel(me, c0, c1, c2, c3, gate_in, y_in, gain_out, w_out, dno_out, stats, cot):
    i = pl.program_id(0)
    pick(me[0] ^ i, (c0, c1, c2, c3), cot)
    dno = mm(cot[...], w_out[...], NT)
    dno_out[...] = dno
    gate = gate_in[...].astype(f32)
    gated = y_in[...] * (gate * jax.nn.sigmoid(gate))
    squares = jnp.sum(gated * gated, axis=-1, keepdims=True)
    products = jnp.sum(gated * gain_out[...] * dno, axis=-1, keepdims=True)
    lane_at = lax.broadcasted_iota(jnp.int32, (SPAN, SPAN), 1)
    both = jnp.zeros((SPAN, SPAN), f32)
    for s in range(ROWS // SPAN):
        rows = slice(s * SPAN, (s + 1) * SPAN)
        both = jnp.where(lane_at == 2 * s, squares[rows], both)
        both = jnp.where(lane_at == 2 * s + 1, products[rows], both)
    stats[0] = both.T[0:8, :]


def out_kernel(
    me, c0, c1, c2, c3, gate_in, y_in, dno_in, stats, gain_out, w_out, normed,
    bundle, d_gate, dy_out, sums, o_own, o_pair, o_across,
    cot, acc_out, acc_gate, acc_sum, normed_out,
):
    i = pl.program_id(0)
    g = me[0]

    @pl.when(i == 0)
    def _():
        for ref in (acc_out, acc_gate, acc_sum):
            ref[...] = jnp.zeros_like(ref)

    pick(g ^ i, (c0, c1, c2, c3), cot)
    totals = to_columns(stats[0])
    for s in range(ROWS // SPAN):
        rows = slice(s * SPAN, (s + 1) * SPAN)
        rms = lax.rsqrt(totals[:, 2 * s : 2 * s + 1] * (1.0 / DI) + epsilon)
        mean = rms * rms * rms * totals[:, 2 * s + 1 : 2 * s + 2] * (1.0 / DI)
        gate = gate_in[rows, :].astype(f32)
        sig = jax.nn.sigmoid(gate)
        silu = gate * sig
        y = y_in[rows, :]
        gated = y * silu
        scaled = gated * rms
        normed_out[rows, :] = (scaled * gain_out[...]).astype(bf16)
        dno = dno_in[rows, :]
        acc_sum[0:1, :] += jnp.sum(dno * scaled, axis=0, keepdims=True)
        d_gated = rms * gain_out[...] * dno - gated * mean
        dy_out[rows, :] = d_gated * silu
        d_gate[rows, :] = (d_gated * y * (sig * (1.0 + gate * (1.0 - sig)))).astype(bf16)
    acc_out[...] += mm(normed_out[...], cot[...], TN)
    acc_gate[...] += mm(normed[...], d_gate[...], TN)
    put(g ^ i, o_own, o_pair, o_across, mm(normed_out[...], w_out[...], NN).astype(bf16))

    @pl.when(i == pl.num_programs(0) - 1)
    def _():
        sums[...] = acc_sum[...]
        for k in range(4):
            for t in range(3):
                at = 576 * k + 192 * t
                bundle[at : at + 192, :] = acc_gate[
                    192 * k : 192 * k + 192, 128 * t : 128 * t + 128
                ].astype(bf16)
        for t in range(6):
            at = 2304 + XW * t
            bundle[at : at + XW, :] = acc_out[:, 128 * t : 128 * t + 128].astype(bf16)


def split_sum(rows, ones):
    high = rows.astype(bf16)
    rest = rows - high.astype(f32)
    return mm(high, ones, NN) + mm(rest, ones, NN)


def backward_block(
    w_full, normed, proj, v_in, states, dy_in, d_gate, pos, taps, dtb, rate, skip, ones,
    d_state, ext, acc_in, acc_dt, acc_small, d_proj,
):
    row_at = lax.broadcasted_iota(jnp.int32, (SPAN, SPAN), 0)
    lane_at = lax.broadcasted_iota(jnp.int32, (SPAN, SPAN), 1)
    later = (row_at <= lane_at).astype(f32)

    def add(row, value):
        width = value.shape[1]
        acc_small[row : row + 1, :width] += value

    def down(value):
        return jnp.sum(value, axis=0, keepdims=True)

    d_proj[:, :XW] = d_gate[...]
    for s in reversed(range(ROWS // SPAN)):
        at = s * SPAN
        rows = slice(at, at + SPAN)
        dy = dy_in[rows, :]
        dt_rows = proj[rows, XW + CL :].astype(f32) + dtb[...]
        cols, step, step_t, cum, decay, carried, tails, low = span_decays(
            dt_rows, rate[...], pos[s]
        )
        v = v_in[rows, :]
        sig_v = jax.nn.sigmoid(v)
        conv = v * sig_v
        x, b_rows, c_rows = conv[:, :XW], conv[:, XW : XW + NS], conv[:, XW + NS :]
        add(1, down(dy * x))
        state = states[s]
        state_grad = d_state[...]
        scores = mm(c_rows, b_rows, NT)
        from_state = mm(c_rows, state, NN)
        from_grad = mm(b_rows, state_grad, NN)
        carried_all = jnp.concatenate(carried, axis=1)
        tails_all = jnp.concatenate(tails, axis=1)
        dy_carried = dy * carried_all
        x_tail = x * tails_all
        d_scores = jnp.zeros((SPAN, SPAN), f32)
        row_sums = jnp.zeros((SPAN, SPAN), f32)
        col_sums, dxs = [], []
        for p in range(HL // 2):
            lanes = slice(p * SPAN, (p + 1) * SPAN)
            xp, dyp = x[:, lanes], dy[:, lanes]
            halves = jnp.concatenate([jnp.where(low, dyp, 0.0), jnp.where(low, 0.0, dyp)], axis=0)
            d_mixing = mm(halves, xp, NT)
            mixing = []
            for k in range(2):
                h = 2 * p + k
                kept = decay(h)
                kept_step = kept * step_t[h : h + 1, :]
                mixing.append(kept_step * scores)
                d_mix = d_mixing[k * SPAN : (k + 1) * SPAN, :]
                d_scores = d_scores + d_mix * kept_step
                plain = d_mix * kept * scores
                col_sums.append(down(plain))
                row_sum = jnp.sum(plain * step_t[h : h + 1, :], axis=1, keepdims=True)
                row_sums = jnp.where(lane_at == h, row_sum, row_sums)
            inner = mm(jnp.concatenate(mixing, axis=0), halves, TN)
            dxs.append(inner + skip[:, lanes] * dyp + tails[p] * from_grad[:, lanes])
        dx = jnp.concatenate(dxs, axis=1)
        d_c = mm(d_scores, b_rows, NN) + mm(dy_carried, state, NT)
        d_b = mm(d_scores, c_rows, TN) + mm(x_tail, state_grad, NT)

        end_decay = carried_all[SPAN - 1 :, :]
        through = end_decay * down(state * state_grad)
        last = lax.broadcasted_iota(jnp.int32, (SPAN, XW), 0) == SPAN - 1
        from_start = split_sum(
            dy_carried * from_state + jnp.where(last, through, 0.0), ones[...]
        )
        to_end = split_sum(x * from_grad, ones[...])
        end_plain = jnp.exp(cum[SPAN - 1 :, :] - cum) * cols[:, 5:6]
        to_end_kept = to_end * end_plain
        to_end_step = to_end_kept * step
        col_sum = to_columns(jnp.concatenate(col_sums, axis=0))
        d_cum = row_sums - col_sum * step + from_start - to_end_step
        d_cum = d_cum + jnp.where(row_at == SPAN - 1, down(to_end_step), 0.0)
        d_log = mm_exact(later, d_cum, NN)
        d_step = col_sum + to_end_kept + rate[...] * d_log
        d_dt = d_step * jax.nn.sigmoid(dt_rows)
        add(2, down(d_dt))
        add(3, down(d_log * step) * rate[...])
        d_proj[rows, XW + CL :] = d_dt.astype(bf16)
        d_state[...] = end_decay * state_grad + mm(c_rows, dy_carried, TN)

        dv = jnp.concatenate([dx, d_b, d_c], axis=1) * (sig_v * (1.0 + v * (1.0 - sig_v)))
        ext[rows, :] = dv
        add(4, down(dv))
        conv_in = proj[rows, XW : XW + CL].astype(f32)
        add(8, down(dv * conv_in))
        d_conv = taps[3:4, :] * dv
        for lag in range(1, 4):
            window = ext[at + lag : at + lag + SPAN, :] * cols[:, 5 + lag : 6 + lag]
            d_conv = d_conv + taps[3 - lag : 4 - lag, :] * window
            add(8 - lag, down(window * conv_in))
        d_proj[rows, XW : XW + CL] = d_conv.astype(bf16)

    ext[ROWS:, :] = ext[0:8, :]
    d_normed = mm(d_proj[...], w_full[...], NT)
    add(9, down(d_normed * normed[...].astype(f32)))
    acc_in[...] += mm(normed[...], d_proj[:, XW : XW + CL], TN)
    acc_dt[...] += mm(d_proj[:, XW + CL :], normed[...], TN)[0:8, :]
    return d_normed.astype(bf16)


def late_kernel(
    w_full, normed, proj, v_in, states, dy_in, d_gate, pos, taps, dtb, rate, skip, ones,
    d_state, edge, acc_in, acc_dt, acc_small, d_normed,
    ext, d_proj,
):
    @pl.when(pl.program_id(0) == 0)
    def _():
        for ref in (d_state, acc_in, acc_dt, acc_small):
            ref[...] = jnp.zeros_like(ref)
        ext[ROWS:, :] = jnp.zeros((8, CL), f32)

    d_normed[...] = backward_block(
        w_full, normed, proj, v_in, states, dy_in, d_gate, pos, taps, dtb, rate, skip, ones,
        d_state, ext, acc_in, acc_dt, acc_small, d_proj,
    )
    edge[...] = ext[ROWS:, :]


def early_kernel(
    me, w_full, normed, proj, v_in, states, dy_in, d_gate, pos, taps, dtb, rate, skip, ones,
    d_state_in, edge, acc_in_in, acc_dt_in, acc_small_in, d_normed_in, sums,
    bundle, n_own, n_pair, n_across,
    d_state, ext, acc_in, acc_dt, acc_small, d_proj, small,
):
    i = pl.num_programs(0) - 1 - pl.program_id(0)
    g = me[0]

    @pl.when(pl.program_id(0) == 0)
    def _():
        d_state[...] = d_state_in[...]
        ext[ROWS:, :] = edge[...]
        acc_in[...] = acc_in_in[...]
        acc_dt[...] = acc_dt_in[...]
        acc_small[...] = acc_small_in[...]
        small[...] = jnp.zeros_like(small)
        for j in range(2):
            put(g ^ (2 + j), n_own, n_pair, n_across, d_normed_in[ROWS * j : ROWS * j + ROWS, :])

    value = backward_block(
        w_full, normed, proj, v_in, states, dy_in, d_gate, pos, taps, dtb, rate, skip, ones,
        d_state, ext, acc_in, acc_dt, acc_small, d_proj,
    )
    put(g ^ i, n_own, n_pair, n_across, value)

    @pl.when(i == 0)
    def _():
        def place(k, piece, value):
            at = 32 * k + 16 * (piece % 2)
            bundle[piece // 2, at : at + 16, :] = value.astype(bf16)

        def lay(start, source, row, first, tiles):
            for t in range(tiles):
                lanes = slice(first + 128 * t, first + 128 * t + 128)
                small[start + t : start + t + 1, :] = source[row : row + 1, lanes]

        for j in range(4):
            lay(16 + 5 * j, acc_small, 5 + j, 0, 5)
        lay(36, acc_small, 4, 0, 5)
        lay(43, sums, 0, 0, 3)
        lay(46, acc_small, 1, 0, 3)
        lay(49, acc_small, 2, 0, 1)
        lay(50, acc_small, 3, 0, 1)
        for k in range(4):
            for tile in range(5):
                for q in range(12):
                    place(
                        k,
                        12 * tile + q,
                        acc_in[
                            192 * k + 16 * q : 192 * k + 16 * q + 16,
                            128 * tile : 128 * tile + 128,
                        ],
                    )
            for h in range(HL):
                small[2 * h : 2 * h + 1, :] = acc_dt[h : h + 1, 192 * k : 192 * k + 128]
                small[2 * h + 1 : 2 * h + 2, 0:64] = acc_dt[
                    h : h + 1, 192 * k + 128 : 192 * k + 192
                ]
            small[41:42, :] = acc_small[9:10, 192 * k : 192 * k + 128]
            small[42:43, 0:64] = acc_small[9:10, 192 * k + 128 : 192 * k + 192]
            for q in range(4):
                place(k, 60 + q, small[16 * q : 16 * q + 16, :])


def assemble_kernel(
    me, gates0, gates1, gates2, gates3, parts, gain_in,
    grad_in, grad_kernel, grad_bias, grad_gain_in, grad_gain_out, grad_skip,
    grad_dt, grad_log,
    wide, turned,
):
    g = me[0]

    def piece(k, row, count=192):
        return parts[k, row : row + count, :].astype(f32)

    for d, gates in enumerate((gates0, gates1, gates2, gates3)):
        for t in range(3):
            start = pl.multiple_of((g ^ d) * XW + 128 * t, 128)
            grad_in[:, pl.ds(start, 128)] = gates[192 * t : 192 * t + 192, :].astype(f32)
    for k in range(4):
        for t in range(3):
            lanes = slice(DI + k * XW + 128 * t, DI + k * XW + 128 * t + 128)
            grad_in[:, lanes] = piece(k, 192 * t)
    for t in range(3, 5):
        lanes = slice(2 * DI + 128 * (t - 3), 2 * DI + 128 * (t - 2))
        grad_in[:, lanes] = (piece(0, 192 * t) + piece(1, 192 * t)) + (
            piece(2, 192 * t) + piece(3, 192 * t)
        )

    turned[...] = jnp.zeros_like(turned)
    wide[...] = jnp.zeros_like(wide)
    gain = jnp.zeros((2, 128), f32)
    for k in range(4):
        rest = piece(k, 960, 64)
        for h in range(HL):
            at = HL * k + h
            turned[at : at + 1, 0:128] = rest[2 * h : 2 * h + 1, :]
            turned[at : at + 1, 128:256] = rest[2 * h + 1 : 2 * h + 2, :]
        for j in range(5):
            for t in range(3):
                lanes = slice(k * XW + 128 * t, k * XW + 128 * t + 128)
                wide[j : j + 1, lanes] = rest[16 + 5 * j + t : 17 + 5 * j + t, :]
            for t in range(3, 5):
                lanes = slice(DI + 128 * (t - 3), DI + 128 * (t - 2))
                wide[j : j + 1, lanes] += rest[16 + 5 * j + t : 17 + 5 * j + t, :]
        gain = gain + rest[41:43, :]
    grad_in[:, DI + CW :] = turned[...].T[0:192, 0:NH]
    grad_gain_in[:, 0:128] = gain[0:1, :] / gain_in[:, 0:128]
    grad_gain_in[:, 128:192] = gain[1:2, 0:64] / gain_in[:, 128:192]
    for k in range(4):

        @pl.when(g == k)
        def _(k=k):
            grad_kernel[...] = wide[0:4, 448 * k : 448 * k + 448]
            grad_bias[...] = wide[4:5, 448 * k : 448 * k + 448]

    own = parts[g, 960:1024, :].astype(f32)
    for t in range(3):
        grad_gain_out[:, 128 * t : 128 * t + 128] = own[43 + t : 44 + t, :]
    lane_at = lax.broadcasted_iota(jnp.int32, (1, 128), 1)
    skips = jnp.zeros((1, 128), f32)
    for t in range(3):
        row = own[46 + t : 47 + t, :]
        first = jnp.sum(jnp.where(lane_at < HP, row, 0.0), axis=1, keepdims=True)
        second = jnp.sum(jnp.where(lane_at < HP, 0.0, row), axis=1, keepdims=True)
        skips = jnp.where(lane_at == 2 * t, first, skips)
        skips = jnp.where(lane_at == 2 * t + 1, second, skips)
    grad_skip[...] = skips[:, 0:HL]
    grad_dt[...] = own[49:50, 0:HL]
    grad_log[...] = own[50:51, 0:HL]


def whole(shape):
    zeros = (0,) * len(shape)
    return pl.BlockSpec(shape, lambda i: zeros)


def blocked(shape, place):
    zeros = (0,) * (len(shape) - 1)
    return pl.BlockSpec(shape, lambda i: (place(i),) + zeros)


scalar_spec = pl.BlockSpec(memory_space=pltpu.SMEM)
vmem_spec = pl.BlockSpec(memory_space=pltpu.VMEM)


def shape(dims, dtype):
    return jax.ShapeDtypeStruct(dims, dtype)


def call(body, name, micros, **kwargs):
    return pl.pallas_call(
        body,
        name=name,
        compiler_params=pltpu.CompilerParams(vmem_limit_bytes=vmem_bytes),
        cost_estimate=pl.CostEstimate(
            flops=int(micros * 1e9), bytes_accessed=1 << 20, transcendentals=0
        ),
        **kwargs,
    )


def among(value, d):
    return lax.ppermute(value, "group", [(i, i ^ d) for i in range(4)])


def local(
    tokens, segments, cotangent, gain_in, w_in, kernel, conv_bias, dt_bias, a_log, skip_gain,
    gain_out, w_out,
):
    reps = lax.axis_size("rep")
    g = lax.axis_index("group")
    me = g.astype(jnp.int32).reshape(1)
    tok = tokens.reshape(ROWS, D)
    cot = cotangent.reshape(ROWS, D)
    part = whole((ROWS, D))
    blocks = 4

    w0, w1, w2, w3, both0 = call(
        columns_kernel,
        "columns",
        2,
        in_specs=[scalar_spec] + [vmem_spec] * 6,
        out_specs=[vmem_spec] * 5,
        out_shape=(shape((192, PW), bf16),) * 4 + (shape((ROWS + 16, D), bf16),),
        scratch_shapes=[pltpu.VMEM((16, D), f32)],
    )(
        me, w_in, tok, kernel, conv_bias, gain_in,
        segments.reshape(1, ROWS),
    )

    def across(value, d):
        pairs = [(i * reps + r, (i ^ d) * reps + (r ^ 1)) for r in range(reps) for i in range(4)]
        return lax.ppermute(value, ("group", "rep"), pairs)

    w2 = across(w2, 2)
    both2 = among(both0, 2)
    w3 = across(w3, 3)
    w1 = among(w1, 1)
    both1 = among(both0, 1)
    both2, cot_late = lax.optimization_barrier((both2, cot))
    both3 = among(both2, 1)
    c2 = among(cot_late, 2)
    c1 = among(cot_late, 1)
    c3 = among(c2, 1)
    length = blocks * ROWS
    spans = length // SPAN

    dtb = jnp.pad(dt_bias.astype(f32), (0, 128 - HL)).reshape(1, 128)
    rate = jnp.pad(-jnp.exp(a_log.astype(f32)), (0, 128 - HL)).reshape(1, 128)
    skip = jnp.repeat(skip_gain.astype(f32), HP).reshape(1, XW)
    gain_o = gain_out.astype(f32).reshape(1, XW)

    def up(i):
        return i

    by_owner_specs = [part, whole((2 * ROWS, D)), part]
    by_owner_shapes = tuple(shape((n * ROWS, D), bf16) for n in (1, 2, 1))

    def to_owner(own, pair, over):
        got = among(pair, 1).astype(f32)
        other = (over.astype(f32) + got[ROWS:]).astype(bf16)
        return own, got[:ROWS], among(other, 2)

    w_full, normed, proj, v_rows, states, y_rows, pos, taps, gain_in_all = call(
        forward_kernel,
        "forward",
        15,
        grid=(blocks,),
        in_specs=[scalar_spec]
        + [whole((ROWS + 16, D))] * 4
        + [whole((192, PW))] * 4
        + [whole((1, 128)), whole((1, 128)), whole((1, XW))],
        out_specs=[
            whole((D, PW)),
            blocked((ROWS, D), up),
            blocked((ROWS, PW), up),
            blocked((ROWS, CL), up),
            blocked((2, NS, XW), up),
            blocked((ROWS, XW), up),
            whole((8, 16, SPAN)),
            whole((8, CL)),
            whole((1, D)),
        ],
        out_shape=(
            shape((D, PW), bf16),
            shape((length, D), bf16),
            shape((length, PW), bf16),
            shape((length, CL), f32),
            shape((spans, NS, XW), f32),
            shape((length, XW), f32),
            shape((spans, 16, SPAN), f32),
            shape((8, CL), f32),
            shape((1, D), f32),
        ),
        scratch_shapes=[
            pltpu.VMEM((ROWS, D), bf16),
            pltpu.VMEM((NS, XW), f32),
            pltpu.VMEM((ROWS + 8, CL), f32),
            pltpu.VMEM((8, CW), f32),
            pltpu.VMEM((8, 128), f32),
        ],
    )(
        me, both0, both1, both2, both3, w0, w1, w2, w3, dtb, rate, skip,
    )

    gate_spec = pl.BlockSpec((ROWS, XW), lambda i: (i, 0))
    dno, stats = call(
        sums_kernel,
        "sums",
        4,
        grid=(blocks,),
        in_specs=[scalar_spec]
        + [part] * 4
        + [gate_spec, blocked((ROWS, XW), up), whole((1, XW)), whole((XW, D))],
        out_specs=[blocked((ROWS, XW), up), blocked((1, 8, SPAN), up)],
        out_shape=(shape((length, XW), f32), shape((blocks, 8, SPAN), f32)),
        scratch_shapes=[pltpu.VMEM((ROWS, D), bf16)],
    )(me, cot, c1, c2, c3, proj, y_rows, gain_o, w_out)
    stats = lax.psum(stats, "group")

    bundle1, d_gate, dy, sums, *o_parts = call(
        out_kernel,
        "out",
        7,
        grid=(blocks,),
        in_specs=[scalar_spec]
        + [part] * 4
        + [
            gate_spec, blocked((ROWS, XW), up), blocked((ROWS, XW), up),
            blocked((1, 8, SPAN), up), whole((1, XW)), whole((XW, D)), blocked((ROWS, D), up),
        ],
        out_specs=[
            whole((4608, 128)), blocked((ROWS, XW), up), blocked((ROWS, XW), up), whole((8, XW)),
        ]
        + by_owner_specs,
        out_shape=(
            shape((4608, 128), bf16), shape((length, XW), bf16), shape((length, XW), f32),
            shape((8, XW), f32),
        )
        + by_owner_shapes,
        scratch_shapes=[
            pltpu.VMEM((ROWS, D), bf16),
            pltpu.VMEM((XW, D), f32),
            pltpu.VMEM((D, XW), f32),
            pltpu.VMEM((8, XW), f32),
            pltpu.VMEM((ROWS, XW), bf16),
        ],
    )(me, cot, c1, c2, c3, proj, y_rows, dno, stats, gain_o, w_out, normed)

    def spread(value):
        return lax.all_to_all(value, "rep", 0, 0, tiled=True)

    received1 = spread(bundle1.reshape(reps, 144, 128))
    branches = to_owner(*o_parts)

    ones = jnp.asarray(np.arange(XW)[:, None] // HP == np.arange(128)[None, :], bf16)
    half = blocks // 2
    shared = [
        shape((NS, XW), f32), shape((8, CL), f32), shape((D, CL), f32), shape((8, D), f32),
        shape((16, D), f32),
    ]

    def backward_specs(last):
        def back(i):
            return last - i

        return [
            whole((D, PW)),
            blocked((ROWS, D), back),
            blocked((ROWS, PW), back),
            blocked((ROWS, CL), back),
            blocked((2, NS, XW), back),
            blocked((ROWS, XW), back),
            blocked((ROWS, XW), back),
            blocked((2, 16, SPAN), back),
            whole((8, CL)), whole((1, 128)), whole((1, 128)), whole((1, XW)), whole((XW, 128)),
        ]

    operands = (w_full, normed, proj, v_rows, states, dy, d_gate, pos, taps, dtb, rate, skip, ones)
    handed = call(
        late_kernel,
        "late",
        12,
        grid=(half,),
        in_specs=backward_specs(blocks - 1),
        out_specs=[whole(v.shape) for v in shared]
        + [blocked((ROWS, D), lambda i: half - 1 - i)],
        out_shape=shared + [shape((half * ROWS, D), bf16)],
        scratch_shapes=[pltpu.VMEM((ROWS + 8, CL), f32), pltpu.VMEM((ROWS, PW), bf16)],
    )(*operands)

    def total(received):
        return jnp.sum(received.astype(f32), axis=0).astype(bf16)

    reduced1 = total(received1)
    reduced1, handed, branches = lax.optimization_barrier((reduced1, handed, branches))
    flat1 = spread(jnp.broadcast_to(reduced1[None], (reps, 144, 128))).reshape(4608, 128)
    bundle2, *n_parts = call(
        early_kernel,
        "early",
        12,
        grid=(half,),
        in_specs=[scalar_spec]
        + backward_specs(half - 1)
        + [whole(v.shape) for v in shared]
        + [whole((half * ROWS, D)), whole((8, XW))],
        out_specs=[whole((32, 128, 128))] + by_owner_specs,
        out_shape=(shape((32, 128, 128), bf16),) + by_owner_shapes,
        scratch_shapes=[
            pltpu.VMEM((NS, XW), f32),
            pltpu.VMEM((ROWS + 8, CL), f32),
            pltpu.VMEM((D, CL), f32),
            pltpu.VMEM((8, D), f32),
            pltpu.VMEM((16, D), f32),
            pltpu.VMEM((ROWS, PW), bf16),
            pltpu.VMEM((64, 128), f32),
        ],
    )(me, *operands, *handed, sums)

    bundle2, flat1 = lax.optimization_barrier((bundle2, flat1))
    received2 = spread(bundle2)
    d_parts = to_owner(*n_parts)
    by_member = flat1[:2304].reshape(4, 576, 128)
    gates = [lax.dynamic_index_in_dim(by_member, g ^ d, 0, keepdims=False) for d in range(4)]
    gates = [gates[0]] + [among(gates[d], d) for d in range(1, 4)]
    reduced2, gates, d_parts = lax.optimization_barrier((total(received2), gates, d_parts))
    parts = lax.all_to_all(
        jnp.broadcast_to(reduced2.reshape(4, 1, 32, 128), (4, reps, 32, 128)).reshape(
            4 * reps, 32, 128
        ),
        ("group", "rep"), 0, 0, tiled=True,
    ).reshape(4, 32 * reps, 128)
    grad_w_out = flat1[2304:].reshape(6, XW, 128).transpose(1, 0, 2).reshape(XW, D).astype(f32)

    x = tok.astype(f32)
    branch = sum(value.astype(f32) for value in branches)
    layer_out = (x + branch).astype(bf16).reshape(tokens.shape)
    d_normed = sum(value.astype(f32) for value in d_parts)
    rms_in = lax.rsqrt(jnp.mean(x * x, axis=-1, keepdims=True) + epsilon)
    scaled = d_normed * gain_in_all
    grad_tokens = (
        cot.astype(f32)
        + rms_in * scaled
        - x * (rms_in * rms_in * rms_in * jnp.mean(x * scaled, axis=-1, keepdims=True))
    ).reshape(tokens.shape)

    grads = call(
        assemble_kernel,
        "assemble",
        4,
        in_specs=[scalar_spec] + [vmem_spec] * 6,
        out_specs=[vmem_spec] * 8,
        out_shape=(
            shape((192, 3352), f32), shape((4, 448), f32),
            shape((1, 448), f32), shape((1, 192), f32), shape((1, XW), f32), shape((1, HL), f32),
            shape((1, HL), f32), shape((1, HL), f32),
        ),
        scratch_shapes=[pltpu.VMEM((8, CW), f32), pltpu.VMEM((128, 256), f32)],
    )(me, *gates, parts, gain_in.astype(f32).reshape(1, 192))
    grad_w_in, grad_kernel, grad_bias, grad_gi, grad_go, grad_s, grad_d, grad_l = grads
    return (
        layer_out,
        grad_tokens,
        grad_gi.reshape(-1),
        grad_w_in,
        grad_kernel,
        grad_bias.reshape(-1),
        grad_d.reshape(-1),
        grad_l.reshape(-1),
        grad_s.reshape(-1),
        grad_go.reshape(-1),
        grad_w_out,
    )


def solution(mesh):
    sequences = P("rep", "group", None)
    vector = P("group")
    matrix = P("group", None)
    return jax.shard_map(
        local,
        mesh=mesh,
        in_specs=(
            sequences, P("rep", "group"), sequences, vector, matrix, P(None, "group"),
            vector, vector, vector, vector, vector, matrix,
        ),
        out_specs=(
            sequences, sequences, vector, matrix, P(None, "group"), vector, vector, vector,
            vector, vector, matrix,
        ),
        check_vma=False,
    )
```

```python
import jax
import jax.numpy as jnp
import numpy as np
from jax import lax
from jax.experimental import pallas as pl
from jax.experimental.pallas import tpu as pltpu
from jax.sharding import PartitionSpec as P

D = 768
NH = 24
HP = 64
NS = 128
DI = 1536
CW = 1792
SPAN = 128
ROWS = 256
HL = 6
XW = HL * HP
CL = XW + 2 * NS
PW = XW + CL + 128
CUT = 640
epsilon = 1e-05
f32 = jnp.float32
bf16 = jnp.bfloat16
NN = ((1,), (0,))
NT = ((1,), (1,))
TN = ((0,), (0,))
vmem_bytes = 56 * 1024 * 1024


def mm(a, b, dims):
    return lax.dot_general(
        a.astype(bf16), b.astype(bf16), (dims, ((), ())), preferred_element_type=f32
    )


def mm_exact(a, b, dims):
    return lax.dot_general(
        a, b, (dims, ((), ())), preferred_element_type=f32, precision=lax.Precision.HIGHEST
    )


def to_columns(rows):
    short = SPAN - rows.shape[0]
    return jnp.concatenate([rows, jnp.zeros((short, SPAN), f32)], axis=0).T


def softplus(v):
    return jnp.maximum(v, 0.0) + jnp.log1p(jnp.exp(-jnp.abs(v)))


def over_lanes(column):
    return jnp.broadcast_to(column, (SPAN, SPAN))


def span_decays(dt_rows, rate, pos_rows):
    row_at = lax.broadcasted_iota(jnp.int32, (SPAN, SPAN), 0)
    lane_at = lax.broadcasted_iota(jnp.int32, (SPAN, SPAN), 1)
    pos = to_columns(pos_rows)
    step = softplus(dt_rows)
    cum = mm_exact((row_at >= lane_at).astype(f32), step * rate, NN)
    cum_t = cum.T
    step_t = step.T
    allowed = (over_lanes(pos[:, 0:1]) == pos_rows[0:1, :]) & (row_at >= lane_at)
    low = lane_at < HP
    cums = [over_lanes(cum[:, h : h + 1]) for h in range(HL)]
    linked = pos[:, 4:5]
    tail = pos[:, 5:6]
    carried, tails = [], []
    for p in range(HL // 2):
        both = jnp.where(low, cums[2 * p], cums[2 * p + 1])
        steps = jnp.where(
            low, over_lanes(step[:, 2 * p : 2 * p + 1]), over_lanes(step[:, 2 * p + 1 : 2 * p + 2])
        )
        carried.append(jnp.exp(both) * linked)
        tails.append(jnp.exp(both[SPAN - 1 :, :] - both) * tail * steps)

    def decay(h):
        return jnp.where(allowed, jnp.exp(jnp.minimum(cums[h] - cum_t[h : h + 1, :], 0.0)), 0.0)

    return pos, step, step_t, cum, decay, carried, tails, low


def pick(index, sources, target):
    for d, source in enumerate(sources):

        @pl.when(index == d)
        def _(source=source):
            target[...] = source[...]


def put(index, own, pair, across, value):
    low, high = pair.at[0:ROWS, :], pair.at[ROWS : 2 * ROWS, :]
    for d, target in enumerate((own, low, across, high)):

        @pl.when(index == d)
        def _(target=target):
            target[...] = value


def columns_kernel(
    me, w_in, tok, taps, bias, gain_in, seg, w0, w1, w2, w3a, w3b, out, rows, last
):
    g = me[0]
    for d, send in enumerate((w0, w1, w2, last)):
        start = (g ^ d) * XW
        send[:, :XW] = w_in[:, pl.ds(pl.multiple_of(start, 128), XW)]
        send[:, XW : 2 * XW] = w_in[:, pl.ds(pl.multiple_of(DI + start, 128), XW)]
        send[:, 2 * XW : XW + CL] = w_in[:, 2 * DI : DI + CW]
        send[:, XW + CL :] = jnp.concatenate(
            [w_in[:, DI + CW :], jnp.zeros((192, 128 - NH), bf16)], axis=1
        )
    w3a[...] = last[:, :CUT]
    w3b[...] = last[:, CUT:]
    out[0:ROWS, :] = tok[...]
    rows[...] = jnp.zeros_like(rows)
    rows[0:4, 0:448] = taps[...].astype(f32)
    rows[4:5, 0:448] = bias[...].astype(f32).reshape(1, 448)
    rows[5:6, 0:192] = gain_in[...].astype(f32).reshape(1, 192)
    rows[6:7, 0:ROWS] = seg[...].astype(f32)
    out[ROWS : ROWS + 16, :] = rows[...].astype(bf16)


def gather_short(g, parts, taps, gain_in, pos, wide, seg):
    for d, part in enumerate(parts):
        rows = part[ROWS : ROWS + 16, :].astype(f32)
        for k in range(4):

            @pl.when((g ^ d) == k)
            def _(k=k, rows=rows):
                wide[0:5, 448 * k : 448 * k + 448] = rows[0:5, 0:448]
                gain_in[:, 192 * k : 192 * k + 192] = rows[5:6, 0:192]
                seg[2 * k : 2 * k + 1, :] = rows[6:7, 0:128]
                seg[2 * k + 1 : 2 * k + 2, :] = rows[6:7, 128:256]

    taps[...] = jnp.zeros_like(taps)
    taps[0:5, 0:XW] = wide[0:5, pl.ds(pl.multiple_of(g * XW, 128), XW)]
    taps[0:5, XW:] = wide[0:5, DI:]
    ids = seg[...]
    row_at = lax.broadcasted_iota(jnp.int32, (8, 128), 0)
    lane_at = lax.broadcasted_iota(jnp.int32, (8, 128), 1)
    one = jnp.full((1, 128), -1.0, f32)
    earlier = jnp.concatenate([one, ids[0:7]], axis=0)
    later = jnp.concatenate([ids[1:8], one], axis=0)
    ends = jnp.broadcast_to(ids[:, 127:128], (8, 128))
    starts = jnp.broadcast_to(earlier[:, 127:128], (8, 128))
    features = [ids]
    for lag in range(1, 4):
        shifted = jnp.where(
            lane_at >= lag, pltpu.roll(ids, lag, 1), pltpu.roll(earlier, lag, 1)
        )
        features.append((shifted == ids).astype(f32))
    features += [(ids == starts).astype(f32), (ids == ends).astype(f32)]
    for lag in range(1, 4):
        shifted = jnp.where(
            lane_at < 128 - lag, pltpu.roll(ids, 128 - lag, 1), pltpu.roll(later, 128 - lag, 1)
        )
        features.append((shifted == ids).astype(f32))
    pos[...] = jnp.zeros_like(pos)
    for j, feature in enumerate(features):
        for n in range(8):
            pos[n, j : j + 1, :] = feature[n : n + 1, :]


def forward_kernel(
    me, t0, t1, t2, t3, w0, w1, w2, w3a, w3b, dtb, rate, skip,
    w_full, normed, proj, v_out, states, y_out, pos, taps, gain_in,
    tok, state, ext, wide, seg,
):
    i = pl.program_id(0)
    g = me[0]

    @pl.when(i == 0)
    def _():
        row_at = lax.broadcasted_iota(jnp.int32, (128, 128), 0)
        lane_at = lax.broadcasted_iota(jnp.int32, (128, 128), 1)
        chosen = ((row_at == lane_at + g * HL) & (lane_at < HL)).astype(bf16)
        for d, part in enumerate((w0, w1, w2)):
            rows = pl.ds(pl.multiple_of((g ^ d) * 192, 64), 192)
            w_full[rows, : XW + CL] = part[:, : XW + CL]
            w_full[rows, XW + CL :] = mm(part[:, XW + CL :], chosen, NN).astype(bf16)
        rows = pl.ds(pl.multiple_of((g ^ 3) * 192, 64), 192)
        w_full[rows, :CUT] = w3a[...]
        w_full[rows, CUT : XW + CL] = w3b[:, : XW + CL - CUT]
        w_full[rows, XW + CL :] = mm(w3b[:, XW + CL - CUT :], chosen, NN).astype(bf16)
        state[...] = jnp.zeros_like(state)
        ext[0:8, :] = jnp.zeros((8, CL), f32)
        gather_short(g, (t0, t1, t2, t3), taps, gain_in, pos, wide, seg)

    for d, source in enumerate((t0, t1, t2, t3)):

        @pl.when((g ^ i) == d)
        def _(source=source):
            tok[...] = source[0:ROWS, :]

    x = tok[...].astype(f32)
    rms = lax.rsqrt(jnp.mean(x * x, axis=-1, keepdims=True) + epsilon)
    low_rows = (x * rms * gain_in[...]).astype(bf16)
    normed[...] = low_rows
    proj[...] = mm(low_rows, w_full[...], NN).astype(bf16)
    ext[8 : 8 + ROWS, :] = proj[:, XW : XW + CL].astype(f32)
    for s in range(ROWS // SPAN):
        at = s * SPAN
        rows = slice(at, at + SPAN)
        dt_rows = proj[rows, XW + CL :].astype(f32) + dtb[...]
        pos_rows = pos[2 * i + s]
        cols, step, step_t, cum, decay, carried, tails, low = span_decays(
            dt_rows, rate[...], pos_rows
        )
        v = taps[4:5, :] + taps[3:4, :] * ext[8 + at : 8 + at + SPAN, :]
        for lag in range(1, 4):
            window = ext[8 + at - lag : 8 + at - lag + SPAN, :]
            v = v + (taps[3 - lag : 4 - lag, :] * cols[:, lag : lag + 1]) * window
        v_out[rows, :] = v
        conv = v * jax.nn.sigmoid(v)
        b_rows, c_rows = conv[:, XW : XW + NS], conv[:, XW + NS :]
        scores = mm(c_rows, b_rows, NT)
        states[s] = state[...]
        from_state = mm(c_rows, state[...], NN)
        ys, ends, decays_end = [], [], []
        for p in range(HL // 2):
            lanes = slice(p * SPAN, (p + 1) * SPAN)
            xp = conv[:, lanes]
            mixing = [
                decay(h) * scores * step_t[h : h + 1, :] for h in (2 * p, 2 * p + 1)
            ]
            inner = mm(
                jnp.concatenate(mixing, axis=1),
                jnp.concatenate([jnp.where(low, xp, 0.0), jnp.where(low, 0.0, xp)], axis=0),
                NN,
            )
            ys.append(inner + carried[p] * from_state[:, lanes] + skip[:, lanes] * xp)
            ends.append(tails[p] * xp)
            decays_end.append(carried[p][SPAN - 1 :, :])
        y_out[rows, :] = jnp.concatenate(ys, axis=1)
        state[...] = jnp.concatenate(decays_end, axis=1) * state[...] + mm(
            b_rows, jnp.concatenate(ends, axis=1), TN
        )
    ext[0:8, :] = ext[ROWS : ROWS + 8, :]


def sums_kernel(me, c0, c1, c2, c3, gate_in, y_in, gain_out, w_out, dno_out, stats, cot):
    i = pl.program_id(0)
    pick(me[0] ^ i, (c0, c1, c2, c3), cot)
    dno = mm(cot[...], w_out[...], NT)
    dno_out[...] = dno
    gate = gate_in[...].astype(f32)
    gated = y_in[...] * (gate * jax.nn.sigmoid(gate))
    squares = jnp.sum(gated * gated, axis=-1, keepdims=True)
    products = jnp.sum(gated * gain_out[...] * dno, axis=-1, keepdims=True)
    lane_at = lax.broadcasted_iota(jnp.int32, (SPAN, SPAN), 1)
    both = jnp.zeros((SPAN, SPAN), f32)
    for s in range(ROWS // SPAN):
        rows = slice(s * SPAN, (s + 1) * SPAN)
        both = jnp.where(lane_at == 2 * s, squares[rows], both)
        both = jnp.where(lane_at == 2 * s + 1, products[rows], both)
    stats[0] = both.T[0:8, :]


def branch_kernel(me, gate_in, y_in, gain_out, w_out, o_own, o_pair, o_across):
    gate = gate_in[...].astype(f32)
    gated = y_in[...] * (gate * jax.nn.sigmoid(gate)) * gain_out[...]
    value = mm(gated, w_out[...], NN).astype(bf16)
    put(me[0] ^ pl.program_id(0), o_own, o_pair, o_across, value)


def out_kernel(
    me, c0, c1, c2, c3, gate_in, y_in, dno_in, s0, s1, s2, s3, gain_out,
    bundle, d_gate, dy_out, sums,
    cot, acc_out, acc_sum, normed_out,
):
    i = pl.program_id(0)
    g = me[0]

    @pl.when(i == 0)
    def _():
        for ref in (acc_out, acc_sum):
            ref[...] = jnp.zeros_like(ref)

    pick(g ^ i, (c0, c1, c2, c3), cot)
    totals = to_columns((s0[0] + s1[0]) + (s2[0] + s3[0]))
    for s in range(ROWS // SPAN):
        rows = slice(s * SPAN, (s + 1) * SPAN)
        rms = lax.rsqrt(totals[:, 2 * s : 2 * s + 1] * (1.0 / DI) + epsilon)
        mean = rms * rms * rms * totals[:, 2 * s + 1 : 2 * s + 2] * (1.0 / DI)
        gate = gate_in[rows, :].astype(f32)
        sig = jax.nn.sigmoid(gate)
        silu = gate * sig
        y = y_in[rows, :]
        gated = y * silu
        scaled = gated * rms
        normed_out[rows, :] = (scaled * gain_out[...]).astype(bf16)
        dno = dno_in[rows, :]
        acc_sum[0:1, :] += jnp.sum(dno * scaled, axis=0, keepdims=True)
        d_gated = rms * gain_out[...] * dno - gated * mean
        dy_out[rows, :] = d_gated * silu
        d_gate[rows, :] = (d_gated * y * (sig * (1.0 + gate * (1.0 - sig)))).astype(bf16)
    acc_out[...] += mm(normed_out[...], cot[...], TN)

    @pl.when(i == pl.num_programs(0) - 1)
    def _():
        sums[...] = acc_sum[...]
        for t in range(6):
            bundle[XW * t : XW * t + XW, :] = acc_out[:, 128 * t : 128 * t + 128].astype(bf16)


def split_sum(rows, ones):
    high = rows.astype(bf16)
    rest = rows - high.astype(f32)
    return mm(high, ones, NN) + mm(rest, ones, NN)


def backward_block(
    w_full, normed, proj, v_in, states, dy_in, d_gate, pos, taps, dtb, rate, skip, ones,
    d_state, ext, acc_in, acc_dt, acc_small, d_proj,
):
    row_at = lax.broadcasted_iota(jnp.int32, (SPAN, SPAN), 0)
    lane_at = lax.broadcasted_iota(jnp.int32, (SPAN, SPAN), 1)
    later = (row_at <= lane_at).astype(f32)

    def add(row, value):
        width = value.shape[1]
        acc_small[row : row + 1, :width] += value

    def down(value):
        return jnp.sum(value, axis=0, keepdims=True)

    d_proj[:, :XW] = d_gate[...]
    for s in reversed(range(ROWS // SPAN)):
        at = s * SPAN
        rows = slice(at, at + SPAN)
        dy = dy_in[rows, :]
        dt_rows = proj[rows, XW + CL :].astype(f32) + dtb[...]
        cols, step, step_t, cum, decay, carried, tails, low = span_decays(
            dt_rows, rate[...], pos[s]
        )
        v = v_in[rows, :]
        sig_v = jax.nn.sigmoid(v)
        conv = v * sig_v
        x, b_rows, c_rows = conv[:, :XW], conv[:, XW : XW + NS], conv[:, XW + NS :]
        add(1, down(dy * x))
        state = states[s]
        state_grad = d_state[...]
        scores = mm(c_rows, b_rows, NT)
        from_state = mm(c_rows, state, NN)
        from_grad = mm(b_rows, state_grad, NN)
        carried_all = jnp.concatenate(carried, axis=1)
        tails_all = jnp.concatenate(tails, axis=1)
        dy_carried = dy * carried_all
        x_tail = x * tails_all
        d_scores = jnp.zeros((SPAN, SPAN), f32)
        row_sums = jnp.zeros((SPAN, SPAN), f32)
        col_sums, dxs = [], []
        for p in range(HL // 2):
            lanes = slice(p * SPAN, (p + 1) * SPAN)
            xp, dyp = x[:, lanes], dy[:, lanes]
            halves = jnp.concatenate([jnp.where(low, dyp, 0.0), jnp.where(low, 0.0, dyp)], axis=0)
            d_mixing = mm(halves, xp, NT)
            mixing = []
            for k in range(2):
                h = 2 * p + k
                kept = decay(h)
                kept_step = kept * step_t[h : h + 1, :]
                mixing.append(kept_step * scores)
                d_mix = d_mixing[k * SPAN : (k + 1) * SPAN, :]
                d_scores = d_scores + d_mix * kept_step
                plain = d_mix * kept * scores
                col_sums.append(down(plain))
                row_sum = jnp.sum(plain * step_t[h : h + 1, :], axis=1, keepdims=True)
                row_sums = jnp.where(lane_at == h, row_sum, row_sums)
            inner = mm(jnp.concatenate(mixing, axis=0), halves, TN)
            dxs.append(inner + skip[:, lanes] * dyp + tails[p] * from_grad[:, lanes])
        dx = jnp.concatenate(dxs, axis=1)
        d_c = mm(d_scores, b_rows, NN) + mm(dy_carried, state, NT)
        d_b = mm(d_scores, c_rows, TN) + mm(x_tail, state_grad, NT)

        end_decay = carried_all[SPAN - 1 :, :]
        through = end_decay * down(state * state_grad)
        last = lax.broadcasted_iota(jnp.int32, (SPAN, XW), 0) == SPAN - 1
        from_start = split_sum(
            dy_carried * from_state + jnp.where(last, through, 0.0), ones[...]
        )
        to_end = split_sum(x * from_grad, ones[...])
        end_plain = jnp.exp(cum[SPAN - 1 :, :] - cum) * cols[:, 5:6]
        to_end_kept = to_end * end_plain
        to_end_step = to_end_kept * step
        col_sum = to_columns(jnp.concatenate(col_sums, axis=0))
        d_cum = row_sums - col_sum * step + from_start - to_end_step
        d_cum = d_cum + jnp.where(row_at == SPAN - 1, down(to_end_step), 0.0)
        d_log = mm_exact(later, d_cum, NN)
        d_step = col_sum + to_end_kept + rate[...] * d_log
        d_dt = d_step * jax.nn.sigmoid(dt_rows)
        add(2, down(d_dt))
        add(3, down(d_log * step) * rate[...])
        d_proj[rows, XW + CL :] = d_dt.astype(bf16)
        d_state[...] = end_decay * state_grad + mm(c_rows, dy_carried, TN)

        dv = jnp.concatenate([dx, d_b, d_c], axis=1) * (sig_v * (1.0 + v * (1.0 - sig_v)))
        ext[rows, :] = dv
        add(4, down(dv))
        conv_in = proj[rows, XW : XW + CL].astype(f32)
        add(8, down(dv * conv_in))
        d_conv = taps[3:4, :] * dv
        for lag in range(1, 4):
            window = ext[at + lag : at + lag + SPAN, :] * cols[:, 5 + lag : 6 + lag]
            d_conv = d_conv + taps[3 - lag : 4 - lag, :] * window
            add(8 - lag, down(window * conv_in))
        d_proj[rows, XW : XW + CL] = d_conv.astype(bf16)

    ext[ROWS:, :] = ext[0:8, :]
    d_normed = mm(d_proj[...], w_full[...], NT)
    add(9, down(d_normed * normed[...].astype(f32)))
    acc_in[...] += mm(normed[...], d_proj[:, : XW + CL], TN)
    acc_dt[...] += mm(d_proj[:, XW + CL :], normed[...], TN)[0:8, :]
    return d_normed.astype(bf16)


def backward_kernel(
    me, w_full, normed, proj, v_in, states, dy_in, d_gate, pos, taps, dtb, rate, skip, ones, sums,
    bundle, n_own, n_pair, n_across,
    d_state, ext, acc_in, acc_dt, acc_small, d_proj, small,
):
    i = pl.num_programs(0) - 1 - pl.program_id(0)
    g = me[0]

    @pl.when(pl.program_id(0) == 0)
    def _():
        for ref in (d_state, acc_in, acc_dt, acc_small, small):
            ref[...] = jnp.zeros_like(ref)
        ext[ROWS:, :] = jnp.zeros((8, CL), f32)

    value = backward_block(
        w_full, normed, proj, v_in, states, dy_in, d_gate, pos, taps, dtb, rate, skip, ones,
        d_state, ext, acc_in, acc_dt, acc_small, d_proj,
    )
    put(g ^ i, n_own, n_pair, n_across, value)

    @pl.when(i == 0)
    def _():
        def lay(start, source, row, tiles):
            for k in range(4):
                for t in range(tiles):
                    small[k, start + t : start + t + 1, :] = source[
                        row : row + 1, 128 * t : 128 * t + 128
                    ]

        for j in range(4):
            lay(16 + 5 * j, acc_small, 5 + j, 5)
        lay(36, acc_small, 4, 5)
        lay(43, sums, 0, 3)
        lay(46, acc_small, 1, 3)
        lay(49, acc_small, 2, 1)
        lay(50, acc_small, 3, 1)
        for k in range(4):
            for tile in range(8):
                for q in range(4):
                    bundle[4 * tile + q, 48 * k : 48 * k + 48, :] = acc_in[
                        192 * k + 48 * q : 192 * k + 48 * q + 48, 128 * tile : 128 * tile + 128
                    ].astype(bf16)
            first, second = 192 * k, 192 * k + 128
            for h in range(HL):
                small[k, 2 * h : 2 * h + 1, :] = acc_dt[h : h + 1, first : first + 128]
                small[k, 2 * h + 1 : 2 * h + 2, 0:64] = acc_dt[h : h + 1, second : second + 64]
            small[k, 41:42, :] = acc_small[9:10, first : first + 128]
            small[k, 42:43, 0:64] = acc_small[9:10, second : second + 64]
        for r in range(32):
            if r < 16:
                value = jnp.concatenate([small[k, 4 * r : 4 * r + 4, :] for k in range(4)], axis=0)
            else:
                value = jnp.zeros((16, 128), f32)
            bundle[r, 192:208, :] = value.astype(bf16)


def w_out_kernel(place, p0, p1, p2, p3, grad_out):
    for d, part in enumerate((p0, p1, p2, p3)):
        source = (place[0] + 4 - d) % 4
        for j in range(3):
            half = 3 * source + j
            rows = pl.ds(pl.multiple_of((half % 2) * 192, 64), 192)
            lanes = pl.ds(pl.multiple_of((half // 2) * 128, 128), 128)
            grad_out[rows, lanes] = part[192 * j : 192 * j + 192, :].astype(f32)


def assemble_kernel(
    me, parts, shorts, gain_in,
    grad_in, grad_kernel, grad_bias, grad_gain_in, grad_gain_out, grad_skip, grad_dt, grad_log,
    wide, turned,
):
    g = me[0]
    for tile in range(8):
        for q in range(4):
            pieces = [parts[32 * k + 4 * tile + q, 0:48, :].astype(f32) for k in range(4)]
            rows = slice(48 * q, 48 * q + 48)
            if tile < 6:
                for k in range(4):
                    start = (tile // 3) * DI + k * XW + (tile % 3) * 128
                    grad_in[rows, start : start + 128] = pieces[k]
            else:
                start = 2 * DI + 128 * (tile - 6)
                grad_in[rows, start : start + 128] = (pieces[0] + pieces[1]) + (
                    pieces[2] + pieces[3]
                )

    turned[...] = jnp.zeros_like(turned)
    wide[...] = jnp.zeros_like(wide)
    gain = jnp.zeros((2, 128), f32)
    for k in range(4):
        rest = shorts[k]
        for h in range(HL):
            at = HL * k + h
            turned[at : at + 1, 0:128] = rest[2 * h : 2 * h + 1, :]
            turned[at : at + 1, 128:256] = rest[2 * h + 1 : 2 * h + 2, :]
        for j in range(5):
            for t in range(3):
                lanes = slice(k * XW + 128 * t, k * XW + 128 * t + 128)
                wide[j : j + 1, lanes] = rest[16 + 5 * j + t : 17 + 5 * j + t, :]
            for t in range(3, 5):
                lanes = slice(DI + 128 * (t - 3), DI + 128 * (t - 2))
                wide[j : j + 1, lanes] += rest[16 + 5 * j + t : 17 + 5 * j + t, :]
        gain = gain + rest[41:43, :]
    grad_in[:, DI + CW :] = turned[...].T[0:192, 0:NH]
    grad_gain_in[:, 0:128] = gain[0:1, :] / gain_in[:, 0:128]
    grad_gain_in[:, 128:192] = gain[1:2, 0:64] / gain_in[:, 128:192]
    for k in range(4):

        @pl.when(g == k)
        def _(k=k):
            grad_kernel[...] = wide[0:4, 448 * k : 448 * k + 448]
            grad_bias[...] = wide[4:5, 448 * k : 448 * k + 448]

    own = shorts[g]
    grad_gain_out[...] = jnp.concatenate([own[43 + t : 44 + t, :] for t in range(3)], axis=1).reshape(XW)
    lane_at = lax.broadcasted_iota(jnp.int32, (1, 128), 1)
    skips = jnp.zeros((1, 128), f32)
    for t in range(3):
        row = own[46 + t : 47 + t, :]
        first = jnp.sum(jnp.where(lane_at < HP, row, 0.0), axis=1, keepdims=True)
        second = jnp.sum(jnp.where(lane_at < HP, 0.0, row), axis=1, keepdims=True)
        skips = jnp.where(lane_at == 2 * t, first, skips)
        skips = jnp.where(lane_at == 2 * t + 1, second, skips)
    grad_skip[...] = skips[:, 0:HL]
    grad_dt[...] = own[49:50, 0:HL]
    grad_log[...] = own[50:51, 0:HL]


def whole(shape):
    zeros = (0,) * len(shape)
    return pl.BlockSpec(shape, lambda i: zeros)


def blocked(shape, place):
    zeros = (0,) * (len(shape) - 1)
    return pl.BlockSpec(shape, lambda i: (place(i),) + zeros)


scalar_spec = pl.BlockSpec(memory_space=pltpu.SMEM)
vmem_spec = pl.BlockSpec(memory_space=pltpu.VMEM)


def shape(dims, dtype):
    return jax.ShapeDtypeStruct(dims, dtype)


def call(body, name, micros, **kwargs):
    return pl.pallas_call(
        body,
        name=name,
        compiler_params=pltpu.CompilerParams(vmem_limit_bytes=vmem_bytes),
        cost_estimate=pl.CostEstimate(
            flops=int(micros * 1e9), bytes_accessed=1 << 20, transcendentals=0
        ),
        **kwargs,
    )


def among(value, d):
    return lax.ppermute(value, "group", [(i, i ^ d) for i in range(4)])


def local(
    tokens, segments, cotangent, gain_in, w_in, kernel, conv_bias, dt_bias, a_log, skip_gain,
    gain_out, w_out,
):
    reps = lax.axis_size("rep")
    g = lax.axis_index("group")
    me = g.astype(jnp.int32).reshape(1)
    tok = tokens.reshape(ROWS, D)
    cot = cotangent.reshape(ROWS, D)
    part = whole((ROWS, D))
    blocks = 4

    w0, w1, w2, w3a, w3b, both0 = call(
        columns_kernel,
        "columns",
        2,
        in_specs=[scalar_spec] + [vmem_spec] * 6,
        out_specs=[vmem_spec] * 6,
        out_shape=(shape((192, PW), bf16),) * 3
        + (shape((192, CUT), bf16), shape((192, PW - CUT), bf16), shape((ROWS + 16, D), bf16)),
        scratch_shapes=[pltpu.VMEM((16, D), f32), pltpu.VMEM((192, PW), bf16)],
    )(
        me, w_in, tok, kernel, conv_bias, gain_in,
        segments.reshape(1, ROWS),
    )

    def across(value, d):
        pairs = [(i * reps + r, (i ^ d) * reps + (r ^ 1)) for r in range(reps) for i in range(4)]
        return lax.ppermute(value, ("group", "rep"), pairs)

    w2 = across(w2, 2)
    both2 = among(both0, 2)
    w3b = across(w3b, 3)
    w3a = among(w3a, 3)
    both2, both0, cot_late, w1 = lax.optimization_barrier((both2, both0, cot, w1))
    w1 = among(w1, 1)
    both1 = among(both0, 1)
    both3 = among(both2, 1)
    c2 = among(cot_late, 2)
    c1 = among(cot_late, 1)
    c3 = among(cot_late, 3)
    length = blocks * ROWS
    spans = length // SPAN

    dtb = jnp.pad(dt_bias.astype(f32), (0, 128 - HL)).reshape(1, 128)
    rate = jnp.pad(-jnp.exp(a_log.astype(f32)), (0, 128 - HL)).reshape(1, 128)
    skip = jnp.repeat(skip_gain.astype(f32), HP).reshape(1, XW)
    gain_o = gain_out.astype(f32).reshape(1, XW)

    def up(i):
        return i

    by_owner_specs = [part, whole((2 * ROWS, D)), part]
    by_owner_shapes = tuple(shape((n * ROWS, D), bf16) for n in (1, 2, 1))

    def to_core(own, pair, over):
        got = among(pair, 1)
        other = (over.astype(f32) + got[ROWS:].astype(f32)).astype(bf16)
        return own, got[:ROWS], other

    def to_owner(own, got, other):
        return own, got, among(other, 2)

    w_full, normed, proj, v_rows, states, y_rows, pos, taps, gain_in_all = call(
        forward_kernel,
        "forward",
        15,
        grid=(blocks,),
        in_specs=[scalar_spec]
        + [whole((ROWS + 16, D))] * 4
        + [whole((192, PW))] * 3
        + [whole((192, CUT)), whole((192, PW - CUT))]
        + [whole((1, 128)), whole((1, 128)), whole((1, XW))],
        out_specs=[
            whole((D, PW)),
            blocked((ROWS, D), up),
            blocked((ROWS, PW), up),
            blocked((ROWS, CL), up),
            blocked((2, NS, XW), up),
            blocked((ROWS, XW), up),
            whole((8, 16, SPAN)),
            whole((8, CL)),
            whole((1, D)),
        ],
        out_shape=(
            shape((D, PW), bf16),
            shape((length, D), bf16),
            shape((length, PW), bf16),
            shape((length, CL), f32),
            shape((spans, NS, XW), f32),
            shape((length, XW), f32),
            shape((spans, 16, SPAN), f32),
            shape((8, CL), f32),
            shape((1, D), f32),
        ),
        scratch_shapes=[
            pltpu.VMEM((ROWS, D), bf16),
            pltpu.VMEM((NS, XW), f32),
            pltpu.VMEM((ROWS + 8, CL), f32),
            pltpu.VMEM((8, CW), f32),
            pltpu.VMEM((8, 128), f32),
        ],
    )(
        me, both0, both1, both2, both3, w0, w1, w2, w3a, w3b, dtb, rate, skip,
    )

    gate_spec = pl.BlockSpec((ROWS, XW), lambda i: (i, 0))
    dno, stats = call(
        sums_kernel,
        "sums",
        4,
        grid=(blocks,),
        in_specs=[scalar_spec]
        + [part] * 4
        + [gate_spec, blocked((ROWS, XW), up), whole((1, XW)), whole((XW, D))],
        out_specs=[blocked((ROWS, XW), up), blocked((1, 8, SPAN), up)],
        out_shape=(shape((length, XW), f32), shape((blocks, 8, SPAN), f32)),
        scratch_shapes=[pltpu.VMEM((ROWS, D), bf16)],
    )(me, cot, c1, c2, c3, proj, y_rows, gain_o, w_out)
    all_stats = [stats] + [among(stats, d) for d in range(1, 4)]

    o_parts = call(
        branch_kernel,
        "branch",
        3,
        grid=(blocks,),
        in_specs=[
            scalar_spec, gate_spec, blocked((ROWS, XW), up), whole((1, XW)), whole((XW, D)),
        ],
        out_specs=by_owner_specs,
        out_shape=by_owner_shapes,
    )(me, proj, y_rows, gain_o, w_out)
    o_parts, all_stats = lax.optimization_barrier((o_parts, all_stats))

    bundle1, d_gate, dy, sums = call(
        out_kernel,
        "out",
        6,
        grid=(blocks,),
        in_specs=[scalar_spec]
        + [part] * 4
        + [gate_spec, blocked((ROWS, XW), up), blocked((ROWS, XW), up)]
        + [blocked((1, 8, SPAN), up)] * 4
        + [whole((1, XW))],
        out_specs=[
            whole((2304, 128)), blocked((ROWS, XW), up), blocked((ROWS, XW), up), whole((8, XW)),
        ],
        out_shape=(
            shape((2304, 128), bf16), shape((length, XW), bf16), shape((length, XW), f32),
            shape((8, XW), f32),
        ),
        scratch_shapes=[
            pltpu.VMEM((ROWS, D), bf16),
            pltpu.VMEM((XW, D), f32),
            pltpu.VMEM((8, XW), f32),
            pltpu.VMEM((ROWS, XW), bf16),
        ],
    )(me, cot, c1, c2, c3, proj, y_rows, dno, *all_stats, gain_o)

    def spread(value):
        return lax.all_to_all(value, "rep", 0, 0, tiled=True)

    received1 = spread(bundle1.reshape(reps, 72, 128))
    branches = to_core(*o_parts)
    dy, branches = lax.optimization_barrier((dy, branches))
    branches = to_owner(*branches)
    ones = jnp.asarray(np.arange(XW)[:, None] // HP == np.arange(128)[None, :], bf16)

    def back(i):
        return blocks - 1 - i

    bundle2, *n_parts = call(
        backward_kernel,
        "backward",
        26,
        grid=(blocks,),
        in_specs=[
            scalar_spec,
            whole((D, PW)),
            blocked((ROWS, D), back),
            blocked((ROWS, PW), back),
            blocked((ROWS, CL), back),
            blocked((2, NS, XW), back),
            blocked((ROWS, XW), back),
            blocked((ROWS, XW), back),
            blocked((2, 16, SPAN), back),
            whole((8, CL)), whole((1, 128)), whole((1, 128)), whole((1, XW)), whole((XW, 128)),
            whole((8, XW)),
        ],
        out_specs=[whole((32, 208, 128))] + by_owner_specs,
        out_shape=(shape((32, 208, 128), bf16),) + by_owner_shapes,
        scratch_shapes=[
            pltpu.VMEM((NS, XW), f32),
            pltpu.VMEM((ROWS + 8, CL), f32),
            pltpu.VMEM((D, XW + CL), f32),
            pltpu.VMEM((8, D), f32),
            pltpu.VMEM((16, D), f32),
            pltpu.VMEM((ROWS, PW), bf16),
            pltpu.VMEM((4, 64, 128), f32),
        ],
    )(
        me, w_full, normed, proj, v_rows, states, dy, d_gate, pos, taps, dtb, rate, skip, ones,
        sums,
    )

    def total(received):
        return jnp.sum(received.astype(f32), axis=0).astype(bf16)

    r = lax.axis_index("rep")

    def along(value, step):
        stride, by = step
        pairs = [
            (n, n - (n // stride % 4) * stride + ((n // stride + by) % 4) * stride)
            for n in range(reps)
        ]
        return lax.ppermute(value, "rep", pairs)

    bundle2, received1, branches = lax.optimization_barrier((bundle2, received1, branches))
    received2 = spread(bundle2)
    d_parts = to_core(*n_parts)
    d_parts = to_owner(*d_parts)
    mine = total(received1)
    other = lax.ppermute(mine, "rep", [(n, n ^ 1) for n in range(reps)])
    two = jnp.where(r % 2 == 0, jnp.stack([mine, other]), jnp.stack([other, mine]))
    z_parts = [along(two, (2, by)) for by in (3, 2, 1)] + [two]
    z_all = jnp.stack(z_parts + z_parts[:3])
    eight = lax.dynamic_slice_in_dim(z_all, 3 - r // 2 % 4, 4, axis=0).reshape(576, 128)
    reduced2, eight, d_parts = lax.optimization_barrier((total(received2), eight, d_parts))
    x_parts = [eight] + [along(eight, (8, by)) for by in (1, 2, 3)]
    payload = jnp.concatenate(
        [
            reduced2[:192].reshape(4, 48, 128),
            reduced2[192:].reshape(4, 4, 128),
            jnp.zeros((4, 4, 128), bf16),
        ],
        axis=1,
    )
    parts = lax.all_to_all(
        jnp.broadcast_to(payload[:, None], (4, reps, 56, 128)).reshape(4 * reps, 56, 128),
        ("group", "rep"), 0, 0, tiled=True,
    )
    shorts = parts.reshape(4, reps, 56, 128)[:, :16, 48:52].astype(f32).reshape(4, 64, 128)
    place = (r // 8).astype(jnp.int32).reshape(1)
    grad_w_out = call(
        w_out_kernel,
        "w_out",
        2,
        in_specs=[scalar_spec] + [vmem_spec] * 4,
        out_specs=vmem_spec,
        out_shape=shape((XW, D), f32),
    )(place, *x_parts)

    x = tok.astype(f32)
    branch = sum(value.astype(f32) for value in branches)
    squares = sum(lax.dynamic_index_in_dim(v, g, 0, keepdims=False) for v in all_stats)
    rms_out = lax.rsqrt(squares[0:4:2].reshape(ROWS, 1) * (1.0 / DI) + epsilon)
    layer_out = (x + rms_out * branch).astype(bf16).reshape(tokens.shape)
    d_normed = sum(value.astype(f32) for value in d_parts)
    rms_in = lax.rsqrt(jnp.mean(x * x, axis=-1, keepdims=True) + epsilon)
    scaled = d_normed * gain_in_all
    grad_tokens = (
        cot.astype(f32)
        + rms_in * scaled
        - x * (rms_in * rms_in * rms_in * jnp.mean(x * scaled, axis=-1, keepdims=True))
    ).reshape(tokens.shape)

    grads = call(
        assemble_kernel,
        "assemble",
        4,
        in_specs=[scalar_spec] + [vmem_spec] * 3,
        out_specs=[vmem_spec] * 8,
        out_shape=(
            shape((192, 3352), f32), shape((4, 448), f32),
            shape((1, 448), f32), shape((1, 192), f32), shape((XW,), f32), shape((1, HL), f32),
            shape((1, HL), f32), shape((1, HL), f32),
        ),
        scratch_shapes=[pltpu.VMEM((8, CW), f32), pltpu.VMEM((128, 256), f32)],
    )(me, parts, shorts, gain_in.astype(f32).reshape(1, 192))
    grad_w_in, grad_kernel, grad_bias, grad_gi, grad_go, grad_s, grad_d, grad_l = grads
    return (
        layer_out,
        grad_tokens,
        grad_gi.reshape(-1),
        grad_w_in,
        grad_kernel,
        grad_bias.reshape(-1),
        grad_d.reshape(-1),
        grad_l.reshape(-1),
        grad_s.reshape(-1),
        grad_go,
        grad_w_out,
    )


def solution(mesh):
    sequences = P("rep", "group", None)
    vector = P("group")
    matrix = P("group", None)
    return jax.shard_map(
        local,
        mesh=mesh,
        in_specs=(
            sequences, P("rep", "group"), sequences, vector, matrix, P(None, "group"),
            vector, vector, vector, vector, vector, matrix,
        ),
        out_specs=(
            sequences, sequences, vector, matrix, P(None, "group"), vector, vector, vector,
            vector, vector, matrix,
        ),
        check_vma=False,
    )
```

```python
import jax
import jax.numpy as jnp
import numpy as np
from jax import lax
from jax.experimental import pallas as pl
from jax.experimental.pallas import tpu as pltpu
from jax.sharding import PartitionSpec as P

D = 768
NH = 24
HP = 64
NS = 128
DI = 1536
CW = 1792
SPAN = 128
ROWS = 256
HL = 6
XW = HL * HP
CL = XW + 2 * NS
PW = XW + CL + 128
CUT = 640
epsilon = 1e-05
f32 = jnp.float32
bf16 = jnp.bfloat16
NN = ((1,), (0,))
NT = ((1,), (1,))
TN = ((0,), (0,))
vmem_bytes = 56 * 1024 * 1024


def mm(a, b, dims):
    return lax.dot_general(
        a.astype(bf16), b.astype(bf16), (dims, ((), ())), preferred_element_type=f32
    )


def mm_exact(a, b, dims):
    return lax.dot_general(
        a, b, (dims, ((), ())), preferred_element_type=f32, precision=lax.Precision.HIGHEST
    )


def to_columns(rows):
    short = SPAN - rows.shape[0]
    return jnp.concatenate([rows, jnp.zeros((short, SPAN), f32)], axis=0).T


def softplus(v):
    return jnp.maximum(v, 0.0) + jnp.log1p(jnp.exp(-jnp.abs(v)))


def over_lanes(column):
    return jnp.broadcast_to(column, (SPAN, SPAN))


def span_decays(dt_rows, rate, pos_rows):
    row_at = lax.broadcasted_iota(jnp.int32, (SPAN, SPAN), 0)
    lane_at = lax.broadcasted_iota(jnp.int32, (SPAN, SPAN), 1)
    pos = to_columns(pos_rows)
    step = softplus(dt_rows)
    cum = mm_exact((row_at >= lane_at).astype(f32), step * rate, NN)
    cum_t = cum.T
    step_t = step.T
    allowed = (over_lanes(pos[:, 0:1]) == pos_rows[0:1, :]) & (row_at >= lane_at)
    low = lane_at < HP
    cums = [over_lanes(cum[:, h : h + 1]) for h in range(HL)]
    linked = pos[:, 4:5]
    tail = pos[:, 5:6]
    carried, tails = [], []
    for p in range(HL // 2):
        both = jnp.where(low, cums[2 * p], cums[2 * p + 1])
        steps = jnp.where(
            low, over_lanes(step[:, 2 * p : 2 * p + 1]), over_lanes(step[:, 2 * p + 1 : 2 * p + 2])
        )
        carried.append(jnp.exp(both) * linked)
        tails.append(jnp.exp(both[SPAN - 1 :, :] - both) * tail * steps)

    def decay(h):
        return jnp.where(allowed, jnp.exp(jnp.minimum(cums[h] - cum_t[h : h + 1, :], 0.0)), 0.0)

    return pos, step, step_t, cum, decay, carried, tails, low


def pick(index, sources, target):
    for d, source in enumerate(sources):

        @pl.when(index == d)
        def _(source=source):
            target[...] = source[...]


def put(index, own, pair, across, value):
    low, high = pair.at[0:ROWS, :], pair.at[ROWS : 2 * ROWS, :]
    for d, target in enumerate((own, low, across, high)):

        @pl.when(index == d)
        def _(target=target):
            target[...] = value


def columns_kernel(
    me, w_in, tok, taps, bias, gain_in, seg, w0, w1, w2, w3a, w3b, out, rows, last
):
    g = me[0]
    for d, send in enumerate((w0, w1, w2, last)):
        start = (g ^ d) * XW
        send[:, :XW] = w_in[:, pl.ds(pl.multiple_of(start, 128), XW)]
        send[:, XW : 2 * XW] = w_in[:, pl.ds(pl.multiple_of(DI + start, 128), XW)]
        send[:, 2 * XW : XW + CL] = w_in[:, 2 * DI : DI + CW]
        send[:, XW + CL :] = jnp.concatenate(
            [w_in[:, DI + CW :], jnp.zeros((192, 128 - NH), bf16)], axis=1
        )
    w3a[...] = last[:, :CUT]
    w3b[...] = last[:, CUT:]
    out[0:ROWS, :] = tok[...]
    rows[...] = jnp.zeros_like(rows)
    rows[0:4, 0:448] = taps[...].astype(f32)
    rows[4:5, 0:448] = bias[...].astype(f32).reshape(1, 448)
    rows[5:6, 0:192] = gain_in[...].astype(f32).reshape(1, 192)
    rows[6:7, 0:ROWS] = seg[...].astype(f32)
    out[ROWS : ROWS + 16, :] = rows[...].astype(bf16)


def gather_short(g, parts, taps, gain_in, pos, wide, seg):
    for d, part in enumerate(parts):
        rows = part[ROWS : ROWS + 16, :].astype(f32)
        for k in range(4):

            @pl.when((g ^ d) == k)
            def _(k=k, rows=rows):
                wide[0:5, 448 * k : 448 * k + 448] = rows[0:5, 0:448]
                gain_in[:, 192 * k : 192 * k + 192] = rows[5:6, 0:192]
                seg[2 * k : 2 * k + 1, :] = rows[6:7, 0:128]
                seg[2 * k + 1 : 2 * k + 2, :] = rows[6:7, 128:256]

    taps[...] = jnp.zeros_like(taps)
    taps[0:5, 0:XW] = wide[0:5, pl.ds(pl.multiple_of(g * XW, 128), XW)]
    taps[0:5, XW:] = wide[0:5, DI:]
    ids = seg[...]
    row_at = lax.broadcasted_iota(jnp.int32, (8, 128), 0)
    lane_at = lax.broadcasted_iota(jnp.int32, (8, 128), 1)
    one = jnp.full((1, 128), -1.0, f32)
    earlier = jnp.concatenate([one, ids[0:7]], axis=0)
    later = jnp.concatenate([ids[1:8], one], axis=0)
    ends = jnp.broadcast_to(ids[:, 127:128], (8, 128))
    starts = jnp.broadcast_to(earlier[:, 127:128], (8, 128))
    features = [ids]
    for lag in range(1, 4):
        shifted = jnp.where(
            lane_at >= lag, pltpu.roll(ids, lag, 1), pltpu.roll(earlier, lag, 1)
        )
        features.append((shifted == ids).astype(f32))
    features += [(ids == starts).astype(f32), (ids == ends).astype(f32)]
    for lag in range(1, 4):
        shifted = jnp.where(
            lane_at < 128 - lag, pltpu.roll(ids, 128 - lag, 1), pltpu.roll(later, 128 - lag, 1)
        )
        features.append((shifted == ids).astype(f32))
    pos[...] = jnp.zeros_like(pos)
    for j, feature in enumerate(features):
        for n in range(8):
            pos[n, j : j + 1, :] = feature[n : n + 1, :]


def forward_kernel(
    me, t0, t1, t2, t3, w0, w1, w2, w3a, w3b, dtb, rate, skip,
    w_full, normed, proj, v_out, states, y_out, pos, taps, gain_in,
    tok, state, ext, wide, seg,
):
    i = pl.program_id(0)
    g = me[0]

    @pl.when(i == 0)
    def _():
        row_at = lax.broadcasted_iota(jnp.int32, (128, 128), 0)
        lane_at = lax.broadcasted_iota(jnp.int32, (128, 128), 1)
        chosen = ((row_at == lane_at + g * HL) & (lane_at < HL)).astype(bf16)
        for d, part in enumerate((w0, w1, w2)):
            rows = pl.ds(pl.multiple_of((g ^ d) * 192, 64), 192)
            w_full[rows, : XW + CL] = part[:, : XW + CL]
            w_full[rows, XW + CL :] = mm(part[:, XW + CL :], chosen, NN).astype(bf16)
        rows = pl.ds(pl.multiple_of((g ^ 3) * 192, 64), 192)
        w_full[rows, :CUT] = w3a[...]
        w_full[rows, CUT : XW + CL] = w3b[:, : XW + CL - CUT]
        w_full[rows, XW + CL :] = mm(w3b[:, XW + CL - CUT :], chosen, NN).astype(bf16)
        state[...] = jnp.zeros_like(state)
        ext[0:8, :] = jnp.zeros((8, CL), f32)
        gather_short(g, (t0, t1, t2, t3), taps, gain_in, pos, wide, seg)

    for d, source in enumerate((t0, t1, t2, t3)):

        @pl.when((g ^ i) == d)
        def _(source=source):
            tok[...] = source[0:ROWS, :]

    x = tok[...].astype(f32)
    rms = lax.rsqrt(jnp.mean(x * x, axis=-1, keepdims=True) + epsilon)
    low_rows = (x * rms * gain_in[...]).astype(bf16)
    normed[...] = low_rows
    proj[...] = mm(low_rows, w_full[...], NN).astype(bf16)
    ext[8 : 8 + ROWS, :] = proj[:, XW : XW + CL].astype(f32)
    for s in range(ROWS // SPAN):
        at = s * SPAN
        rows = slice(at, at + SPAN)
        dt_rows = proj[rows, XW + CL :].astype(f32) + dtb[...]
        pos_rows = pos[2 * i + s]
        cols, step, step_t, cum, decay, carried, tails, low = span_decays(
            dt_rows, rate[...], pos_rows
        )
        v = taps[4:5, :] + taps[3:4, :] * ext[8 + at : 8 + at + SPAN, :]
        for lag in range(1, 4):
            window = ext[8 + at - lag : 8 + at - lag + SPAN, :]
            v = v + (taps[3 - lag : 4 - lag, :] * cols[:, lag : lag + 1]) * window
        v_out[rows, :] = v
        conv = v * jax.nn.sigmoid(v)
        b_rows, c_rows = conv[:, XW : XW + NS], conv[:, XW + NS :]
        scores = mm(c_rows, b_rows, NT)
        states[s] = state[...]
        from_state = mm(c_rows, state[...], NN)
        ys, ends, decays_end = [], [], []
        for p in range(HL // 2):
            lanes = slice(p * SPAN, (p + 1) * SPAN)
            xp = conv[:, lanes]
            mixing = [
                decay(h) * scores * step_t[h : h + 1, :] for h in (2 * p, 2 * p + 1)
            ]
            inner = mm(
                jnp.concatenate(mixing, axis=1),
                jnp.concatenate([jnp.where(low, xp, 0.0), jnp.where(low, 0.0, xp)], axis=0),
                NN,
            )
            ys.append(inner + carried[p] * from_state[:, lanes] + skip[:, lanes] * xp)
            ends.append(tails[p] * xp)
            decays_end.append(carried[p][SPAN - 1 :, :])
        y_out[rows, :] = jnp.concatenate(ys, axis=1)
        state[...] = jnp.concatenate(decays_end, axis=1) * state[...] + mm(
            b_rows, jnp.concatenate(ends, axis=1), TN
        )
    ext[0:8, :] = ext[ROWS : ROWS + 8, :]


def sums_kernel(me, c0, c1, c2, c3, gate_in, y_in, gain_out, w_out, dno_out, stats, cot):
    i = pl.program_id(0)
    pick(me[0] ^ i, (c0, c1, c2, c3), cot)
    dno = mm(cot[...], w_out[...], NT)
    dno_out[...] = dno
    gate = gate_in[...].astype(f32)
    gated = y_in[...] * (gate * jax.nn.sigmoid(gate))
    squares = jnp.sum(gated * gated, axis=-1, keepdims=True)
    products = jnp.sum(gated * gain_out[...] * dno, axis=-1, keepdims=True)
    lane_at = lax.broadcasted_iota(jnp.int32, (SPAN, SPAN), 1)
    both = jnp.zeros((SPAN, SPAN), f32)
    for s in range(ROWS // SPAN):
        rows = slice(s * SPAN, (s + 1) * SPAN)
        both = jnp.where(lane_at == 2 * s, squares[rows], both)
        both = jnp.where(lane_at == 2 * s + 1, products[rows], both)
    stats[0] = both.T[0:8, :]


def branch_kernel(me, gate_in, y_in, gain_out, w_out, o_own, o_pair, o_across):
    gate = gate_in[...].astype(f32)
    gated = y_in[...] * (gate * jax.nn.sigmoid(gate)) * gain_out[...]
    value = mm(gated, w_out[...], NN).astype(bf16)
    put(me[0] ^ pl.program_id(0), o_own, o_pair, o_across, value)


def out_kernel(
    me, c0, c1, c2, c3, gate_in, y_in, dno_in, s0, s1, s2, s3, gain_out,
    bundle, d_gate, dy_out, sums,
    cot, acc_out, acc_sum, normed_out,
):
    i = pl.program_id(0)
    g = me[0]

    @pl.when(i == 0)
    def _():
        for ref in (acc_out, acc_sum):
            ref[...] = jnp.zeros_like(ref)

    pick(g ^ i, (c0, c1, c2, c3), cot)
    totals = to_columns((s0[0] + s1[0]) + (s2[0] + s3[0]))
    for s in range(ROWS // SPAN):
        rows = slice(s * SPAN, (s + 1) * SPAN)
        rms = lax.rsqrt(totals[:, 2 * s : 2 * s + 1] * (1.0 / DI) + epsilon)
        mean = rms * rms * rms * totals[:, 2 * s + 1 : 2 * s + 2] * (1.0 / DI)
        gate = gate_in[rows, :].astype(f32)
        sig = jax.nn.sigmoid(gate)
        silu = gate * sig
        y = y_in[rows, :]
        gated = y * silu
        scaled = gated * rms
        normed_out[rows, :] = (scaled * gain_out[...]).astype(bf16)
        dno = dno_in[rows, :]
        acc_sum[0:1, :] += jnp.sum(dno * scaled, axis=0, keepdims=True)
        d_gated = rms * gain_out[...] * dno - gated * mean
        dy_out[rows, :] = d_gated * silu
        d_gate[rows, :] = (d_gated * y * (sig * (1.0 + gate * (1.0 - sig)))).astype(bf16)
    acc_out[...] += mm(normed_out[...], cot[...], TN)

    @pl.when(i == pl.num_programs(0) - 1)
    def _():
        sums[...] = acc_sum[...]
        for t in range(6):
            bundle[XW * t : XW * t + XW, :] = acc_out[:, 128 * t : 128 * t + 128].astype(bf16)


def split_sum(rows, ones):
    high = rows.astype(bf16)
    rest = rows - high.astype(f32)
    return mm(high, ones, NN) + mm(rest, ones, NN)


def backward_block(
    w_full, normed, proj, v_in, states, dy_in, d_gate, pos, taps, dtb, rate, skip, ones,
    d_state, ext, acc_in, acc_dt, acc_small, d_proj,
):
    row_at = lax.broadcasted_iota(jnp.int32, (SPAN, SPAN), 0)
    lane_at = lax.broadcasted_iota(jnp.int32, (SPAN, SPAN), 1)
    later = (row_at <= lane_at).astype(f32)

    def add(row, value):
        width = value.shape[1]
        acc_small[row : row + 1, :width] += value

    def down(value):
        return jnp.sum(value, axis=0, keepdims=True)

    d_proj[:, :XW] = d_gate[...]
    for s in reversed(range(ROWS // SPAN)):
        at = s * SPAN
        rows = slice(at, at + SPAN)
        dy = dy_in[rows, :]
        dt_rows = proj[rows, XW + CL :].astype(f32) + dtb[...]
        cols, step, step_t, cum, decay, carried, tails, low = span_decays(
            dt_rows, rate[...], pos[s]
        )
        v = v_in[rows, :]
        sig_v = jax.nn.sigmoid(v)
        conv = v * sig_v
        x, b_rows, c_rows = conv[:, :XW], conv[:, XW : XW + NS], conv[:, XW + NS :]
        add(1, down(dy * x))
        state = states[s]
        state_grad = d_state[...]
        scores = mm(c_rows, b_rows, NT)
        from_state = mm(c_rows, state, NN)
        from_grad = mm(b_rows, state_grad, NN)
        carried_all = jnp.concatenate(carried, axis=1)
        tails_all = jnp.concatenate(tails, axis=1)
        dy_carried = dy * carried_all
        x_tail = x * tails_all
        d_scores = jnp.zeros((SPAN, SPAN), f32)
        row_sums = jnp.zeros((SPAN, SPAN), f32)
        col_sums, dxs = [], []
        for p in range(HL // 2):
            lanes = slice(p * SPAN, (p + 1) * SPAN)
            xp, dyp = x[:, lanes], dy[:, lanes]
            halves = jnp.concatenate([jnp.where(low, dyp, 0.0), jnp.where(low, 0.0, dyp)], axis=0)
            d_mixing = mm(halves, xp, NT)
            mixing = []
            for k in range(2):
                h = 2 * p + k
                kept = decay(h)
                kept_step = kept * step_t[h : h + 1, :]
                mixing.append(kept_step * scores)
                d_mix = d_mixing[k * SPAN : (k + 1) * SPAN, :]
                d_scores = d_scores + d_mix * kept_step
                plain = d_mix * kept * scores
                col_sums.append(down(plain))
                row_sum = jnp.sum(plain * step_t[h : h + 1, :], axis=1, keepdims=True)
                row_sums = jnp.where(lane_at == h, row_sum, row_sums)
            inner = mm(jnp.concatenate(mixing, axis=0), halves, TN)
            dxs.append(inner + skip[:, lanes] * dyp + tails[p] * from_grad[:, lanes])
        dx = jnp.concatenate(dxs, axis=1)
        d_c = mm(d_scores, b_rows, NN) + mm(dy_carried, state, NT)
        d_b = mm(d_scores, c_rows, TN) + mm(x_tail, state_grad, NT)

        end_decay = carried_all[SPAN - 1 :, :]
        through = end_decay * down(state * state_grad)
        last = lax.broadcasted_iota(jnp.int32, (SPAN, XW), 0) == SPAN - 1
        from_start = split_sum(
            dy_carried * from_state + jnp.where(last, through, 0.0), ones[...]
        )
        to_end = split_sum(x * from_grad, ones[...])
        end_plain = jnp.exp(cum[SPAN - 1 :, :] - cum) * cols[:, 5:6]
        to_end_kept = to_end * end_plain
        to_end_step = to_end_kept * step
        col_sum = to_columns(jnp.concatenate(col_sums, axis=0))
        d_cum = row_sums - col_sum * step + from_start - to_end_step
        d_cum = d_cum + jnp.where(row_at == SPAN - 1, down(to_end_step), 0.0)
        d_log = mm_exact(later, d_cum, NN)
        d_step = col_sum + to_end_kept + rate[...] * d_log
        d_dt = d_step * jax.nn.sigmoid(dt_rows)
        add(2, down(d_dt))
        add(3, down(d_log * step) * rate[...])
        d_proj[rows, XW + CL :] = d_dt.astype(bf16)
        d_state[...] = end_decay * state_grad + mm(c_rows, dy_carried, TN)

        dv = jnp.concatenate([dx, d_b, d_c], axis=1) * (sig_v * (1.0 + v * (1.0 - sig_v)))
        ext[rows, :] = dv
        add(4, down(dv))
        conv_in = proj[rows, XW : XW + CL].astype(f32)
        add(8, down(dv * conv_in))
        d_conv = taps[3:4, :] * dv
        for lag in range(1, 4):
            window = ext[at + lag : at + lag + SPAN, :] * cols[:, 5 + lag : 6 + lag]
            d_conv = d_conv + taps[3 - lag : 4 - lag, :] * window
            add(8 - lag, down(window * conv_in))
        d_proj[rows, XW : XW + CL] = d_conv.astype(bf16)

    ext[ROWS:, :] = ext[0:8, :]
    d_normed = mm(d_proj[...], w_full[...], NT)
    add(9, down(d_normed * normed[...].astype(f32)))
    acc_in[...] += mm(normed[...], d_proj[:, : XW + CL], TN)
    acc_dt[...] += mm(d_proj[:, XW + CL :], normed[...], TN)[0:8, :]
    return d_normed.astype(bf16)


def backward_kernel(
    me, w_full, normed, proj, v_in, states, dy_in, d_gate, pos, taps, dtb, rate, skip, ones, sums,
    bundle, n_own, n_pair, n_across,
    d_state, ext, acc_in, acc_dt, acc_small, d_proj, small,
):
    i = pl.num_programs(0) - 1 - pl.program_id(0)
    g = me[0]

    @pl.when(pl.program_id(0) == 0)
    def _():
        for ref in (d_state, acc_in, acc_dt, acc_small, small):
            ref[...] = jnp.zeros_like(ref)
        ext[ROWS:, :] = jnp.zeros((8, CL), f32)

    value = backward_block(
        w_full, normed, proj, v_in, states, dy_in, d_gate, pos, taps, dtb, rate, skip, ones,
        d_state, ext, acc_in, acc_dt, acc_small, d_proj,
    )
    put(g ^ i, n_own, n_pair, n_across, value)

    @pl.when(i == 0)
    def _():
        def lay(start, source, row, tiles):
            for k in range(4):
                for t in range(tiles):
                    small[k, start + t : start + t + 1, :] = source[
                        row : row + 1, 128 * t : 128 * t + 128
                    ]

        for j in range(4):
            lay(16 + 5 * j, acc_small, 5 + j, 5)
        lay(36, acc_small, 4, 5)
        lay(43, sums, 0, 3)
        lay(46, acc_small, 1, 3)
        lay(49, acc_small, 2, 1)
        lay(50, acc_small, 3, 1)
        for k in range(4):
            for tile in range(8):
                for q in range(4):
                    bundle[4 * tile + q, 48 * k : 48 * k + 48, :] = acc_in[
                        192 * k + 48 * q : 192 * k + 48 * q + 48, 128 * tile : 128 * tile + 128
                    ].astype(bf16)
            first, second = 192 * k, 192 * k + 128
            for h in range(HL):
                small[k, 2 * h : 2 * h + 1, :] = acc_dt[h : h + 1, first : first + 128]
                small[k, 2 * h + 1 : 2 * h + 2, 0:64] = acc_dt[h : h + 1, second : second + 64]
            small[k, 41:42, :] = acc_small[9:10, first : first + 128]
            small[k, 42:43, 0:64] = acc_small[9:10, second : second + 64]
        for r in range(32):
            if r < 16:
                value = jnp.concatenate([small[k, 4 * r : 4 * r + 4, :] for k in range(4)], axis=0)
            else:
                value = jnp.zeros((16, 128), f32)
            bundle[r, 192:208, :] = value.astype(bf16)


def assemble_kernel(
    me, parts, gain_in,
    grad_in, grad_out, grad_kernel, grad_bias, grad_gain_in, grad_gain_out, grad_skip, grad_dt,
    grad_log,
    wide, turned, shorts,
):
    g = me[0]
    for r in range(32):
        tile, q = r // 4, r % 4
        chunks = [parts[32 * k + r].astype(f32) for k in range(4)]
        rows = slice(48 * q, 48 * q + 48)
        if tile < 6:
            for k in range(4):
                start = (tile // 3) * DI + k * XW + (tile % 3) * 128
                grad_in[rows, start : start + 128] = chunks[k][:48]
        else:
            start = 2 * DI + 128 * (tile - 6)
            grad_in[rows, start : start + 128] = (chunks[0][:48] + chunks[1][:48]) + (
                chunks[2][:48] + chunks[3][:48]
            )
        for k in range(4):
            first = 72 * r + 18 * k
            done = 0
            while done < 18:
                column, row = divmod(first + done, XW)
                count = min(18 - done, XW - row)
                grad_out[row : row + count, 128 * column : 128 * column + 128] = chunks[k][
                    48 + done : 48 + done + count
                ]
                done += count
            if r < 16:
                shorts[k, 4 * r : 4 * r + 4, :] = chunks[k][66:70]

    turned[...] = jnp.zeros_like(turned)
    wide[...] = jnp.zeros_like(wide)
    gain = jnp.zeros((2, 128), f32)
    for k in range(4):
        rest = shorts[k]
        for h in range(HL):
            at = HL * k + h
            turned[at : at + 1, 0:128] = rest[2 * h : 2 * h + 1, :]
            turned[at : at + 1, 128:256] = rest[2 * h + 1 : 2 * h + 2, :]
        for j in range(5):
            for t in range(3):
                lanes = slice(k * XW + 128 * t, k * XW + 128 * t + 128)
                wide[j : j + 1, lanes] = rest[16 + 5 * j + t : 17 + 5 * j + t, :]
            for t in range(3, 5):
                lanes = slice(DI + 128 * (t - 3), DI + 128 * (t - 2))
                wide[j : j + 1, lanes] += rest[16 + 5 * j + t : 17 + 5 * j + t, :]
        gain = gain + rest[41:43, :]
    grad_in[:, DI + CW :] = turned[...].T[0:192, 0:NH]
    grad_gain_in[:, 0:128] = gain[0:1, :] / gain_in[:, 0:128]
    grad_gain_in[:, 128:192] = gain[1:2, 0:64] / gain_in[:, 128:192]
    for k in range(4):

        @pl.when(g == k)
        def _(k=k):
            grad_kernel[...] = wide[0:4, 448 * k : 448 * k + 448]
            grad_bias[...] = wide[4:5, 448 * k : 448 * k + 448]

    own = shorts[g]
    grad_gain_out[...] = jnp.concatenate([own[43 + t : 44 + t, :] for t in range(3)], axis=1).reshape(XW)
    lane_at = lax.broadcasted_iota(jnp.int32, (1, 128), 1)
    skips = jnp.zeros((1, 128), f32)
    for t in range(3):
        row = own[46 + t : 47 + t, :]
        first = jnp.sum(jnp.where(lane_at < HP, row, 0.0), axis=1, keepdims=True)
        second = jnp.sum(jnp.where(lane_at < HP, 0.0, row), axis=1, keepdims=True)
        skips = jnp.where(lane_at == 2 * t, first, skips)
        skips = jnp.where(lane_at == 2 * t + 1, second, skips)
    grad_skip[...] = skips[:, 0:HL]
    grad_dt[...] = own[49:50, 0:HL]
    grad_log[...] = own[50:51, 0:HL]


def whole(shape):
    zeros = (0,) * len(shape)
    return pl.BlockSpec(shape, lambda i: zeros)


def blocked(shape, place):
    zeros = (0,) * (len(shape) - 1)
    return pl.BlockSpec(shape, lambda i: (place(i),) + zeros)


scalar_spec = pl.BlockSpec(memory_space=pltpu.SMEM)
vmem_spec = pl.BlockSpec(memory_space=pltpu.VMEM)


def shape(dims, dtype):
    return jax.ShapeDtypeStruct(dims, dtype)


def call(body, name, micros, **kwargs):
    return pl.pallas_call(
        body,
        name=name,
        compiler_params=pltpu.CompilerParams(vmem_limit_bytes=vmem_bytes),
        cost_estimate=pl.CostEstimate(
            flops=int(micros * 1e9), bytes_accessed=1 << 20, transcendentals=0
        ),
        **kwargs,
    )


def among(value, d):
    return lax.ppermute(value, "group", [(i, i ^ d) for i in range(4)])


def local(
    tokens, segments, cotangent, gain_in, w_in, kernel, conv_bias, dt_bias, a_log, skip_gain,
    gain_out, w_out,
):
    reps = lax.axis_size("rep")
    g = lax.axis_index("group")
    me = g.astype(jnp.int32).reshape(1)
    tok = tokens.reshape(ROWS, D)
    cot = cotangent.reshape(ROWS, D)
    part = whole((ROWS, D))
    blocks = 4

    w0, w1, w2, w3a, w3b, both0 = call(
        columns_kernel,
        "columns",
        2,
        in_specs=[scalar_spec] + [vmem_spec] * 6,
        out_specs=[vmem_spec] * 6,
        out_shape=(shape((192, PW), bf16),) * 3
        + (shape((192, CUT), bf16), shape((192, PW - CUT), bf16), shape((ROWS + 16, D), bf16)),
        scratch_shapes=[pltpu.VMEM((16, D), f32), pltpu.VMEM((192, PW), bf16)],
    )(
        me, w_in, tok, kernel, conv_bias, gain_in,
        segments.reshape(1, ROWS),
    )

    def across(value, d):
        pairs = [(i * reps + r, (i ^ d) * reps + (r ^ 1)) for r in range(reps) for i in range(4)]
        return lax.ppermute(value, ("group", "rep"), pairs)

    w2 = across(w2, 2)
    both2 = among(both0, 2)
    w3b = across(w3b, 3)
    w3a = among(w3a, 3)
    both2, both0, cot_late, w1 = lax.optimization_barrier((both2, both0, cot, w1))
    w1 = among(w1, 1)
    both1 = among(both0, 1)
    both3 = among(both2, 1)
    c2 = among(cot_late, 2)
    c1 = among(cot_late, 1)
    c3 = among(cot_late, 3)
    length = blocks * ROWS
    spans = length // SPAN

    dtb = jnp.pad(dt_bias.astype(f32), (0, 128 - HL)).reshape(1, 128)
    rate = jnp.pad(-jnp.exp(a_log.astype(f32)), (0, 128 - HL)).reshape(1, 128)
    skip = jnp.repeat(skip_gain.astype(f32), HP).reshape(1, XW)
    gain_o = gain_out.astype(f32).reshape(1, XW)

    def up(i):
        return i

    by_owner_specs = [part, whole((2 * ROWS, D)), part]
    by_owner_shapes = tuple(shape((n * ROWS, D), bf16) for n in (1, 2, 1))

    def to_core(own, pair, over):
        got = among(pair, 1)
        other = (over.astype(f32) + got[ROWS:].astype(f32)).astype(bf16)
        return own, got[:ROWS], other

    def to_owner(own, got, other):
        return own, got, among(other, 2)

    w_full, normed, proj, v_rows, states, y_rows, pos, taps, gain_in_all = call(
        forward_kernel,
        "forward",
        15,
        grid=(blocks,),
        in_specs=[scalar_spec]
        + [whole((ROWS + 16, D))] * 4
        + [whole((192, PW))] * 3
        + [whole((192, CUT)), whole((192, PW - CUT))]
        + [whole((1, 128)), whole((1, 128)), whole((1, XW))],
        out_specs=[
            whole((D, PW)),
            blocked((ROWS, D), up),
            blocked((ROWS, PW), up),
            blocked((ROWS, CL), up),
            blocked((2, NS, XW), up),
            blocked((ROWS, XW), up),
            whole((8, 16, SPAN)),
            whole((8, CL)),
            whole((1, D)),
        ],
        out_shape=(
            shape((D, PW), bf16),
            shape((length, D), bf16),
            shape((length, PW), bf16),
            shape((length, CL), f32),
            shape((spans, NS, XW), f32),
            shape((length, XW), f32),
            shape((spans, 16, SPAN), f32),
            shape((8, CL), f32),
            shape((1, D), f32),
        ),
        scratch_shapes=[
            pltpu.VMEM((ROWS, D), bf16),
            pltpu.VMEM((NS, XW), f32),
            pltpu.VMEM((ROWS + 8, CL), f32),
            pltpu.VMEM((8, CW), f32),
            pltpu.VMEM((8, 128), f32),
        ],
    )(
        me, both0, both1, both2, both3, w0, w1, w2, w3a, w3b, dtb, rate, skip,
    )

    gate_spec = pl.BlockSpec((ROWS, XW), lambda i: (i, 0))
    dno, stats = call(
        sums_kernel,
        "sums",
        4,
        grid=(blocks,),
        in_specs=[scalar_spec]
        + [part] * 4
        + [gate_spec, blocked((ROWS, XW), up), whole((1, XW)), whole((XW, D))],
        out_specs=[blocked((ROWS, XW), up), blocked((1, 8, SPAN), up)],
        out_shape=(shape((length, XW), f32), shape((blocks, 8, SPAN), f32)),
        scratch_shapes=[pltpu.VMEM((ROWS, D), bf16)],
    )(me, cot, c1, c2, c3, proj, y_rows, gain_o, w_out)
    all_stats = [stats] + [among(stats, d) for d in range(1, 4)]

    o_parts = call(
        branch_kernel,
        "branch",
        3,
        grid=(blocks,),
        in_specs=[
            scalar_spec, gate_spec, blocked((ROWS, XW), up), whole((1, XW)), whole((XW, D)),
        ],
        out_specs=by_owner_specs,
        out_shape=by_owner_shapes,
    )(me, proj, y_rows, gain_o, w_out)
    o_parts, all_stats = lax.optimization_barrier((o_parts, all_stats))

    bundle1, d_gate, dy, sums = call(
        out_kernel,
        "out",
        6,
        grid=(blocks,),
        in_specs=[scalar_spec]
        + [part] * 4
        + [gate_spec, blocked((ROWS, XW), up), blocked((ROWS, XW), up)]
        + [blocked((1, 8, SPAN), up)] * 4
        + [whole((1, XW))],
        out_specs=[
            whole((2304, 128)), blocked((ROWS, XW), up), blocked((ROWS, XW), up), whole((8, XW)),
        ],
        out_shape=(
            shape((2304, 128), bf16), shape((length, XW), bf16), shape((length, XW), f32),
            shape((8, XW), f32),
        ),
        scratch_shapes=[
            pltpu.VMEM((ROWS, D), bf16),
            pltpu.VMEM((XW, D), f32),
            pltpu.VMEM((8, XW), f32),
            pltpu.VMEM((ROWS, XW), bf16),
        ],
    )(me, cot, c1, c2, c3, proj, y_rows, dno, *all_stats, gain_o)

    def spread(value):
        return lax.all_to_all(value, "rep", 0, 0, tiled=True)

    received1 = spread(bundle1.reshape(reps, 72, 128))
    branches = to_core(*o_parts)
    dy, branches = lax.optimization_barrier((dy, branches))
    branches = to_owner(*branches)
    ones = jnp.asarray(np.arange(XW)[:, None] // HP == np.arange(128)[None, :], bf16)

    def back(i):
        return blocks - 1 - i

    bundle2, *n_parts = call(
        backward_kernel,
        "backward",
        26,
        grid=(blocks,),
        in_specs=[
            scalar_spec,
            whole((D, PW)),
            blocked((ROWS, D), back),
            blocked((ROWS, PW), back),
            blocked((ROWS, CL), back),
            blocked((2, NS, XW), back),
            blocked((ROWS, XW), back),
            blocked((ROWS, XW), back),
            blocked((2, 16, SPAN), back),
            whole((8, CL)), whole((1, 128)), whole((1, 128)), whole((1, XW)), whole((XW, 128)),
            whole((8, XW)),
        ],
        out_specs=[whole((32, 208, 128))] + by_owner_specs,
        out_shape=(shape((32, 208, 128), bf16),) + by_owner_shapes,
        scratch_shapes=[
            pltpu.VMEM((NS, XW), f32),
            pltpu.VMEM((ROWS + 8, CL), f32),
            pltpu.VMEM((D, XW + CL), f32),
            pltpu.VMEM((8, D), f32),
            pltpu.VMEM((16, D), f32),
            pltpu.VMEM((ROWS, PW), bf16),
            pltpu.VMEM((4, 64, 128), f32),
        ],
    )(
        me, w_full, normed, proj, v_rows, states, dy, d_gate, pos, taps, dtb, rate, skip, ones,
        sums,
    )

    def total(received):
        return jnp.sum(received.astype(f32), axis=0).astype(bf16)

    bundle2, received1, branches = lax.optimization_barrier((bundle2, received1, branches))
    received2 = spread(bundle2)
    d_parts = to_core(*n_parts)
    d_parts = to_owner(*d_parts)
    by_member = total(received1).reshape(4, 18, 128)
    turns = [lax.dynamic_index_in_dim(by_member, g ^ d, 0, keepdims=False) for d in range(4)]
    turns = jnp.stack([turns[0]] + [among(turns[d], d) for d in range(1, 4)])
    outs = jnp.stack([lax.dynamic_index_in_dim(turns, g ^ k, 0, keepdims=False) for k in range(4)])
    reduced2, outs = lax.optimization_barrier((total(received2), outs))
    payload = jnp.concatenate(
        [
            reduced2[:192].reshape(4, 48, 128),
            outs,
            reduced2[192:].reshape(4, 4, 128),
            jnp.zeros((4, 2, 128), bf16),
        ],
        axis=1,
    )
    parts = lax.all_to_all(
        jnp.broadcast_to(payload[:, None], (4, reps, 72, 128)).reshape(4 * reps, 72, 128),
        ("group", "rep"), 0, 0, tiled=True,
    )

    x = tok.astype(f32)
    branch = sum(value.astype(f32) for value in branches)
    squares = sum(lax.dynamic_index_in_dim(v, g, 0, keepdims=False) for v in all_stats)
    rms_out = lax.rsqrt(squares[0:4:2].reshape(ROWS, 1) * (1.0 / DI) + epsilon)
    layer_out = (x + rms_out * branch).astype(bf16).reshape(tokens.shape)
    d_normed = sum(value.astype(f32) for value in d_parts)
    rms_in = lax.rsqrt(jnp.mean(x * x, axis=-1, keepdims=True) + epsilon)
    scaled = d_normed * gain_in_all
    grad_tokens = (
        cot.astype(f32)
        + rms_in * scaled
        - x * (rms_in * rms_in * rms_in * jnp.mean(x * scaled, axis=-1, keepdims=True))
    ).reshape(tokens.shape)

    grads = call(
        assemble_kernel,
        "assemble",
        4,
        in_specs=[scalar_spec] + [vmem_spec] * 2,
        out_specs=[vmem_spec] * 9,
        out_shape=(
            shape((192, 3352), f32), shape((XW, D), f32), shape((4, 448), f32),
            shape((1, 448), f32), shape((1, 192), f32), shape((XW,), f32), shape((1, HL), f32),
            shape((1, HL), f32), shape((1, HL), f32),
        ),
        scratch_shapes=[
            pltpu.VMEM((8, CW), f32),
            pltpu.VMEM((128, 256), f32),
            pltpu.VMEM((4, 64, 128), f32),
        ],
    )(me, parts, gain_in.astype(f32).reshape(1, 192))
    grad_w_in, grad_w_out, grad_kernel, grad_bias, grad_gi, grad_go, grad_s, grad_d, grad_l = grads
    return (
        layer_out,
        grad_tokens,
        grad_gi.reshape(-1),
        grad_w_in,
        grad_kernel,
        grad_bias.reshape(-1),
        grad_d.reshape(-1),
        grad_l.reshape(-1),
        grad_s.reshape(-1),
        grad_go,
        grad_w_out,
    )


def solution(mesh):
    sequences = P("rep", "group", None)
    vector = P("group")
    matrix = P("group", None)
    return jax.shard_map(
        local,
        mesh=mesh,
        in_specs=(
            sequences, P("rep", "group"), sequences, vector, matrix, P(None, "group"),
            vector, vector, vector, vector, vector, matrix,
        ),
        out_specs=(
            sequences, sequences, vector, matrix, P(None, "group"), vector, vector, vector,
            vector, vector, matrix,
        ),
        check_vma=False,
    )
```

```python
import jax
import jax.numpy as jnp
import numpy as np
from jax import lax
from jax.experimental import pallas as pl
from jax.experimental.pallas import tpu as pltpu
from jax.sharding import PartitionSpec as P

D = 768
NH = 24
HP = 64
NS = 128
DI = 1536
CW = 1792
SPAN = 128
ROWS = 256
HL = 6
XW = HL * HP
CL = XW + 2 * NS
PW = XW + CL + 128
CUT = 640
epsilon = 1e-05
f32 = jnp.float32
bf16 = jnp.bfloat16
NN = ((1,), (0,))
NT = ((1,), (1,))
TN = ((0,), (0,))
vmem_bytes = 56 * 1024 * 1024


def mm(a, b, dims):
    return lax.dot_general(
        a.astype(bf16), b.astype(bf16), (dims, ((), ())), preferred_element_type=f32
    )


def mm_exact(a, b, dims):
    return lax.dot_general(
        a, b, (dims, ((), ())), preferred_element_type=f32, precision=lax.Precision.HIGHEST
    )


def to_columns(rows):
    short = SPAN - rows.shape[0]
    return jnp.concatenate([rows, jnp.zeros((short, SPAN), f32)], axis=0).T


def softplus(v):
    return jnp.maximum(v, 0.0) + jnp.log1p(jnp.exp(-jnp.abs(v)))


def over_lanes(column):
    return jnp.broadcast_to(column, (SPAN, SPAN))


def span_decays(dt_rows, rate, pos_rows):
    row_at = lax.broadcasted_iota(jnp.int32, (SPAN, SPAN), 0)
    lane_at = lax.broadcasted_iota(jnp.int32, (SPAN, SPAN), 1)
    pos = to_columns(pos_rows)
    step = softplus(dt_rows)
    cum = mm_exact((row_at >= lane_at).astype(f32), step * rate, NN)
    cum_t = cum.T
    step_t = step.T
    allowed = (over_lanes(pos[:, 0:1]) == pos_rows[0:1, :]) & (row_at >= lane_at)
    low = lane_at < HP
    cums = [over_lanes(cum[:, h : h + 1]) for h in range(HL)]
    linked = pos[:, 4:5]
    tail = pos[:, 5:6]
    carried, tails = [], []
    for p in range(HL // 2):
        both = jnp.where(low, cums[2 * p], cums[2 * p + 1])
        steps = jnp.where(
            low, over_lanes(step[:, 2 * p : 2 * p + 1]), over_lanes(step[:, 2 * p + 1 : 2 * p + 2])
        )
        carried.append(jnp.exp(both) * linked)
        tails.append(jnp.exp(both[SPAN - 1 :, :] - both) * tail * steps)

    def decay(h):
        return jnp.where(allowed, jnp.exp(jnp.minimum(cums[h] - cum_t[h : h + 1, :], 0.0)), 0.0)

    return pos, step, step_t, cum, decay, carried, tails, low


def pick(index, sources, target):
    for d, source in enumerate(sources):

        @pl.when(index == d)
        def _(source=source):
            target[...] = source[...]


def put(index, own, pair, across, value):
    low, high = pair.at[0:ROWS, :], pair.at[ROWS : 2 * ROWS, :]
    for d, target in enumerate((own, low, across, high)):

        @pl.when(index == d)
        def _(target=target):
            target[...] = value


def columns_kernel(
    me, w_in, tok, taps, bias, gain_in, seg, w0, w1, w2, w3a, w3b, out, rows, last
):
    g = me[0]
    for d, send in enumerate((w0, w1, w2, last)):
        start = (g ^ d) * XW
        send[:, :XW] = w_in[:, pl.ds(pl.multiple_of(start, 128), XW)]
        send[:, XW : 2 * XW] = w_in[:, pl.ds(pl.multiple_of(DI + start, 128), XW)]
        send[:, 2 * XW : XW + CL] = w_in[:, 2 * DI : DI + CW]
        send[:, XW + CL :] = jnp.concatenate(
            [w_in[:, DI + CW :], jnp.zeros((192, 128 - NH), bf16)], axis=1
        )
    w3a[...] = last[:, :CUT]
    w3b[...] = last[:, CUT:]
    out[0:ROWS, :] = tok[...]
    rows[...] = jnp.zeros_like(rows)
    rows[0:4, 0:448] = taps[...].astype(f32)
    rows[4:5, 0:448] = bias[...].astype(f32).reshape(1, 448)
    rows[5:6, 0:192] = gain_in[...].astype(f32).reshape(1, 192)
    rows[6:7, 0:ROWS] = seg[...].astype(f32)
    out[ROWS : ROWS + 16, :] = rows[...].astype(bf16)


def gather_short(g, parts, taps, gain_in, pos, wide, seg):
    for d, part in enumerate(parts):
        rows = part[ROWS : ROWS + 16, :].astype(f32)
        for k in range(4):

            @pl.when((g ^ d) == k)
            def _(k=k, rows=rows):
                wide[0:5, 448 * k : 448 * k + 448] = rows[0:5, 0:448]
                gain_in[:, 192 * k : 192 * k + 192] = rows[5:6, 0:192]
                seg[2 * k : 2 * k + 1, :] = rows[6:7, 0:128]
                seg[2 * k + 1 : 2 * k + 2, :] = rows[6:7, 128:256]

    taps[...] = jnp.zeros_like(taps)
    taps[0:5, 0:XW] = wide[0:5, pl.ds(pl.multiple_of(g * XW, 128), XW)]
    taps[0:5, XW:] = wide[0:5, DI:]
    ids = seg[...]
    row_at = lax.broadcasted_iota(jnp.int32, (8, 128), 0)
    lane_at = lax.broadcasted_iota(jnp.int32, (8, 128), 1)
    one = jnp.full((1, 128), -1.0, f32)
    earlier = jnp.concatenate([one, ids[0:7]], axis=0)
    later = jnp.concatenate([ids[1:8], one], axis=0)
    ends = jnp.broadcast_to(ids[:, 127:128], (8, 128))
    starts = jnp.broadcast_to(earlier[:, 127:128], (8, 128))
    features = [ids]
    for lag in range(1, 4):
        shifted = jnp.where(
            lane_at >= lag, pltpu.roll(ids, lag, 1), pltpu.roll(earlier, lag, 1)
        )
        features.append((shifted == ids).astype(f32))
    features += [(ids == starts).astype(f32), (ids == ends).astype(f32)]
    for lag in range(1, 4):
        shifted = jnp.where(
            lane_at < 128 - lag, pltpu.roll(ids, 128 - lag, 1), pltpu.roll(later, 128 - lag, 1)
        )
        features.append((shifted == ids).astype(f32))
    pos[...] = jnp.zeros_like(pos)
    for j, feature in enumerate(features):
        for n in range(8):
            pos[n, j : j + 1, :] = feature[n : n + 1, :]


def forward_kernel(
    me, t0, t1, t2, t3, w0, w1, w2, w3a, w3b, dtb, rate, skip,
    w_full, normed, proj, v_out, states, y_out, pos, taps, gain_in,
    tok, state, ext, wide, seg,
):
    i = pl.program_id(0)
    g = me[0]

    @pl.when(i == 0)
    def _():
        row_at = lax.broadcasted_iota(jnp.int32, (128, 128), 0)
        lane_at = lax.broadcasted_iota(jnp.int32, (128, 128), 1)
        chosen = ((row_at == lane_at + g * HL) & (lane_at < HL)).astype(bf16)
        for d, part in enumerate((w0, w1, w2)):
            rows = pl.ds(pl.multiple_of((g ^ d) * 192, 64), 192)
            w_full[rows, : XW + CL] = part[:, : XW + CL]
            w_full[rows, XW + CL :] = mm(part[:, XW + CL :], chosen, NN).astype(bf16)
        rows = pl.ds(pl.multiple_of((g ^ 3) * 192, 64), 192)
        w_full[rows, :CUT] = w3a[...]
        w_full[rows, CUT : XW + CL] = w3b[:, : XW + CL - CUT]
        w_full[rows, XW + CL :] = mm(w3b[:, XW + CL - CUT :], chosen, NN).astype(bf16)
        state[...] = jnp.zeros_like(state)
        ext[0:8, :] = jnp.zeros((8, CL), f32)
        gather_short(g, (t0, t1, t2, t3), taps, gain_in, pos, wide, seg)

    for d, source in enumerate((t0, t1, t2, t3)):

        @pl.when((g ^ i) == d)
        def _(source=source):
            tok[...] = source[0:ROWS, :]

    x = tok[...].astype(f32)
    rms = lax.rsqrt(jnp.mean(x * x, axis=-1, keepdims=True) + epsilon)
    low_rows = (x * rms * gain_in[...]).astype(bf16)
    normed[...] = low_rows
    proj[...] = mm(low_rows, w_full[...], NN).astype(bf16)
    ext[8 : 8 + ROWS, :] = proj[:, XW : XW + CL].astype(f32)
    found = []
    for s in range(ROWS // SPAN):
        at = s * SPAN
        dt_rows = proj[at : at + SPAN, XW + CL :].astype(f32) + dtb[...]
        found.append(span_decays(dt_rows, rate[...], pos[2 * i + s]))
    convs = []
    for s, (cols, *_) in enumerate(found):
        at = s * SPAN
        v = taps[4:5, :] + taps[3:4, :] * ext[8 + at : 8 + at + SPAN, :]
        for lag in range(1, 4):
            window = ext[8 + at - lag : 8 + at - lag + SPAN, :]
            v = v + (taps[3 - lag : 4 - lag, :] * cols[:, lag : lag + 1]) * window
        v_out[at : at + SPAN, :] = v
        convs.append(v * jax.nn.sigmoid(v))
    inners = []
    for conv, (_, _, step_t, _, decay, _, _, low) in zip(convs, found):
        scores = mm(conv[:, XW + NS :], conv[:, XW : XW + NS], NT)
        products = []
        for p in range(HL // 2):
            xp = conv[:, p * SPAN : (p + 1) * SPAN]
            mixing = [
                decay(h) * scores * step_t[h : h + 1, :] for h in (2 * p, 2 * p + 1)
            ]
            products.append(
                mm(
                    jnp.concatenate(mixing, axis=1),
                    jnp.concatenate([jnp.where(low, xp, 0.0), jnp.where(low, 0.0, xp)], axis=0),
                    NN,
                )
                + skip[:, p * SPAN : (p + 1) * SPAN] * xp
            )
        inners.append(jnp.concatenate(products, axis=1))
    for s, (conv, inner, (_, _, _, _, _, carried, tails, _)) in enumerate(
        zip(convs, inners, found)
    ):
        carried_all = jnp.concatenate(carried, axis=1)
        tails_all = jnp.concatenate(tails, axis=1)
        now = state[...]
        states[s] = now
        from_state = mm(conv[:, XW + NS :], now, NN)
        y_out[s * SPAN : (s + 1) * SPAN, :] = inner + carried_all * from_state
        fresh = mm(conv[:, XW : XW + NS], tails_all * conv[:, :XW], TN)
        state[...] = carried_all[SPAN - 1 :, :] * now + fresh
    ext[0:8, :] = ext[ROWS : ROWS + 8, :]


def sums_kernel(me, c0, c1, c2, c3, gate_in, y_in, gain_out, w_out, dno_out, stats, cot):
    i = pl.program_id(0)
    pick(me[0] ^ i, (c0, c1, c2, c3), cot)
    dno = mm(cot[...], w_out[...], NT)
    dno_out[...] = dno
    gate = gate_in[...].astype(f32)
    gated = y_in[...] * (gate * jax.nn.sigmoid(gate))
    squares = jnp.sum(gated * gated, axis=-1, keepdims=True)
    products = jnp.sum(gated * gain_out[...] * dno, axis=-1, keepdims=True)
    lane_at = lax.broadcasted_iota(jnp.int32, (SPAN, SPAN), 1)
    both = jnp.zeros((SPAN, SPAN), f32)
    for s in range(ROWS // SPAN):
        rows = slice(s * SPAN, (s + 1) * SPAN)
        both = jnp.where(lane_at == 2 * s, squares[rows], both)
        both = jnp.where(lane_at == 2 * s + 1, products[rows], both)
    stats[0] = both.T[0:8, :]


def branch_kernel(me, gate_in, y_in, gain_out, w_out, o_own, o_pair, o_across):
    gate = gate_in[...].astype(f32)
    gated = y_in[...] * (gate * jax.nn.sigmoid(gate)) * gain_out[...]
    value = mm(gated, w_out[...], NN).astype(bf16)
    put(me[0] ^ pl.program_id(0), o_own, o_pair, o_across, value)


def out_kernel(
    me, c0, c1, c2, c3, gate_in, y_in, dno_in, s0, s1, s2, s3, gain_out,
    bundle, d_gate, dy_out, sums,
    cot, acc_out, acc_sum, normed_out,
):
    i = pl.program_id(0)
    g = me[0]

    @pl.when(i == 0)
    def _():
        for ref in (acc_out, acc_sum):
            ref[...] = jnp.zeros_like(ref)

    pick(g ^ i, (c0, c1, c2, c3), cot)
    totals = to_columns((s0[0] + s1[0]) + (s2[0] + s3[0]))
    for s in range(ROWS // SPAN):
        rows = slice(s * SPAN, (s + 1) * SPAN)
        rms = lax.rsqrt(totals[:, 2 * s : 2 * s + 1] * (1.0 / DI) + epsilon)
        mean = rms * rms * rms * totals[:, 2 * s + 1 : 2 * s + 2] * (1.0 / DI)
        gate = gate_in[rows, :].astype(f32)
        sig = jax.nn.sigmoid(gate)
        silu = gate * sig
        y = y_in[rows, :]
        gated = y * silu
        scaled = gated * rms
        normed_out[rows, :] = (scaled * gain_out[...]).astype(bf16)
        dno = dno_in[rows, :]
        acc_sum[0:1, :] += jnp.sum(dno * scaled, axis=0, keepdims=True)
        d_gated = rms * gain_out[...] * dno - gated * mean
        dy_out[rows, :] = d_gated * silu
        d_gate[rows, :] = (d_gated * y * (sig * (1.0 + gate * (1.0 - sig)))).astype(bf16)
    acc_out[...] += mm(normed_out[...], cot[...], TN)

    @pl.when(i == pl.num_programs(0) - 1)
    def _():
        sums[...] = acc_sum[...]
        for t in range(6):
            bundle[XW * t : XW * t + XW, :] = acc_out[:, 128 * t : 128 * t + 128].astype(bf16)


def split_sum(rows, ones):
    high = rows.astype(bf16)
    rest = rows - high.astype(f32)
    return mm(high, ones, NN) + mm(rest, ones, NN)


def backward_block(
    w_full, normed, proj, v_in, states, dy_in, d_gate, pos, taps, dtb, rate, skip, ones,
    d_state, ext, acc_in, acc_dt, acc_small, d_proj,
):
    row_at = lax.broadcasted_iota(jnp.int32, (SPAN, SPAN), 0)
    lane_at = lax.broadcasted_iota(jnp.int32, (SPAN, SPAN), 1)
    later = (row_at <= lane_at).astype(f32)

    def add(row, value):
        width = value.shape[1]
        acc_small[row : row + 1, :width] += value

    def down(value):
        return jnp.sum(value, axis=0, keepdims=True)

    d_proj[:, :XW] = d_gate[...]
    found = {}
    for s in reversed(range(ROWS // SPAN)):
        rows = slice(s * SPAN, (s + 1) * SPAN)
        dt_rows = proj[rows, XW + CL :].astype(f32) + dtb[...]
        found[s] = (dt_rows,) + span_decays(dt_rows, rate[...], pos[s])
    inside = {}
    for s in reversed(range(ROWS // SPAN)):
        rows = slice(s * SPAN, (s + 1) * SPAN)
        dy = dy_in[rows, :]
        _, _, _, step_t, _, decay, carried, _, low = found[s]
        v = v_in[rows, :]
        sig_v = jax.nn.sigmoid(v)
        conv = v * sig_v
        x, b_rows, c_rows = conv[:, :XW], conv[:, XW : XW + NS], conv[:, XW + NS :]
        add(1, down(dy * x))
        scores = mm(c_rows, b_rows, NT)
        from_state = mm(c_rows, states[s], NN)
        d_scores = jnp.zeros((SPAN, SPAN), f32)
        row_sums = jnp.zeros((SPAN, SPAN), f32)
        col_sums, inners = [], []
        for p in range(HL // 2):
            lanes = slice(p * SPAN, (p + 1) * SPAN)
            xp, dyp = x[:, lanes], dy[:, lanes]
            halves = jnp.concatenate([jnp.where(low, dyp, 0.0), jnp.where(low, 0.0, dyp)], axis=0)
            d_mixing = mm(halves, xp, NT)
            mixing = []
            for k in range(2):
                h = 2 * p + k
                kept = decay(h)
                kept_step = kept * step_t[h : h + 1, :]
                mixing.append(kept_step * scores)
                d_mix = d_mixing[k * SPAN : (k + 1) * SPAN, :]
                d_scores = d_scores + d_mix * kept_step
                plain = d_mix * kept * scores
                col_sums.append(down(plain))
                row_sum = jnp.sum(plain * step_t[h : h + 1, :], axis=1, keepdims=True)
                row_sums = jnp.where(lane_at == h, row_sum, row_sums)
            inners.append(mm(jnp.concatenate(mixing, axis=0), halves, TN) + skip[:, lanes] * dyp)
        inner = jnp.concatenate(inners, axis=1)
        inside[s] = (v, sig_v, x, b_rows, c_rows, from_state, d_scores, row_sums, col_sums, inner)
    for s in reversed(range(ROWS // SPAN)):
        at = s * SPAN
        rows = slice(at, at + SPAN)
        dy = dy_in[rows, :]
        dt_rows, cols, step, _, cum, _, carried, tails, _ = found[s]
        v, sig_v, x, b_rows, c_rows, from_state, d_scores, row_sums, col_sums, inner = inside[s]
        state = states[s]
        state_grad = d_state[...]
        from_grad = mm(b_rows, state_grad, NN)
        carried_all = jnp.concatenate(carried, axis=1)
        tails_all = jnp.concatenate(tails, axis=1)
        dy_carried = dy * carried_all
        x_tail = x * tails_all
        dx = inner + tails_all * from_grad
        d_c = mm(d_scores, b_rows, NN) + mm(dy_carried, state, NT)
        d_b = mm(d_scores, c_rows, TN) + mm(x_tail, state_grad, NT)

        end_decay = carried_all[SPAN - 1 :, :]
        through = end_decay * down(state * state_grad)
        last = lax.broadcasted_iota(jnp.int32, (SPAN, XW), 0) == SPAN - 1
        from_start = split_sum(
            dy_carried * from_state + jnp.where(last, through, 0.0), ones[...]
        )
        to_end = split_sum(x * from_grad, ones[...])
        end_plain = jnp.exp(cum[SPAN - 1 :, :] - cum) * cols[:, 5:6]
        to_end_kept = to_end * end_plain
        to_end_step = to_end_kept * step
        col_sum = to_columns(jnp.concatenate(col_sums, axis=0))
        d_cum = row_sums - col_sum * step + from_start - to_end_step
        d_cum = d_cum + jnp.where(row_at == SPAN - 1, down(to_end_step), 0.0)
        d_log = mm_exact(later, d_cum, NN)
        d_step = col_sum + to_end_kept + rate[...] * d_log
        d_dt = d_step * jax.nn.sigmoid(dt_rows)
        add(2, down(d_dt))
        add(3, down(d_log * step) * rate[...])
        d_proj[rows, XW + CL :] = d_dt.astype(bf16)
        d_state[...] = end_decay * state_grad + mm(c_rows, dy_carried, TN)

        dv = jnp.concatenate([dx, d_b, d_c], axis=1) * (sig_v * (1.0 + v * (1.0 - sig_v)))
        ext[rows, :] = dv
        add(4, down(dv))
        conv_in = proj[rows, XW : XW + CL].astype(f32)
        add(8, down(dv * conv_in))
        d_conv = taps[3:4, :] * dv
        for lag in range(1, 4):
            window = ext[at + lag : at + lag + SPAN, :] * cols[:, 5 + lag : 6 + lag]
            d_conv = d_conv + taps[3 - lag : 4 - lag, :] * window
            add(8 - lag, down(window * conv_in))
        d_proj[rows, XW : XW + CL] = d_conv.astype(bf16)

    ext[ROWS:, :] = ext[0:8, :]
    d_normed = mm(d_proj[...], w_full[...], NT)
    add(9, down(d_normed * normed[...].astype(f32)))
    acc_in[...] += mm(normed[...], d_proj[:, : XW + CL], TN)
    acc_dt[...] += mm(d_proj[:, XW + CL :], normed[...], TN)[0:8, :]
    return d_normed.astype(bf16)


def backward_kernel(
    me, w_full, normed, proj, v_in, states, dy_in, d_gate, pos, taps, dtb, rate, skip, ones, sums,
    bundle, n_own, n_pair, n_across,
    d_state, ext, acc_in, acc_dt, acc_small, d_proj, small,
):
    i = pl.num_programs(0) - 1 - pl.program_id(0)
    g = me[0]

    @pl.when(pl.program_id(0) == 0)
    def _():
        for ref in (d_state, acc_in, acc_dt, acc_small, small):
            ref[...] = jnp.zeros_like(ref)
        ext[ROWS:, :] = jnp.zeros((8, CL), f32)

    value = backward_block(
        w_full, normed, proj, v_in, states, dy_in, d_gate, pos, taps, dtb, rate, skip, ones,
        d_state, ext, acc_in, acc_dt, acc_small, d_proj,
    )
    put(g ^ i, n_own, n_pair, n_across, value)

    @pl.when(i == 0)
    def _():
        def lay(start, source, row, tiles):
            for k in range(4):
                for t in range(tiles):
                    small[k, start + t : start + t + 1, :] = source[
                        row : row + 1, 128 * t : 128 * t + 128
                    ]

        for j in range(4):
            lay(16 + 5 * j, acc_small, 5 + j, 5)
        lay(36, acc_small, 4, 5)
        lay(43, sums, 0, 3)
        lay(46, acc_small, 1, 3)
        lay(49, acc_small, 2, 1)
        lay(50, acc_small, 3, 1)
        for k in range(4):
            for tile in range(8):
                for q in range(4):
                    bundle[4 * tile + q, 48 * k : 48 * k + 48, :] = acc_in[
                        192 * k + 48 * q : 192 * k + 48 * q + 48, 128 * tile : 128 * tile + 128
                    ].astype(bf16)
            first, second = 192 * k, 192 * k + 128
            for h in range(HL):
                small[k, 2 * h : 2 * h + 1, :] = acc_dt[h : h + 1, first : first + 128]
                small[k, 2 * h + 1 : 2 * h + 2, 0:64] = acc_dt[h : h + 1, second : second + 64]
            small[k, 41:42, :] = acc_small[9:10, first : first + 128]
            small[k, 42:43, 0:64] = acc_small[9:10, second : second + 64]
        for r in range(32):
            if r < 16:
                value = jnp.concatenate([small[k, 4 * r : 4 * r + 4, :] for k in range(4)], axis=0)
            else:
                value = jnp.zeros((16, 128), f32)
            bundle[r, 192:208, :] = value.astype(bf16)


def assemble_kernel(
    me, parts, gain_in,
    grad_in, grad_out, grad_kernel, grad_bias, grad_gain_in, grad_gain_out, grad_skip, grad_dt,
    grad_log,
    wide, turned, shorts,
):
    g = me[0]
    for r in range(32):
        tile, q = r // 4, r % 4
        chunks = [parts[32 * k + r].astype(f32) for k in range(4)]
        rows = slice(48 * q, 48 * q + 48)
        if tile < 6:
            for k in range(4):
                start = (tile // 3) * DI + k * XW + (tile % 3) * 128
                grad_in[rows, start : start + 128] = chunks[k][:48]
        else:
            start = 2 * DI + 128 * (tile - 6)
            grad_in[rows, start : start + 128] = (chunks[0][:48] + chunks[1][:48]) + (
                chunks[2][:48] + chunks[3][:48]
            )
        for k in range(4):
            first = 72 * r + 18 * k
            done = 0
            while done < 18:
                column, row = divmod(first + done, XW)
                count = min(18 - done, XW - row)
                grad_out[row : row + count, 128 * column : 128 * column + 128] = chunks[k][
                    48 + done : 48 + done + count
                ]
                done += count
            if r < 16:
                shorts[k, 4 * r : 4 * r + 4, :] = chunks[k][66:70]

    turned[...] = jnp.zeros_like(turned)
    wide[...] = jnp.zeros_like(wide)
    gain = jnp.zeros((2, 128), f32)
    for k in range(4):
        rest = shorts[k]
        for h in range(HL):
            at = HL * k + h
            turned[at : at + 1, 0:128] = rest[2 * h : 2 * h + 1, :]
            turned[at : at + 1, 128:256] = rest[2 * h + 1 : 2 * h + 2, :]
        for j in range(5):
            for t in range(3):
                lanes = slice(k * XW + 128 * t, k * XW + 128 * t + 128)
                wide[j : j + 1, lanes] = rest[16 + 5 * j + t : 17 + 5 * j + t, :]
            for t in range(3, 5):
                lanes = slice(DI + 128 * (t - 3), DI + 128 * (t - 2))
                wide[j : j + 1, lanes] += rest[16 + 5 * j + t : 17 + 5 * j + t, :]
        gain = gain + rest[41:43, :]
    grad_in[:, DI + CW :] = turned[...].T[0:192, 0:NH]
    grad_gain_in[:, 0:128] = gain[0:1, :] / gain_in[:, 0:128]
    grad_gain_in[:, 128:192] = gain[1:2, 0:64] / gain_in[:, 128:192]
    for k in range(4):

        @pl.when(g == k)
        def _(k=k):
            grad_kernel[...] = wide[0:4, 448 * k : 448 * k + 448]
            grad_bias[...] = wide[4:5, 448 * k : 448 * k + 448]

    own = shorts[g]
    grad_gain_out[...] = jnp.concatenate([own[43 + t : 44 + t, :] for t in range(3)], axis=1).reshape(XW)
    lane_at = lax.broadcasted_iota(jnp.int32, (1, 128), 1)
    skips = jnp.zeros((1, 128), f32)
    for t in range(3):
        row = own[46 + t : 47 + t, :]
        first = jnp.sum(jnp.where(lane_at < HP, row, 0.0), axis=1, keepdims=True)
        second = jnp.sum(jnp.where(lane_at < HP, 0.0, row), axis=1, keepdims=True)
        skips = jnp.where(lane_at == 2 * t, first, skips)
        skips = jnp.where(lane_at == 2 * t + 1, second, skips)
    grad_skip[...] = skips[:, 0:HL]
    grad_dt[...] = own[49:50, 0:HL]
    grad_log[...] = own[50:51, 0:HL]


def whole(shape):
    zeros = (0,) * len(shape)
    return pl.BlockSpec(shape, lambda i: zeros)


def blocked(shape, place):
    zeros = (0,) * (len(shape) - 1)
    return pl.BlockSpec(shape, lambda i: (place(i),) + zeros)


scalar_spec = pl.BlockSpec(memory_space=pltpu.SMEM)
vmem_spec = pl.BlockSpec(memory_space=pltpu.VMEM)


def shape(dims, dtype):
    return jax.ShapeDtypeStruct(dims, dtype)


def call(body, name, micros, **kwargs):
    return pl.pallas_call(
        body,
        name=name,
        compiler_params=pltpu.CompilerParams(vmem_limit_bytes=vmem_bytes),
        cost_estimate=pl.CostEstimate(
            flops=int(micros * 1e9), bytes_accessed=1 << 20, transcendentals=0
        ),
        **kwargs,
    )


def among(value, d):
    return lax.ppermute(value, "group", [(i, i ^ d) for i in range(4)])


def local(
    tokens, segments, cotangent, gain_in, w_in, kernel, conv_bias, dt_bias, a_log, skip_gain,
    gain_out, w_out,
):
    reps = lax.axis_size("rep")
    g = lax.axis_index("group")
    me = g.astype(jnp.int32).reshape(1)
    tok = tokens.reshape(ROWS, D)
    cot = cotangent.reshape(ROWS, D)
    part = whole((ROWS, D))
    blocks = 4

    w0, w1, w2, w3a, w3b, both0 = call(
        columns_kernel,
        "columns",
        2,
        in_specs=[scalar_spec] + [vmem_spec] * 6,
        out_specs=[vmem_spec] * 6,
        out_shape=(shape((192, PW), bf16),) * 3
        + (shape((192, CUT), bf16), shape((192, PW - CUT), bf16), shape((ROWS + 16, D), bf16)),
        scratch_shapes=[pltpu.VMEM((16, D), f32), pltpu.VMEM((192, PW), bf16)],
    )(
        me, w_in, tok, kernel, conv_bias, gain_in,
        segments.reshape(1, ROWS),
    )

    def across(value, d):
        pairs = [(i * reps + r, (i ^ d) * reps + (r ^ 1)) for r in range(reps) for i in range(4)]
        return lax.ppermute(value, ("group", "rep"), pairs)

    w2 = across(w2, 2)
    both2 = among(both0, 2)
    w3b = across(w3b, 3)
    w3a = among(w3a, 3)
    both2, both0, cot_late, w1 = lax.optimization_barrier((both2, both0, cot, w1))
    w1 = among(w1, 1)
    both1 = among(both0, 1)
    both3 = among(both2, 1)
    c2 = among(cot_late, 2)
    c1 = among(cot_late, 1)
    c3 = among(cot_late, 3)
    length = blocks * ROWS
    spans = length // SPAN

    dtb = jnp.pad(dt_bias.astype(f32), (0, 128 - HL)).reshape(1, 128)
    rate = jnp.pad(-jnp.exp(a_log.astype(f32)), (0, 128 - HL)).reshape(1, 128)
    skip = jnp.repeat(skip_gain.astype(f32), HP).reshape(1, XW)
    gain_o = gain_out.astype(f32).reshape(1, XW)

    def up(i):
        return i

    by_owner_specs = [part, whole((2 * ROWS, D)), part]
    by_owner_shapes = tuple(shape((n * ROWS, D), bf16) for n in (1, 2, 1))

    def to_core(own, pair, over):
        got = among(pair, 1)
        other = (over.astype(f32) + got[ROWS:].astype(f32)).astype(bf16)
        return own, got[:ROWS], other

    def to_owner(own, got, other):
        return own, got, among(other, 2)

    w_full, normed, proj, v_rows, states, y_rows, pos, taps, gain_in_all = call(
        forward_kernel,
        "forward",
        15,
        grid=(blocks,),
        in_specs=[scalar_spec]
        + [whole((ROWS + 16, D))] * 4
        + [whole((192, PW))] * 3
        + [whole((192, CUT)), whole((192, PW - CUT))]
        + [whole((1, 128)), whole((1, 128)), whole((1, XW))],
        out_specs=[
            whole((D, PW)),
            blocked((ROWS, D), up),
            blocked((ROWS, PW), up),
            blocked((ROWS, CL), up),
            blocked((2, NS, XW), up),
            blocked((ROWS, XW), up),
            whole((8, 16, SPAN)),
            whole((8, CL)),
            whole((1, D)),
        ],
        out_shape=(
            shape((D, PW), bf16),
            shape((length, D), bf16),
            shape((length, PW), bf16),
            shape((length, CL), f32),
            shape((spans, NS, XW), f32),
            shape((length, XW), f32),
            shape((spans, 16, SPAN), f32),
            shape((8, CL), f32),
            shape((1, D), f32),
        ),
        scratch_shapes=[
            pltpu.VMEM((ROWS, D), bf16),
            pltpu.VMEM((NS, XW), f32),
            pltpu.VMEM((ROWS + 8, CL), f32),
            pltpu.VMEM((8, CW), f32),
            pltpu.VMEM((8, 128), f32),
        ],
    )(
        me, both0, both1, both2, both3, w0, w1, w2, w3a, w3b, dtb, rate, skip,
    )

    gate_spec = pl.BlockSpec((ROWS, XW), lambda i: (i, 0))
    dno, stats = call(
        sums_kernel,
        "sums",
        4,
        grid=(blocks,),
        in_specs=[scalar_spec]
        + [part] * 4
        + [gate_spec, blocked((ROWS, XW), up), whole((1, XW)), whole((XW, D))],
        out_specs=[blocked((ROWS, XW), up), blocked((1, 8, SPAN), up)],
        out_shape=(shape((length, XW), f32), shape((blocks, 8, SPAN), f32)),
        scratch_shapes=[pltpu.VMEM((ROWS, D), bf16)],
    )(me, cot, c1, c2, c3, proj, y_rows, gain_o, w_out)
    all_stats = [stats] + [among(stats, d) for d in range(1, 4)]

    o_parts = call(
        branch_kernel,
        "branch",
        3,
        grid=(blocks,),
        in_specs=[
            scalar_spec, gate_spec, blocked((ROWS, XW), up), whole((1, XW)), whole((XW, D)),
        ],
        out_specs=by_owner_specs,
        out_shape=by_owner_shapes,
    )(me, proj, y_rows, gain_o, w_out)
    o_parts, all_stats = lax.optimization_barrier((o_parts, all_stats))

    bundle1, d_gate, dy, sums = call(
        out_kernel,
        "out",
        6,
        grid=(blocks,),
        in_specs=[scalar_spec]
        + [part] * 4
        + [gate_spec, blocked((ROWS, XW), up), blocked((ROWS, XW), up)]
        + [blocked((1, 8, SPAN), up)] * 4
        + [whole((1, XW))],
        out_specs=[
            whole((2304, 128)), blocked((ROWS, XW), up), blocked((ROWS, XW), up), whole((8, XW)),
        ],
        out_shape=(
            shape((2304, 128), bf16), shape((length, XW), bf16), shape((length, XW), f32),
            shape((8, XW), f32),
        ),
        scratch_shapes=[
            pltpu.VMEM((ROWS, D), bf16),
            pltpu.VMEM((XW, D), f32),
            pltpu.VMEM((8, XW), f32),
            pltpu.VMEM((ROWS, XW), bf16),
        ],
    )(me, cot, c1, c2, c3, proj, y_rows, dno, *all_stats, gain_o)

    def spread(value):
        return lax.all_to_all(value, "rep", 0, 0, tiled=True)

    received1 = spread(bundle1.reshape(reps, 72, 128))
    branches = to_core(*o_parts)
    dy, branches = lax.optimization_barrier((dy, branches))
    branches = to_owner(*branches)
    ones = jnp.asarray(np.arange(XW)[:, None] // HP == np.arange(128)[None, :], bf16)

    def back(i):
        return blocks - 1 - i

    bundle2, *n_parts = call(
        backward_kernel,
        "backward",
        26,
        grid=(blocks,),
        in_specs=[
            scalar_spec,
            whole((D, PW)),
            blocked((ROWS, D), back),
            blocked((ROWS, PW), back),
            blocked((ROWS, CL), back),
            blocked((2, NS, XW), back),
            blocked((ROWS, XW), back),
            blocked((ROWS, XW), back),
            blocked((2, 16, SPAN), back),
            whole((8, CL)), whole((1, 128)), whole((1, 128)), whole((1, XW)), whole((XW, 128)),
            whole((8, XW)),
        ],
        out_specs=[whole((32, 208, 128))] + by_owner_specs,
        out_shape=(shape((32, 208, 128), bf16),) + by_owner_shapes,
        scratch_shapes=[
            pltpu.VMEM((NS, XW), f32),
            pltpu.VMEM((ROWS + 8, CL), f32),
            pltpu.VMEM((D, XW + CL), f32),
            pltpu.VMEM((8, D), f32),
            pltpu.VMEM((16, D), f32),
            pltpu.VMEM((ROWS, PW), bf16),
            pltpu.VMEM((4, 64, 128), f32),
        ],
    )(
        me, w_full, normed, proj, v_rows, states, dy, d_gate, pos, taps, dtb, rate, skip, ones,
        sums,
    )

    def total(received):
        return jnp.sum(received.astype(f32), axis=0).astype(bf16)

    bundle2, received1, branches = lax.optimization_barrier((bundle2, received1, branches))
    received2 = spread(bundle2)
    d_parts = to_core(*n_parts)
    by_member = total(received1).reshape(4, 18, 128)
    turns = [lax.dynamic_index_in_dim(by_member, g ^ d, 0, keepdims=False) for d in range(4)]
    turns = jnp.stack([turns[0]] + [among(turns[d], d) for d in range(1, 4)])
    outs = jnp.stack([lax.dynamic_index_in_dim(turns, g ^ k, 0, keepdims=False) for k in range(4)])
    reduced2, outs, d_parts = lax.optimization_barrier((total(received2), outs, d_parts))
    d_parts = to_owner(*d_parts)
    payload = jnp.concatenate(
        [
            reduced2[:192].reshape(4, 48, 128),
            outs,
            reduced2[192:].reshape(4, 4, 128),
            jnp.zeros((4, 2, 128), bf16),
        ],
        axis=1,
    )
    parts = lax.all_to_all(
        jnp.broadcast_to(payload[:, None], (4, reps, 72, 128)).reshape(4 * reps, 72, 128),
        ("group", "rep"), 0, 0, tiled=True,
    )

    x = tok.astype(f32)
    branch = sum(value.astype(f32) for value in branches)
    squares = sum(lax.dynamic_index_in_dim(v, g, 0, keepdims=False) for v in all_stats)
    rms_out = lax.rsqrt(squares[0:4:2].reshape(ROWS, 1) * (1.0 / DI) + epsilon)
    layer_out = (x + rms_out * branch).astype(bf16).reshape(tokens.shape)
    d_normed = sum(value.astype(f32) for value in d_parts)
    rms_in = lax.rsqrt(jnp.mean(x * x, axis=-1, keepdims=True) + epsilon)
    scaled = d_normed * gain_in_all
    grad_tokens = (
        cot.astype(f32)
        + rms_in * scaled
        - x * (rms_in * rms_in * rms_in * jnp.mean(x * scaled, axis=-1, keepdims=True))
    ).reshape(tokens.shape)

    grads = call(
        assemble_kernel,
        "assemble",
        4,
        in_specs=[scalar_spec] + [vmem_spec] * 2,
        out_specs=[vmem_spec] * 9,
        out_shape=(
            shape((192, 3352), f32), shape((XW, D), f32), shape((4, 448), f32),
            shape((1, 448), f32), shape((1, 192), f32), shape((XW,), f32), shape((1, HL), f32),
            shape((1, HL), f32), shape((1, HL), f32),
        ),
        scratch_shapes=[
            pltpu.VMEM((8, CW), f32),
            pltpu.VMEM((128, 256), f32),
            pltpu.VMEM((4, 64, 128), f32),
        ],
    )(me, parts, gain_in.astype(f32).reshape(1, 192))
    grad_w_in, grad_w_out, grad_kernel, grad_bias, grad_gi, grad_go, grad_s, grad_d, grad_l = grads
    return (
        layer_out,
        grad_tokens,
        grad_gi.reshape(-1),
        grad_w_in,
        grad_kernel,
        grad_bias.reshape(-1),
        grad_d.reshape(-1),
        grad_l.reshape(-1),
        grad_s.reshape(-1),
        grad_go,
        grad_w_out,
    )


def solution(mesh):
    sequences = P("rep", "group", None)
    vector = P("group")
    matrix = P("group", None)
    return jax.shard_map(
        local,
        mesh=mesh,
        in_specs=(
            sequences, P("rep", "group"), sequences, vector, matrix, P(None, "group"),
            vector, vector, vector, vector, vector, matrix,
        ),
        out_specs=(
            sequences, sequences, vector, matrix, P(None, "group"), vector, vector, vector,
            vector, vector, matrix,
        ),
        check_vma=False,
    )
```

```python
import jax
import jax.numpy as jnp
import numpy as np
from jax import lax
from jax.experimental import pallas as pl
from jax.experimental.pallas import tpu as pltpu
from jax.sharding import PartitionSpec as P

D = 768
NH = 24
HP = 64
NS = 128
DI = 1536
CW = 1792
SPAN = 128
ROWS = 256
HL = 6
XW = HL * HP
CL = XW + 2 * NS
PW = XW + CL + 128
CUT = 640
epsilon = 1e-05
f32 = jnp.float32
bf16 = jnp.bfloat16
NN = ((1,), (0,))
NT = ((1,), (1,))
TN = ((0,), (0,))
vmem_bytes = 56 * 1024 * 1024


def mm(a, b, dims):
    return lax.dot_general(
        a.astype(bf16), b.astype(bf16), (dims, ((), ())), preferred_element_type=f32
    )


def mm_exact(a, b, dims):
    return lax.dot_general(
        a, b, (dims, ((), ())), preferred_element_type=f32, precision=lax.Precision.HIGHEST
    )


def to_columns(rows):
    short = SPAN - rows.shape[0]
    return jnp.concatenate([rows, jnp.zeros((short, SPAN), f32)], axis=0).T


def softplus(v):
    return jnp.maximum(v, 0.0) + jnp.log1p(jnp.exp(-jnp.abs(v)))


def over_lanes(column):
    return jnp.broadcast_to(column, (SPAN, SPAN))


def span_decays(dt_rows, rate, pos_rows):
    row_at = lax.broadcasted_iota(jnp.int32, (SPAN, SPAN), 0)
    lane_at = lax.broadcasted_iota(jnp.int32, (SPAN, SPAN), 1)
    pos = to_columns(pos_rows)
    step = softplus(dt_rows)
    cum = mm_exact((row_at >= lane_at).astype(f32), step * rate, NN)
    cum_t = cum.T
    step_t = step.T
    allowed = (over_lanes(pos[:, 0:1]) == pos_rows[0:1, :]) & (row_at >= lane_at)
    low = lane_at < HP
    cums = [over_lanes(cum[:, h : h + 1]) for h in range(HL)]
    linked = pos[:, 4:5]
    tail = pos[:, 5:6]
    carried, tails = [], []
    for p in range(HL // 2):
        both = jnp.where(low, cums[2 * p], cums[2 * p + 1])
        steps = jnp.where(
            low, over_lanes(step[:, 2 * p : 2 * p + 1]), over_lanes(step[:, 2 * p + 1 : 2 * p + 2])
        )
        carried.append(jnp.exp(both) * linked)
        tails.append(jnp.exp(both[SPAN - 1 :, :] - both) * tail * steps)

    def decay(h):
        return jnp.where(allowed, jnp.exp(jnp.minimum(cums[h] - cum_t[h : h + 1, :], 0.0)), 0.0)

    return pos, step, step_t, cum, decay, carried, tails, low


def pick(index, sources, target):
    for d, source in enumerate(sources):

        @pl.when(index == d)
        def _(source=source):
            target[...] = source[...]


def put(index, own, pair, across, value):
    low, high = pair.at[0:ROWS, :], pair.at[ROWS : 2 * ROWS, :]
    for d, target in enumerate((own, low, across, high)):

        @pl.when(index == d)
        def _(target=target):
            target[...] = value


def columns_kernel(
    me, w_in, tok, taps, bias, gain_in, seg, w0, w1, w2, w3a, w3b, out, rows, last
):
    g = me[0]
    for d, send in enumerate((w0, w1, w2, last)):
        start = (g ^ d) * XW
        send[:, :XW] = w_in[:, pl.ds(pl.multiple_of(start, 128), XW)]
        send[:, XW : 2 * XW] = w_in[:, pl.ds(pl.multiple_of(DI + start, 128), XW)]
        send[:, 2 * XW : XW + CL] = w_in[:, 2 * DI : DI + CW]
        send[:, XW + CL :] = jnp.concatenate(
            [w_in[:, DI + CW :], jnp.zeros((192, 128 - NH), bf16)], axis=1
        )
    w3a[...] = last[:, :CUT]
    w3b[...] = last[:, CUT:]
    out[0:ROWS, :] = tok[...]
    rows[...] = jnp.zeros_like(rows)
    rows[0:4, 0:448] = taps[...].astype(f32)
    rows[4:5, 0:448] = bias[...].astype(f32).reshape(1, 448)
    rows[5:6, 0:192] = gain_in[...].astype(f32).reshape(1, 192)
    rows[6:7, 0:ROWS] = seg[...].astype(f32)
    out[ROWS : ROWS + 16, :] = rows[...].astype(bf16)


def gather_short(g, parts, taps, gain_in, pos, wide, seg):
    for d, part in enumerate(parts):
        rows = part[ROWS : ROWS + 16, :].astype(f32)
        for k in range(4):

            @pl.when((g ^ d) == k)
            def _(k=k, rows=rows):
                wide[0:5, 448 * k : 448 * k + 448] = rows[0:5, 0:448]
                gain_in[:, 192 * k : 192 * k + 192] = rows[5:6, 0:192]
                seg[2 * k : 2 * k + 1, :] = rows[6:7, 0:128]
                seg[2 * k + 1 : 2 * k + 2, :] = rows[6:7, 128:256]

    taps[...] = jnp.zeros_like(taps)
    taps[0:5, 0:XW] = wide[0:5, pl.ds(pl.multiple_of(g * XW, 128), XW)]
    taps[0:5, XW:] = wide[0:5, DI:]
    ids = seg[...]
    row_at = lax.broadcasted_iota(jnp.int32, (8, 128), 0)
    lane_at = lax.broadcasted_iota(jnp.int32, (8, 128), 1)
    one = jnp.full((1, 128), -1.0, f32)
    earlier = jnp.concatenate([one, ids[0:7]], axis=0)
    later = jnp.concatenate([ids[1:8], one], axis=0)
    ends = jnp.broadcast_to(ids[:, 127:128], (8, 128))
    starts = jnp.broadcast_to(earlier[:, 127:128], (8, 128))
    features = [ids]
    for lag in range(1, 4):
        shifted = jnp.where(
            lane_at >= lag, pltpu.roll(ids, lag, 1), pltpu.roll(earlier, lag, 1)
        )
        features.append((shifted == ids).astype(f32))
    features += [(ids == starts).astype(f32), (ids == ends).astype(f32)]
    for lag in range(1, 4):
        shifted = jnp.where(
            lane_at < 128 - lag, pltpu.roll(ids, 128 - lag, 1), pltpu.roll(later, 128 - lag, 1)
        )
        features.append((shifted == ids).astype(f32))
    pos[...] = jnp.zeros_like(pos)
    for j, feature in enumerate(features):
        for n in range(8):
            pos[n, j : j + 1, :] = feature[n : n + 1, :]


def forward_kernel(
    me, t0, t1, t2, t3, w0, w1, w2, w3a, w3b, dtb, rate, skip,
    w_full, normed, proj, v_out, states, y_out, pos, taps, gain_in,
    tok, state, ext, wide, seg,
):
    i = pl.program_id(0)
    g = me[0]

    @pl.when(i == 0)
    def _():
        row_at = lax.broadcasted_iota(jnp.int32, (128, 128), 0)
        lane_at = lax.broadcasted_iota(jnp.int32, (128, 128), 1)
        chosen = ((row_at == lane_at + g * HL) & (lane_at < HL)).astype(bf16)
        for d, part in enumerate((w0, w1, w2)):
            rows = pl.ds(pl.multiple_of((g ^ d) * 192, 64), 192)
            w_full[rows, : XW + CL] = part[:, : XW + CL]
            w_full[rows, XW + CL :] = mm(part[:, XW + CL :], chosen, NN).astype(bf16)
        rows = pl.ds(pl.multiple_of((g ^ 3) * 192, 64), 192)
        w_full[rows, :CUT] = w3a[...]
        w_full[rows, CUT : XW + CL] = w3b[:, : XW + CL - CUT]
        w_full[rows, XW + CL :] = mm(w3b[:, XW + CL - CUT :], chosen, NN).astype(bf16)
        state[...] = jnp.zeros_like(state)
        ext[0:8, :] = jnp.zeros((8, CL), f32)
        gather_short(g, (t0, t1, t2, t3), taps, gain_in, pos, wide, seg)

    for d, source in enumerate((t0, t1, t2, t3)):

        @pl.when((g ^ i) == d)
        def _(source=source):
            tok[...] = source[0:ROWS, :]

    x = tok[...].astype(f32)
    rms = lax.rsqrt(jnp.mean(x * x, axis=-1, keepdims=True) + epsilon)
    low_rows = (x * rms * gain_in[...]).astype(bf16)
    normed[...] = low_rows
    proj[...] = mm(low_rows, w_full[...], NN).astype(bf16)
    ext[8 : 8 + ROWS, :] = proj[:, XW : XW + CL].astype(f32)
    found = []
    for s in range(ROWS // SPAN):
        at = s * SPAN
        dt_rows = proj[at : at + SPAN, XW + CL :].astype(f32) + dtb[...]
        found.append(span_decays(dt_rows, rate[...], pos[2 * i + s]))
    convs = []
    for s, (cols, *_) in enumerate(found):
        at = s * SPAN
        v = taps[4:5, :] + taps[3:4, :] * ext[8 + at : 8 + at + SPAN, :]
        for lag in range(1, 4):
            window = ext[8 + at - lag : 8 + at - lag + SPAN, :]
            v = v + (taps[3 - lag : 4 - lag, :] * cols[:, lag : lag + 1]) * window
        v_out[at : at + SPAN, :] = v
        convs.append(v * jax.nn.sigmoid(v))
    inners = []
    for conv, (_, _, step_t, _, decay, _, _, low) in zip(convs, found):
        scores = mm(conv[:, XW + NS :], conv[:, XW : XW + NS], NT)
        products = []
        for p in range(HL // 2):
            xp = conv[:, p * SPAN : (p + 1) * SPAN]
            mixing = [
                decay(h) * scores * step_t[h : h + 1, :] for h in (2 * p, 2 * p + 1)
            ]
            products.append(
                mm(
                    jnp.concatenate(mixing, axis=1),
                    jnp.concatenate([jnp.where(low, xp, 0.0), jnp.where(low, 0.0, xp)], axis=0),
                    NN,
                )
                + skip[:, p * SPAN : (p + 1) * SPAN] * xp
            )
        inners.append(jnp.concatenate(products, axis=1))
    for s, (conv, inner, (_, _, _, _, _, carried, tails, _)) in enumerate(
        zip(convs, inners, found)
    ):
        carried_all = jnp.concatenate(carried, axis=1)
        tails_all = jnp.concatenate(tails, axis=1)
        now = state[...]
        states[s] = now
        from_state = mm(conv[:, XW + NS :], now, NN)
        y_out[s * SPAN : (s + 1) * SPAN, :] = inner + carried_all * from_state
        fresh = mm(conv[:, XW : XW + NS], tails_all * conv[:, :XW], TN)
        state[...] = carried_all[SPAN - 1 :, :] * now + fresh
    ext[0:8, :] = ext[ROWS : ROWS + 8, :]


def sums_kernel(me, c0, c1, c2, c3, gate_in, y_in, gain_out, w_out, dno_out, stats, cot):
    i = pl.program_id(0)
    pick(me[0] ^ i, (c0, c1, c2, c3), cot)
    dno = mm(cot[...], w_out[...], NT)
    dno_out[...] = dno
    gate = gate_in[...].astype(f32)
    gated = y_in[...] * (gate * jax.nn.sigmoid(gate))
    squares = jnp.sum(gated * gated, axis=-1, keepdims=True)
    products = jnp.sum(gated * gain_out[...] * dno, axis=-1, keepdims=True)
    lane_at = lax.broadcasted_iota(jnp.int32, (SPAN, SPAN), 1)
    both = jnp.zeros((SPAN, SPAN), f32)
    for s in range(ROWS // SPAN):
        rows = slice(s * SPAN, (s + 1) * SPAN)
        both = jnp.where(lane_at == 2 * s, squares[rows], both)
        both = jnp.where(lane_at == 2 * s + 1, products[rows], both)
    stats[0] = both.T[0:8, :]


def branch_kernel(me, gate_in, y_in, gain_out, w_out, o_own, o_pair, o_across):
    gate = gate_in[...].astype(f32)
    gated = y_in[...] * (gate * jax.nn.sigmoid(gate)) * gain_out[...]
    value = mm(gated, w_out[...], NN).astype(bf16)
    put(me[0] ^ pl.program_id(0), o_own, o_pair, o_across, value)


def out_kernel(
    me, c0, c1, c2, c3, gate_in, y_in, dno_in, s0, s1, s2, s3, gain_out, normed,
    bundle, left, d_gate, dy_out, sums,
    cot, acc_out, acc_gate, acc_sum, normed_out,
):
    i = pl.program_id(0)
    g = me[0]

    @pl.when(i == 0)
    def _():
        for ref in (acc_out, acc_gate, acc_sum):
            ref[...] = jnp.zeros_like(ref)

    pick(g ^ i, (c0, c1, c2, c3), cot)
    totals = to_columns((s0[0] + s1[0]) + (s2[0] + s3[0]))
    for s in range(ROWS // SPAN):
        rows = slice(s * SPAN, (s + 1) * SPAN)
        rms = lax.rsqrt(totals[:, 2 * s : 2 * s + 1] * (1.0 / DI) + epsilon)
        mean = rms * rms * rms * totals[:, 2 * s + 1 : 2 * s + 2] * (1.0 / DI)
        gate = gate_in[rows, :].astype(f32)
        sig = jax.nn.sigmoid(gate)
        silu = gate * sig
        y = y_in[rows, :]
        gated = y * silu
        scaled = gated * rms
        normed_out[rows, :] = (scaled * gain_out[...]).astype(bf16)
        dno = dno_in[rows, :]
        acc_sum[0:1, :] += jnp.sum(dno * scaled, axis=0, keepdims=True)
        d_gated = rms * gain_out[...] * dno - gated * mean
        dy_out[rows, :] = d_gated * silu
        d_gate[rows, :] = (d_gated * y * (sig * (1.0 + gate * (1.0 - sig)))).astype(bf16)
    acc_out[...] += mm(normed_out[...], cot[...], TN)
    acc_gate[...] += mm(normed[...], d_gate[...], TN)

    @pl.when(i == pl.num_programs(0) - 1)
    def _():
        sums[...] = acc_sum[...]
        for k in range(4):
            for piece in range(36):
                tile, row = piece // 12, 192 * k + 16 * (piece % 12)
                value = acc_gate[row : row + 16, 128 * tile : 128 * tile + 128].astype(bf16)
                if piece < 32:
                    bundle[piece, 16 * k : 16 * k + 16, :] = value
                else:
                    left[4 * k + piece - 32] = value
        for piece in range(160):
            at = 64 + 16 * (piece % 5)
            tile, row = piece // 24, 16 * (piece % 24)
            if piece < 144:
                value = acc_out[row : row + 16, 128 * tile : 128 * tile + 128].astype(bf16)
            else:
                value = jnp.zeros((16, 128), bf16)
            bundle[piece // 5, at : at + 16, :] = value


def split_sum(rows, ones):
    high = rows.astype(bf16)
    rest = rows - high.astype(f32)
    return mm(high, ones, NN) + mm(rest, ones, NN)


def backward_block(
    w_full, normed, proj, v_in, states, dy_in, d_gate, pos, taps, dtb, rate, skip, ones,
    d_state, ext, acc_in, acc_dt, acc_small, d_proj,
):
    row_at = lax.broadcasted_iota(jnp.int32, (SPAN, SPAN), 0)
    lane_at = lax.broadcasted_iota(jnp.int32, (SPAN, SPAN), 1)
    later = (row_at <= lane_at).astype(f32)

    def add(row, value):
        width = value.shape[1]
        acc_small[row : row + 1, :width] += value

    def down(value):
        return jnp.sum(value, axis=0, keepdims=True)

    d_proj[:, :XW] = d_gate[...]
    found = {}
    for s in reversed(range(ROWS // SPAN)):
        rows = slice(s * SPAN, (s + 1) * SPAN)
        dt_rows = proj[rows, XW + CL :].astype(f32) + dtb[...]
        found[s] = (dt_rows,) + span_decays(dt_rows, rate[...], pos[s])
    inside = {}
    for s in reversed(range(ROWS // SPAN)):
        rows = slice(s * SPAN, (s + 1) * SPAN)
        dy = dy_in[rows, :]
        _, _, _, step_t, _, decay, carried, _, low = found[s]
        v = v_in[rows, :]
        sig_v = jax.nn.sigmoid(v)
        conv = v * sig_v
        x, b_rows, c_rows = conv[:, :XW], conv[:, XW : XW + NS], conv[:, XW + NS :]
        add(1, down(dy * x))
        scores = mm(c_rows, b_rows, NT)
        from_state = mm(c_rows, states[s], NN)
        d_scores = jnp.zeros((SPAN, SPAN), f32)
        row_sums = jnp.zeros((SPAN, SPAN), f32)
        col_sums, inners = [], []
        for p in range(HL // 2):
            lanes = slice(p * SPAN, (p + 1) * SPAN)
            xp, dyp = x[:, lanes], dy[:, lanes]
            halves = jnp.concatenate([jnp.where(low, dyp, 0.0), jnp.where(low, 0.0, dyp)], axis=0)
            d_mixing = mm(halves, xp, NT)
            mixing = []
            for k in range(2):
                h = 2 * p + k
                kept = decay(h)
                kept_step = kept * step_t[h : h + 1, :]
                mixing.append(kept_step * scores)
                d_mix = d_mixing[k * SPAN : (k + 1) * SPAN, :]
                d_scores = d_scores + d_mix * kept_step
                plain = d_mix * kept * scores
                col_sums.append(down(plain))
                row_sum = jnp.sum(plain * step_t[h : h + 1, :], axis=1, keepdims=True)
                row_sums = jnp.where(lane_at == h, row_sum, row_sums)
            inners.append(mm(jnp.concatenate(mixing, axis=0), halves, TN) + skip[:, lanes] * dyp)
        inner = jnp.concatenate(inners, axis=1)
        inside[s] = (v, sig_v, x, b_rows, c_rows, from_state, d_scores, row_sums, col_sums, inner)
    for s in reversed(range(ROWS // SPAN)):
        at = s * SPAN
        rows = slice(at, at + SPAN)
        dy = dy_in[rows, :]
        dt_rows, cols, step, _, cum, _, carried, tails, _ = found[s]
        v, sig_v, x, b_rows, c_rows, from_state, d_scores, row_sums, col_sums, inner = inside[s]
        state = states[s]
        state_grad = d_state[...]
        from_grad = mm(b_rows, state_grad, NN)
        carried_all = jnp.concatenate(carried, axis=1)
        tails_all = jnp.concatenate(tails, axis=1)
        dy_carried = dy * carried_all
        x_tail = x * tails_all
        dx = inner + tails_all * from_grad
        d_c = mm(d_scores, b_rows, NN) + mm(dy_carried, state, NT)
        d_b = mm(d_scores, c_rows, TN) + mm(x_tail, state_grad, NT)

        end_decay = carried_all[SPAN - 1 :, :]
        through = end_decay * down(state * state_grad)
        last = lax.broadcasted_iota(jnp.int32, (SPAN, XW), 0) == SPAN - 1
        from_start = split_sum(
            dy_carried * from_state + jnp.where(last, through, 0.0), ones[...]
        )
        to_end = split_sum(x * from_grad, ones[...])
        end_plain = jnp.exp(cum[SPAN - 1 :, :] - cum) * cols[:, 5:6]
        to_end_kept = to_end * end_plain
        to_end_step = to_end_kept * step
        col_sum = to_columns(jnp.concatenate(col_sums, axis=0))
        d_cum = row_sums - col_sum * step + from_start - to_end_step
        d_cum = d_cum + jnp.where(row_at == SPAN - 1, down(to_end_step), 0.0)
        d_log = mm_exact(later, d_cum, NN)
        d_step = col_sum + to_end_kept + rate[...] * d_log
        d_dt = d_step * jax.nn.sigmoid(dt_rows)
        add(2, down(d_dt))
        add(3, down(d_log * step) * rate[...])
        d_proj[rows, XW + CL :] = d_dt.astype(bf16)
        d_state[...] = end_decay * state_grad + mm(c_rows, dy_carried, TN)

        dv = jnp.concatenate([dx, d_b, d_c], axis=1) * (sig_v * (1.0 + v * (1.0 - sig_v)))
        ext[rows, :] = dv
        add(4, down(dv))
        conv_in = proj[rows, XW : XW + CL].astype(f32)
        add(8, down(dv * conv_in))
        d_conv = taps[3:4, :] * dv
        for lag in range(1, 4):
            window = ext[at + lag : at + lag + SPAN, :] * cols[:, 5 + lag : 6 + lag]
            d_conv = d_conv + taps[3 - lag : 4 - lag, :] * window
            add(8 - lag, down(window * conv_in))
        d_proj[rows, XW : XW + CL] = d_conv.astype(bf16)

    ext[ROWS:, :] = ext[0:8, :]
    d_normed = mm(d_proj[...], w_full[...], NT)
    add(9, down(d_normed * normed[...].astype(f32)))
    acc_in[...] += mm(normed[...], d_proj[:, XW : XW + CL], TN)
    acc_dt[...] += mm(d_proj[:, XW + CL :], normed[...], TN)[0:8, :]
    return d_normed.astype(bf16)


def backward_kernel(
    me, w_full, normed, proj, v_in, states, dy_in, d_gate, pos, taps, dtb, rate, skip, ones, sums, left,
    bundle, n_own, n_pair, n_across,
    d_state, ext, acc_in, acc_dt, acc_small, d_proj, small,
):
    i = pl.num_programs(0) - 1 - pl.program_id(0)
    g = me[0]

    @pl.when(pl.program_id(0) == 0)
    def _():
        for ref in (d_state, acc_in, acc_dt, acc_small, small):
            ref[...] = jnp.zeros_like(ref)
        ext[ROWS:, :] = jnp.zeros((8, CL), f32)

    value = backward_block(
        w_full, normed, proj, v_in, states, dy_in, d_gate, pos, taps, dtb, rate, skip, ones,
        d_state, ext, acc_in, acc_dt, acc_small, d_proj,
    )
    put(g ^ i, n_own, n_pair, n_across, value)

    @pl.when(i == 0)
    def _():
        def lay(start, source, row, tiles):
            for k in range(4):
                for t in range(tiles):
                    small[k, start + t : start + t + 1, :] = source[
                        row : row + 1, 128 * t : 128 * t + 128
                    ]

        for j in range(4):
            lay(16 + 5 * j, acc_small, 5 + j, 5)
        lay(36, acc_small, 4, 5)
        lay(43, sums, 0, 3)
        lay(46, acc_small, 1, 3)
        lay(49, acc_small, 2, 1)
        lay(50, acc_small, 3, 1)
        for k in range(4):
            for piece in range(64):
                at = 32 * k + 16 * (piece % 2)
                tile, row = piece // 12, 192 * k + 16 * (piece % 12)
                if piece < 60:
                    value = acc_in[row : row + 16, 128 * tile : 128 * tile + 128].astype(bf16)
                else:
                    value = left[4 * k + piece - 60]
                bundle[piece // 2, at : at + 16, :] = value
            first, second = 192 * k, 192 * k + 128
            for h in range(HL):
                small[k, 2 * h : 2 * h + 1, :] = acc_dt[h : h + 1, first : first + 128]
                small[k, 2 * h + 1 : 2 * h + 2, 0:64] = acc_dt[h : h + 1, second : second + 64]
            small[k, 41:42, :] = acc_small[9:10, first : first + 128]
            small[k, 42:43, 0:64] = acc_small[9:10, second : second + 64]
        for r in range(32):
            if r < 16:
                value = jnp.concatenate([small[k, 4 * r : 4 * r + 4, :] for k in range(4)], axis=0)
            else:
                value = jnp.zeros((16, 128), f32)
            bundle[r, 128:144, :] = value.astype(bf16)


def assemble_kernel(
    me, parts, gain_in,
    grad_in, grad_out, grad_kernel, grad_bias, grad_gain_in, grad_gain_out, grad_skip, grad_dt,
    grad_log,
    wide, turned, shorts,
):
    g = me[0]
    for r in range(32):
        chunks = [parts[32 * k + r].astype(f32) for k in range(4)]
        pieces = [(0, r)]
        for n in (2 * r, 2 * r + 1):
            pieces.append((16 + 16 * (n % 2), 36 + n if n < 60 else n - 28))
        for at, piece in pieces:
            tile, row = piece // 12, 16 * (piece % 12)
            values = [chunk[at : at + 16] for chunk in chunks]
            if tile < 6:
                for k in range(4):
                    start = (tile // 3) * DI + k * XW + (tile % 3) * 128
                    grad_in[row : row + 16, start : start + 128] = values[k]
            else:
                start = 2 * DI + 128 * (tile - 6)
                grad_in[row : row + 16, start : start + 128] = (values[0] + values[1]) + (
                    values[2] + values[3]
                )
        for k in range(4):
            done = 0
            while done < 20:
                piece, inside = divmod(20 * k + done, 16)
                piece += 5 * r
                count = min(20 - done, 16 - inside)
                if piece < 144:
                    row, column = 16 * (piece % 24) + inside, 128 * (piece // 24)
                    grad_out[row : row + count, column : column + 128] = chunks[k][
                        48 + done : 48 + done + count
                    ]
                done += count
            if r < 16:
                shorts[k, 4 * r : 4 * r + 4, :] = chunks[k][68:72]

    turned[...] = jnp.zeros_like(turned)
    wide[...] = jnp.zeros_like(wide)
    gain = jnp.zeros((2, 128), f32)
    for k in range(4):
        rest = shorts[k]
        for h in range(HL):
            at = HL * k + h
            turned[at : at + 1, 0:128] = rest[2 * h : 2 * h + 1, :]
            turned[at : at + 1, 128:256] = rest[2 * h + 1 : 2 * h + 2, :]
        for j in range(5):
            for t in range(3):
                lanes = slice(k * XW + 128 * t, k * XW + 128 * t + 128)
                wide[j : j + 1, lanes] = rest[16 + 5 * j + t : 17 + 5 * j + t, :]
            for t in range(3, 5):
                lanes = slice(DI + 128 * (t - 3), DI + 128 * (t - 2))
                wide[j : j + 1, lanes] += rest[16 + 5 * j + t : 17 + 5 * j + t, :]
        gain = gain + rest[41:43, :]
    grad_in[:, DI + CW :] = turned[...].T[0:192, 0:NH]
    grad_gain_in[:, 0:128] = gain[0:1, :] / gain_in[:, 0:128]
    grad_gain_in[:, 128:192] = gain[1:2, 0:64] / gain_in[:, 128:192]
    for k in range(4):

        @pl.when(g == k)
        def _(k=k):
            grad_kernel[...] = wide[0:4, 448 * k : 448 * k + 448]
            grad_bias[...] = wide[4:5, 448 * k : 448 * k + 448]

    own = shorts[g]
    grad_gain_out[...] = jnp.concatenate([own[43 + t : 44 + t, :] for t in range(3)], axis=1).reshape(XW)
    lane_at = lax.broadcasted_iota(jnp.int32, (1, 128), 1)
    skips = jnp.zeros((1, 128), f32)
    for t in range(3):
        row = own[46 + t : 47 + t, :]
        first = jnp.sum(jnp.where(lane_at < HP, row, 0.0), axis=1, keepdims=True)
        second = jnp.sum(jnp.where(lane_at < HP, 0.0, row), axis=1, keepdims=True)
        skips = jnp.where(lane_at == 2 * t, first, skips)
        skips = jnp.where(lane_at == 2 * t + 1, second, skips)
    grad_skip[...] = skips[:, 0:HL]
    grad_dt[...] = own[49:50, 0:HL]
    grad_log[...] = own[50:51, 0:HL]


def whole(shape):
    zeros = (0,) * len(shape)
    return pl.BlockSpec(shape, lambda i: zeros)


def blocked(shape, place):
    zeros = (0,) * (len(shape) - 1)
    return pl.BlockSpec(shape, lambda i: (place(i),) + zeros)


scalar_spec = pl.BlockSpec(memory_space=pltpu.SMEM)
vmem_spec = pl.BlockSpec(memory_space=pltpu.VMEM)


def shape(dims, dtype):
    return jax.ShapeDtypeStruct(dims, dtype)


def call(body, name, micros, **kwargs):
    return pl.pallas_call(
        body,
        name=name,
        compiler_params=pltpu.CompilerParams(vmem_limit_bytes=vmem_bytes),
        cost_estimate=pl.CostEstimate(
            flops=int(micros * 1e9), bytes_accessed=1 << 20, transcendentals=0
        ),
        **kwargs,
    )


def among(value, d):
    return lax.ppermute(value, "group", [(i, i ^ d) for i in range(4)])


def local(
    tokens, segments, cotangent, gain_in, w_in, kernel, conv_bias, dt_bias, a_log, skip_gain,
    gain_out, w_out,
):
    reps = lax.axis_size("rep")
    g = lax.axis_index("group")
    me = g.astype(jnp.int32).reshape(1)
    tok = tokens.reshape(ROWS, D)
    cot = cotangent.reshape(ROWS, D)
    part = whole((ROWS, D))
    blocks = 4

    w0, w1, w2, w3a, w3b, both0 = call(
        columns_kernel,
        "columns",
        2,
        in_specs=[scalar_spec] + [vmem_spec] * 6,
        out_specs=[vmem_spec] * 6,
        out_shape=(shape((192, PW), bf16),) * 3
        + (shape((192, CUT), bf16), shape((192, PW - CUT), bf16), shape((ROWS + 16, D), bf16)),
        scratch_shapes=[pltpu.VMEM((16, D), f32), pltpu.VMEM((192, PW), bf16)],
    )(
        me, w_in, tok, kernel, conv_bias, gain_in,
        segments.reshape(1, ROWS),
    )

    def across(value, d):
        pairs = [(i * reps + r, (i ^ d) * reps + (r ^ 1)) for r in range(reps) for i in range(4)]
        return lax.ppermute(value, ("group", "rep"), pairs)

    w2 = across(w2, 2)
    both2 = among(both0, 2)
    w3b = across(w3b, 3)
    w3a = among(w3a, 3)
    both2, both0, cot_late, w1 = lax.optimization_barrier((both2, both0, cot, w1))
    w1 = among(w1, 1)
    both1 = among(both0, 1)
    both3 = among(both2, 1)
    c2 = among(cot_late, 2)
    c1 = among(cot_late, 1)
    c3 = among(cot_late, 3)
    length = blocks * ROWS
    spans = length // SPAN

    dtb = jnp.pad(dt_bias.astype(f32), (0, 128 - HL)).reshape(1, 128)
    rate = jnp.pad(-jnp.exp(a_log.astype(f32)), (0, 128 - HL)).reshape(1, 128)
    skip = jnp.repeat(skip_gain.astype(f32), HP).reshape(1, XW)
    gain_o = gain_out.astype(f32).reshape(1, XW)

    def up(i):
        return i

    by_owner_specs = [part, whole((2 * ROWS, D)), part]
    by_owner_shapes = tuple(shape((n * ROWS, D), bf16) for n in (1, 2, 1))

    def to_core(own, pair, over):
        got = among(pair, 1)
        other = (over.astype(f32) + got[ROWS:].astype(f32)).astype(bf16)
        return own, got[:ROWS], other

    def to_owner(own, got, other):
        return own, got, among(other, 2)

    w_full, normed, proj, v_rows, states, y_rows, pos, taps, gain_in_all = call(
        forward_kernel,
        "forward",
        15,
        grid=(blocks,),
        in_specs=[scalar_spec]
        + [whole((ROWS + 16, D))] * 4
        + [whole((192, PW))] * 3
        + [whole((192, CUT)), whole((192, PW - CUT))]
        + [whole((1, 128)), whole((1, 128)), whole((1, XW))],
        out_specs=[
            whole((D, PW)),
            blocked((ROWS, D), up),
            blocked((ROWS, PW), up),
            blocked((ROWS, CL), up),
            blocked((2, NS, XW), up),
            blocked((ROWS, XW), up),
            whole((8, 16, SPAN)),
            whole((8, CL)),
            whole((1, D)),
        ],
        out_shape=(
            shape((D, PW), bf16),
            shape((length, D), bf16),
            shape((length, PW), bf16),
            shape((length, CL), f32),
            shape((spans, NS, XW), f32),
            shape((length, XW), f32),
            shape((spans, 16, SPAN), f32),
            shape((8, CL), f32),
            shape((1, D), f32),
        ),
        scratch_shapes=[
            pltpu.VMEM((ROWS, D), bf16),
            pltpu.VMEM((NS, XW), f32),
            pltpu.VMEM((ROWS + 8, CL), f32),
            pltpu.VMEM((8, CW), f32),
            pltpu.VMEM((8, 128), f32),
        ],
    )(
        me, both0, both1, both2, both3, w0, w1, w2, w3a, w3b, dtb, rate, skip,
    )

    gate_spec = pl.BlockSpec((ROWS, XW), lambda i: (i, 0))
    dno, stats = call(
        sums_kernel,
        "sums",
        4,
        grid=(blocks,),
        in_specs=[scalar_spec]
        + [part] * 4
        + [gate_spec, blocked((ROWS, XW), up), whole((1, XW)), whole((XW, D))],
        out_specs=[blocked((ROWS, XW), up), blocked((1, 8, SPAN), up)],
        out_shape=(shape((length, XW), f32), shape((blocks, 8, SPAN), f32)),
        scratch_shapes=[pltpu.VMEM((ROWS, D), bf16)],
    )(me, cot, c1, c2, c3, proj, y_rows, gain_o, w_out)
    all_stats = [stats] + [among(stats, d) for d in range(1, 4)]

    o_parts = call(
        branch_kernel,
        "branch",
        3,
        grid=(blocks,),
        in_specs=[
            scalar_spec, gate_spec, blocked((ROWS, XW), up), whole((1, XW)), whole((XW, D)),
        ],
        out_specs=by_owner_specs,
        out_shape=by_owner_shapes,
    )(me, proj, y_rows, gain_o, w_out)
    o_parts, all_stats = lax.optimization_barrier((o_parts, all_stats))

    bundle1, left, d_gate, dy, sums = call(
        out_kernel,
        "out",
        6,
        grid=(blocks,),
        in_specs=[scalar_spec]
        + [part] * 4
        + [gate_spec, blocked((ROWS, XW), up), blocked((ROWS, XW), up)]
        + [blocked((1, 8, SPAN), up)] * 4
        + [whole((1, XW)), blocked((ROWS, D), up)],
        out_specs=[
            whole((32, 144, 128)), whole((16, 16, 128)), blocked((ROWS, XW), up), blocked((ROWS, XW), up), whole((8, XW)),
        ],
        out_shape=(
            shape((32, 144, 128), bf16), shape((16, 16, 128), bf16),
            shape((length, XW), bf16), shape((length, XW), f32),
            shape((8, XW), f32),
        ),
        scratch_shapes=[
            pltpu.VMEM((ROWS, D), bf16),
            pltpu.VMEM((XW, D), f32),
            pltpu.VMEM((D, XW), f32),
            pltpu.VMEM((8, XW), f32),
            pltpu.VMEM((ROWS, XW), bf16),
        ],
    )(me, cot, c1, c2, c3, proj, y_rows, dno, *all_stats, gain_o, normed)

    def spread(value):
        return lax.all_to_all(value, "rep", 0, 0, tiled=True)

    received1 = spread(bundle1)
    branches = to_core(*o_parts)
    dy, branches = lax.optimization_barrier((dy, branches))
    branches = to_owner(*branches)
    ones = jnp.asarray(np.arange(XW)[:, None] // HP == np.arange(128)[None, :], bf16)

    def back(i):
        return blocks - 1 - i

    bundle2, *n_parts = call(
        backward_kernel,
        "backward",
        26,
        grid=(blocks,),
        in_specs=[
            scalar_spec,
            whole((D, PW)),
            blocked((ROWS, D), back),
            blocked((ROWS, PW), back),
            blocked((ROWS, CL), back),
            blocked((2, NS, XW), back),
            blocked((ROWS, XW), back),
            blocked((ROWS, XW), back),
            blocked((2, 16, SPAN), back),
            whole((8, CL)), whole((1, 128)), whole((1, 128)), whole((1, XW)), whole((XW, 128)),
            whole((8, XW)),
            whole((16, 16, 128)),
        ],
        out_specs=[whole((32, 144, 128))] + by_owner_specs,
        out_shape=(shape((32, 144, 128), bf16),) + by_owner_shapes,
        scratch_shapes=[
            pltpu.VMEM((NS, XW), f32),
            pltpu.VMEM((ROWS + 8, CL), f32),
            pltpu.VMEM((D, CL), f32),
            pltpu.VMEM((8, D), f32),
            pltpu.VMEM((16, D), f32),
            pltpu.VMEM((ROWS, PW), bf16),
            pltpu.VMEM((4, 64, 128), f32),
        ],
    )(
        me, w_full, normed, proj, v_rows, states, dy, d_gate, pos, taps, dtb, rate, skip, ones,
        sums, left,
    )

    def total(received):
        return jnp.sum(received.astype(f32), axis=0).astype(bf16)

    bundle2, received1, branches = lax.optimization_barrier((bundle2, received1, branches))
    received2 = spread(bundle2)
    d_parts = to_core(*n_parts)
    reduced1 = total(received1)
    by_member = reduced1[64:].reshape(4, 20, 128)
    turns = [lax.dynamic_index_in_dim(by_member, g ^ d, 0, keepdims=False) for d in range(4)]
    turns = jnp.stack([turns[0]] + [among(turns[d], d) for d in range(1, 4)])
    outs = jnp.stack([lax.dynamic_index_in_dim(turns, g ^ k, 0, keepdims=False) for k in range(4)])
    first = reduced1[:64].reshape(4, 16, 128)
    reduced2, outs, first, d_parts = lax.optimization_barrier(
        (total(received2), outs, first, d_parts)
    )
    d_parts = to_owner(*d_parts)
    payload = jnp.concatenate(
        [
            first,
            reduced2[:128].reshape(4, 32, 128),
            outs,
            reduced2[128:].reshape(4, 4, 128),
        ],
        axis=1,
    )
    parts = lax.all_to_all(
        jnp.broadcast_to(payload[:, None], (4, reps, 72, 128)).reshape(4 * reps, 72, 128),
        ("group", "rep"), 0, 0, tiled=True,
    )

    x = tok.astype(f32)
    branch = sum(value.astype(f32) for value in branches)
    squares = sum(lax.dynamic_index_in_dim(v, g, 0, keepdims=False) for v in all_stats)
    rms_out = lax.rsqrt(squares[0:4:2].reshape(ROWS, 1) * (1.0 / DI) + epsilon)
    layer_out = (x + rms_out * branch).astype(bf16).reshape(tokens.shape)
    d_normed = sum(value.astype(f32) for value in d_parts)
    rms_in = lax.rsqrt(jnp.mean(x * x, axis=-1, keepdims=True) + epsilon)
    scaled = d_normed * gain_in_all
    grad_tokens = (
        cot.astype(f32)
        + rms_in * scaled
        - x * (rms_in * rms_in * rms_in * jnp.mean(x * scaled, axis=-1, keepdims=True))
    ).reshape(tokens.shape)

    grads = call(
        assemble_kernel,
        "assemble",
        4,
        in_specs=[scalar_spec] + [vmem_spec] * 2,
        out_specs=[vmem_spec] * 9,
        out_shape=(
            shape((192, 3352), f32), shape((XW, D), f32), shape((4, 448), f32),
            shape((1, 448), f32), shape((1, 192), f32), shape((XW,), f32), shape((1, HL), f32),
            shape((1, HL), f32), shape((1, HL), f32),
        ),
        scratch_shapes=[
            pltpu.VMEM((8, CW), f32),
            pltpu.VMEM((128, 256), f32),
            pltpu.VMEM((4, 64, 128), f32),
        ],
    )(me, parts, gain_in.astype(f32).reshape(1, 192))
    grad_w_in, grad_w_out, grad_kernel, grad_bias, grad_gi, grad_go, grad_s, grad_d, grad_l = grads
    return (
        layer_out,
        grad_tokens,
        grad_gi.reshape(-1),
        grad_w_in,
        grad_kernel,
        grad_bias.reshape(-1),
        grad_d.reshape(-1),
        grad_l.reshape(-1),
        grad_s.reshape(-1),
        grad_go,
        grad_w_out,
    )


def solution(mesh):
    sequences = P("rep", "group", None)
    vector = P("group")
    matrix = P("group", None)
    return jax.shard_map(
        local,
        mesh=mesh,
        in_specs=(
            sequences, P("rep", "group"), sequences, vector, matrix, P(None, "group"),
            vector, vector, vector, vector, vector, matrix,
        ),
        out_specs=(
            sequences, sequences, vector, matrix, P(None, "group"), vector, vector, vector,
            vector, vector, matrix,
        ),
        check_vma=False,
    )
```

```python
import jax
import jax.numpy as jnp
import numpy as np
from jax import lax
from jax.experimental import pallas as pl
from jax.experimental.pallas import tpu as pltpu
from jax.sharding import PartitionSpec as P

D = 768
NH = 24
HP = 64
NS = 128
DI = 1536
CW = 1792
SPAN = 128
ROWS = 256
HL = 6
XW = HL * HP
CL = XW + 2 * NS
PW = XW + CL + 128
CUT = 640
epsilon = 1e-05
f32 = jnp.float32
bf16 = jnp.bfloat16
NN = ((1,), (0,))
NT = ((1,), (1,))
TN = ((0,), (0,))
vmem_bytes = 56 * 1024 * 1024


def mm(a, b, dims):
    return lax.dot_general(
        a.astype(bf16), b.astype(bf16), (dims, ((), ())), preferred_element_type=f32
    )


def mm_exact(a, b, dims):
    return lax.dot_general(
        a, b, (dims, ((), ())), preferred_element_type=f32, precision=lax.Precision.HIGHEST
    )


def to_columns(rows):
    short = SPAN - rows.shape[0]
    return jnp.concatenate([rows, jnp.zeros((short, SPAN), f32)], axis=0).T


def softplus(v):
    return jnp.maximum(v, 0.0) + jnp.log1p(jnp.exp(-jnp.abs(v)))


def over_lanes(column):
    return jnp.broadcast_to(column, (SPAN, SPAN))


def span_decays(dt_rows, rate, pos_rows):
    row_at = lax.broadcasted_iota(jnp.int32, (SPAN, SPAN), 0)
    lane_at = lax.broadcasted_iota(jnp.int32, (SPAN, SPAN), 1)
    pos = to_columns(pos_rows)
    step = softplus(dt_rows)
    cum = mm_exact((row_at >= lane_at).astype(f32), step * rate, NN)
    cum_t = cum.T
    step_t = step.T
    allowed = (over_lanes(pos[:, 0:1]) == pos_rows[0:1, :]) & (row_at >= lane_at)
    low = lane_at < HP
    cums = [over_lanes(cum[:, h : h + 1]) for h in range(HL)]
    linked = pos[:, 4:5]
    tail = pos[:, 5:6]
    carried, tails = [], []
    for p in range(HL // 2):
        both = jnp.where(low, cums[2 * p], cums[2 * p + 1])
        steps = jnp.where(
            low, over_lanes(step[:, 2 * p : 2 * p + 1]), over_lanes(step[:, 2 * p + 1 : 2 * p + 2])
        )
        carried.append(jnp.exp(both) * linked)
        tails.append(jnp.exp(both[SPAN - 1 :, :] - both) * tail * steps)

    def decay(h):
        return jnp.where(allowed, jnp.exp(jnp.minimum(cums[h] - cum_t[h : h + 1, :], 0.0)), 0.0)

    return pos, step, step_t, cum, decay, carried, tails, low


def pick(index, sources, target):
    for d, source in enumerate(sources):

        @pl.when(index == d)
        def _(source=source):
            target[...] = source[...]


def put(index, own, pair, across, value):
    low, high = pair.at[0:ROWS, :], pair.at[ROWS : 2 * ROWS, :]
    for d, target in enumerate((own, low, across, high)):

        @pl.when(index == d)
        def _(target=target):
            target[...] = value


def columns_kernel(
    me, w_in, tok, taps, bias, gain_in, seg, w0, w1, w2, w3a, w3b, out, rows, last
):
    g = me[0]
    for d, send in enumerate((w0, w1, w2, last)):
        start = (g ^ d) * XW
        send[:, :XW] = w_in[:, pl.ds(pl.multiple_of(start, 128), XW)]
        send[:, XW : 2 * XW] = w_in[:, pl.ds(pl.multiple_of(DI + start, 128), XW)]
        send[:, 2 * XW : XW + CL] = w_in[:, 2 * DI : DI + CW]
        send[:, XW + CL :] = jnp.concatenate(
            [w_in[:, DI + CW :], jnp.zeros((192, 128 - NH), bf16)], axis=1
        )
    w3a[...] = last[:, :CUT]
    w3b[...] = last[:, CUT:]
    out[0:ROWS, :] = tok[...]
    rows[...] = jnp.zeros_like(rows)
    rows[0:4, 0:448] = taps[...].astype(f32)
    rows[4:5, 0:448] = bias[...].astype(f32).reshape(1, 448)
    rows[5:6, 0:192] = gain_in[...].astype(f32).reshape(1, 192)
    rows[6:7, 0:ROWS] = seg[...].astype(f32)
    out[ROWS : ROWS + 16, :] = rows[...].astype(bf16)


def gather_short(g, parts, taps, gain_in, pos, wide, seg):
    for d, part in enumerate(parts):
        rows = part[ROWS : ROWS + 16, :].astype(f32)
        for k in range(4):

            @pl.when((g ^ d) == k)
            def _(k=k, rows=rows):
                wide[0:5, 448 * k : 448 * k + 448] = rows[0:5, 0:448]
                gain_in[:, 192 * k : 192 * k + 192] = rows[5:6, 0:192]
                seg[2 * k : 2 * k + 1, :] = rows[6:7, 0:128]
                seg[2 * k + 1 : 2 * k + 2, :] = rows[6:7, 128:256]

    taps[...] = jnp.zeros_like(taps)
    taps[0:5, 0:XW] = wide[0:5, pl.ds(pl.multiple_of(g * XW, 128), XW)]
    taps[0:5, XW:] = wide[0:5, DI:]
    ids = seg[...]
    row_at = lax.broadcasted_iota(jnp.int32, (8, 128), 0)
    lane_at = lax.broadcasted_iota(jnp.int32, (8, 128), 1)
    one = jnp.full((1, 128), -1.0, f32)
    earlier = jnp.concatenate([one, ids[0:7]], axis=0)
    later = jnp.concatenate([ids[1:8], one], axis=0)
    ends = jnp.broadcast_to(ids[:, 127:128], (8, 128))
    starts = jnp.broadcast_to(earlier[:, 127:128], (8, 128))
    features = [ids]
    for lag in range(1, 4):
        shifted = jnp.where(
            lane_at >= lag, pltpu.roll(ids, lag, 1), pltpu.roll(earlier, lag, 1)
        )
        features.append((shifted == ids).astype(f32))
    features += [(ids == starts).astype(f32), (ids == ends).astype(f32)]
    for lag in range(1, 4):
        shifted = jnp.where(
            lane_at < 128 - lag, pltpu.roll(ids, 128 - lag, 1), pltpu.roll(later, 128 - lag, 1)
        )
        features.append((shifted == ids).astype(f32))
    pos[...] = jnp.zeros_like(pos)
    for j, feature in enumerate(features):
        for n in range(8):
            pos[n, j : j + 1, :] = feature[n : n + 1, :]


def forward_kernel(
    me, t0, t1, t2, t3, w0, w1, w2, w3a, w3b, dtb, rate, skip,
    w_full, normed, proj, v_out, states, y_out, pos, taps, gain_in,
    tok, state, ext, wide, seg,
):
    i = pl.program_id(0)
    g = me[0]

    @pl.when(i == 0)
    def _():
        row_at = lax.broadcasted_iota(jnp.int32, (128, 128), 0)
        lane_at = lax.broadcasted_iota(jnp.int32, (128, 128), 1)
        chosen = ((row_at == lane_at + g * HL) & (lane_at < HL)).astype(bf16)
        for d, part in enumerate((w0, w1, w2)):
            rows = pl.ds(pl.multiple_of((g ^ d) * 192, 64), 192)
            w_full[rows, : XW + CL] = part[:, : XW + CL]
            w_full[rows, XW + CL :] = mm(part[:, XW + CL :], chosen, NN).astype(bf16)
        rows = pl.ds(pl.multiple_of((g ^ 3) * 192, 64), 192)
        w_full[rows, :CUT] = w3a[...]
        w_full[rows, CUT : XW + CL] = w3b[:, : XW + CL - CUT]
        w_full[rows, XW + CL :] = mm(w3b[:, XW + CL - CUT :], chosen, NN).astype(bf16)
        state[...] = jnp.zeros_like(state)
        ext[0:8, :] = jnp.zeros((8, CL), f32)
        gather_short(g, (t0, t1, t2, t3), taps, gain_in, pos, wide, seg)

    for d, source in enumerate((t0, t1, t2, t3)):

        @pl.when((g ^ i) == d)
        def _(source=source):
            tok[...] = source[0:ROWS, :]

    x = tok[...].astype(f32)
    rms = lax.rsqrt(jnp.mean(x * x, axis=-1, keepdims=True) + epsilon)
    low_rows = (x * rms * gain_in[...]).astype(bf16)
    normed[...] = low_rows
    proj[...] = mm(low_rows, w_full[...], NN).astype(bf16)
    ext[8 : 8 + ROWS, :] = proj[:, XW : XW + CL].astype(f32)
    found = []
    for s in range(ROWS // SPAN):
        at = s * SPAN
        dt_rows = proj[at : at + SPAN, XW + CL :].astype(f32) + dtb[...]
        found.append(span_decays(dt_rows, rate[...], pos[2 * i + s]))
    convs = []
    for s, (cols, *_) in enumerate(found):
        at = s * SPAN
        v = taps[4:5, :] + taps[3:4, :] * ext[8 + at : 8 + at + SPAN, :]
        for lag in range(1, 4):
            window = ext[8 + at - lag : 8 + at - lag + SPAN, :]
            v = v + (taps[3 - lag : 4 - lag, :] * cols[:, lag : lag + 1]) * window
        v_out[at : at + SPAN, :] = v
        convs.append(v * jax.nn.sigmoid(v))
    inners = []
    for conv, (_, _, step_t, _, decay, _, _, low) in zip(convs, found):
        scores = mm(conv[:, XW + NS :], conv[:, XW : XW + NS], NT)
        products = []
        for p in range(HL // 2):
            xp = conv[:, p * SPAN : (p + 1) * SPAN]
            mixing = [
                decay(h) * scores * step_t[h : h + 1, :] for h in (2 * p, 2 * p + 1)
            ]
            products.append(
                mm(
                    jnp.concatenate(mixing, axis=1),
                    jnp.concatenate([jnp.where(low, xp, 0.0), jnp.where(low, 0.0, xp)], axis=0),
                    NN,
                )
                + skip[:, p * SPAN : (p + 1) * SPAN] * xp
            )
        inners.append(jnp.concatenate(products, axis=1))
    for s, (conv, inner, (_, _, _, _, _, carried, tails, _)) in enumerate(
        zip(convs, inners, found)
    ):
        carried_all = jnp.concatenate(carried, axis=1)
        tails_all = jnp.concatenate(tails, axis=1)
        now = state[...]
        states[s] = now
        from_state = mm(conv[:, XW + NS :], now, NN)
        y_out[s * SPAN : (s + 1) * SPAN, :] = inner + carried_all * from_state
        fresh = mm(conv[:, XW : XW + NS], tails_all * conv[:, :XW], TN)
        state[...] = carried_all[SPAN - 1 :, :] * now + fresh
    ext[0:8, :] = ext[ROWS : ROWS + 8, :]


def sums_kernel(me, c0, c1, c2, c3, gate_in, y_in, gain_out, w_out, dno_out, stats, cot):
    i = pl.program_id(0)
    pick(me[0] ^ i, (c0, c1, c2, c3), cot)
    dno = mm(cot[...], w_out[...], NT)
    dno_out[...] = dno
    gate = gate_in[...].astype(f32)
    gated = y_in[...] * (gate * jax.nn.sigmoid(gate))
    squares = jnp.sum(gated * gated, axis=-1, keepdims=True)
    products = jnp.sum(gated * gain_out[...] * dno, axis=-1, keepdims=True)
    lane_at = lax.broadcasted_iota(jnp.int32, (SPAN, SPAN), 1)
    both = jnp.zeros((SPAN, SPAN), f32)
    for s in range(ROWS // SPAN):
        rows = slice(s * SPAN, (s + 1) * SPAN)
        both = jnp.where(lane_at == 2 * s, squares[rows], both)
        both = jnp.where(lane_at == 2 * s + 1, products[rows], both)
    stats[0] = both.T[0:8, :]


def branch_kernel(me, gate_in, y_in, gain_out, w_out, o_own, o_pair, o_across):
    gate = gate_in[...].astype(f32)
    gated = y_in[...] * (gate * jax.nn.sigmoid(gate)) * gain_out[...]
    value = mm(gated, w_out[...], NN).astype(bf16)
    put(me[0] ^ pl.program_id(0), o_own, o_pair, o_across, value)


def out_kernel(
    me, c0, c1, c2, c3, gate_in, y_in, dno_in, s0, s1, s2, s3, gain_out, normed,
    bundle, left, d_gate, dy_out, sums,
    cot, acc_out, acc_gate, acc_sum, normed_out,
):
    i = pl.program_id(0)
    g = me[0]

    @pl.when(i == 0)
    def _():
        for ref in (acc_out, acc_gate, acc_sum):
            ref[...] = jnp.zeros_like(ref)

    pick(g ^ i, (c0, c1, c2, c3), cot)
    totals = to_columns((s0[0] + s1[0]) + (s2[0] + s3[0]))
    for s in range(ROWS // SPAN):
        rows = slice(s * SPAN, (s + 1) * SPAN)
        rms = lax.rsqrt(totals[:, 2 * s : 2 * s + 1] * (1.0 / DI) + epsilon)
        mean = rms * rms * rms * totals[:, 2 * s + 1 : 2 * s + 2] * (1.0 / DI)
        gate = gate_in[rows, :].astype(f32)
        sig = jax.nn.sigmoid(gate)
        silu = gate * sig
        y = y_in[rows, :]
        gated = y * silu
        scaled = gated * rms
        normed_out[rows, :] = (scaled * gain_out[...]).astype(bf16)
        dno = dno_in[rows, :]
        acc_sum[0:1, :] += jnp.sum(dno * scaled, axis=0, keepdims=True)
        d_gated = rms * gain_out[...] * dno - gated * mean
        dy_out[rows, :] = d_gated * silu
        d_gate[rows, :] = (d_gated * y * (sig * (1.0 + gate * (1.0 - sig)))).astype(bf16)
    acc_out[...] += mm(normed_out[...], cot[...], TN)
    acc_gate[...] += mm(normed[...], d_gate[...], TN)

    @pl.when(i == pl.num_programs(0) - 1)
    def _():
        sums[...] = acc_sum[...]
        for k in range(4):
            for piece in range(36):
                tile, row = piece // 12, 192 * k + 16 * (piece % 12)
                value = acc_gate[row : row + 16, 128 * tile : 128 * tile + 128].astype(bf16)
                if piece < 32:
                    bundle[piece, 16 * k : 16 * k + 16, :] = value
                else:
                    left[4 * k + piece - 32] = value
        for piece in range(160):
            at = 64 + 16 * (piece % 5)
            tile, row = piece // 24, 16 * (piece % 24)
            if piece < 144:
                value = acc_out[row : row + 16, 128 * tile : 128 * tile + 128].astype(bf16)
            else:
                value = jnp.zeros((16, 128), bf16)
            bundle[piece // 5, at : at + 16, :] = value


def split_sum(rows, ones):
    high = rows.astype(bf16)
    rest = rows - high.astype(f32)
    return mm(high, ones, NN) + mm(rest, ones, NN)


def backward_block(
    w_full, normed, proj, v_in, states, dy_in, d_gate, pos, taps, dtb, rate, skip, ones,
    d_state, ext, acc_in, acc_dt, acc_small, d_proj,
):
    row_at = lax.broadcasted_iota(jnp.int32, (SPAN, SPAN), 0)
    lane_at = lax.broadcasted_iota(jnp.int32, (SPAN, SPAN), 1)
    later = (row_at <= lane_at).astype(f32)

    def add(row, value):
        width = value.shape[1]
        acc_small[row : row + 1, :width] += value

    def down(value):
        return jnp.sum(value, axis=0, keepdims=True)

    d_proj[:, :XW] = d_gate[...]
    found = {}
    for s in reversed(range(ROWS // SPAN)):
        rows = slice(s * SPAN, (s + 1) * SPAN)
        dt_rows = proj[rows, XW + CL :].astype(f32) + dtb[...]
        found[s] = (dt_rows,) + span_decays(dt_rows, rate[...], pos[s])
    inside = {}
    for s in reversed(range(ROWS // SPAN)):
        rows = slice(s * SPAN, (s + 1) * SPAN)
        dy = dy_in[rows, :]
        _, _, _, step_t, _, decay, carried, _, low = found[s]
        v = v_in[rows, :]
        sig_v = jax.nn.sigmoid(v)
        conv = v * sig_v
        x, b_rows, c_rows = conv[:, :XW], conv[:, XW : XW + NS], conv[:, XW + NS :]
        add(1, down(dy * x))
        scores = mm(c_rows, b_rows, NT)
        from_state = mm(c_rows, states[s], NN)
        d_scores = jnp.zeros((SPAN, SPAN), f32)
        row_sums = jnp.zeros((SPAN, SPAN), f32)
        col_sums, inners = [], []
        for p in range(HL // 2):
            lanes = slice(p * SPAN, (p + 1) * SPAN)
            xp, dyp = x[:, lanes], dy[:, lanes]
            halves = jnp.concatenate([jnp.where(low, dyp, 0.0), jnp.where(low, 0.0, dyp)], axis=0)
            d_mixing = mm(halves, xp, NT)
            mixing = []
            for k in range(2):
                h = 2 * p + k
                kept = decay(h)
                kept_step = kept * step_t[h : h + 1, :]
                mixing.append(kept_step * scores)
                d_mix = d_mixing[k * SPAN : (k + 1) * SPAN, :]
                d_scores = d_scores + d_mix * kept_step
                plain = d_mix * kept * scores
                col_sums.append(down(plain))
                row_sum = jnp.sum(plain * step_t[h : h + 1, :], axis=1, keepdims=True)
                row_sums = jnp.where(lane_at == h, row_sum, row_sums)
            inners.append(mm(jnp.concatenate(mixing, axis=0), halves, TN) + skip[:, lanes] * dyp)
        inner = jnp.concatenate(inners, axis=1)
        inside[s] = (v, sig_v, x, b_rows, c_rows, from_state, d_scores, row_sums, col_sums, inner)
    for s in reversed(range(ROWS // SPAN)):
        at = s * SPAN
        rows = slice(at, at + SPAN)
        dy = dy_in[rows, :]
        dt_rows, cols, step, _, cum, _, carried, tails, _ = found[s]
        v, sig_v, x, b_rows, c_rows, from_state, d_scores, row_sums, col_sums, inner = inside[s]
        state = states[s]
        state_grad = d_state[...]
        from_grad = mm(b_rows, state_grad, NN)
        carried_all = jnp.concatenate(carried, axis=1)
        tails_all = jnp.concatenate(tails, axis=1)
        dy_carried = dy * carried_all
        x_tail = x * tails_all
        dx = inner + tails_all * from_grad
        d_c = mm(d_scores, b_rows, NN) + mm(dy_carried, state, NT)
        d_b = mm(d_scores, c_rows, TN) + mm(x_tail, state_grad, NT)

        end_decay = carried_all[SPAN - 1 :, :]
        through = end_decay * down(state * state_grad)
        last = lax.broadcasted_iota(jnp.int32, (SPAN, XW), 0) == SPAN - 1
        from_start = split_sum(
            dy_carried * from_state + jnp.where(last, through, 0.0), ones[...]
        )
        to_end = split_sum(x * from_grad, ones[...])
        end_plain = jnp.exp(cum[SPAN - 1 :, :] - cum) * cols[:, 5:6]
        to_end_kept = to_end * end_plain
        to_end_step = to_end_kept * step
        col_sum = to_columns(jnp.concatenate(col_sums, axis=0))
        d_cum = row_sums - col_sum * step + from_start - to_end_step
        d_cum = d_cum + jnp.where(row_at == SPAN - 1, down(to_end_step), 0.0)
        d_log = mm_exact(later, d_cum, NN)
        d_step = col_sum + to_end_kept + rate[...] * d_log
        d_dt = d_step * jax.nn.sigmoid(dt_rows)
        add(2, down(d_dt))
        add(3, down(d_log * step) * rate[...])
        d_proj[rows, XW + CL :] = d_dt.astype(bf16)
        d_state[...] = end_decay * state_grad + mm(c_rows, dy_carried, TN)

        dv = jnp.concatenate([dx, d_b, d_c], axis=1) * (sig_v * (1.0 + v * (1.0 - sig_v)))
        ext[rows, :] = dv
        add(4, down(dv))
        conv_in = proj[rows, XW : XW + CL].astype(f32)
        add(8, down(dv * conv_in))
        d_conv = taps[3:4, :] * dv
        for lag in range(1, 4):
            window = ext[at + lag : at + lag + SPAN, :] * cols[:, 5 + lag : 6 + lag]
            d_conv = d_conv + taps[3 - lag : 4 - lag, :] * window
            add(8 - lag, down(window * conv_in))
        d_proj[rows, XW : XW + CL] = d_conv.astype(bf16)

    ext[ROWS:, :] = ext[0:8, :]
    d_normed = mm(d_proj[...], w_full[...], NT)
    add(9, down(d_normed * normed[...].astype(f32)))
    acc_in[...] += mm(normed[...], d_proj[:, XW : XW + CL], TN)
    acc_dt[...] += mm(d_proj[:, XW + CL :], normed[...], TN)[0:8, :]
    return d_normed.astype(bf16)


def backward_kernel(
    me, w_full, normed, proj, v_in, states, dy_in, d_gate, pos, taps, dtb, rate, skip, ones, sums, left,
    bundle, n_own, n_pair, n_across,
    d_state, ext, acc_in, acc_dt, acc_small, d_proj, small,
):
    i = pl.num_programs(0) - 1 - pl.program_id(0)
    g = me[0]

    @pl.when(pl.program_id(0) == 0)
    def _():
        for ref in (d_state, acc_in, acc_dt, acc_small, small):
            ref[...] = jnp.zeros_like(ref)
        ext[ROWS:, :] = jnp.zeros((8, CL), f32)

    value = backward_block(
        w_full, normed, proj, v_in, states, dy_in, d_gate, pos, taps, dtb, rate, skip, ones,
        d_state, ext, acc_in, acc_dt, acc_small, d_proj,
    )
    put(g ^ i, n_own, n_pair, n_across, value)

    @pl.when(i == 0)
    def _():
        def lay(start, source, row, tiles):
            for k in range(4):
                for t in range(tiles):
                    small[k, start + t : start + t + 1, :] = source[
                        row : row + 1, 128 * t : 128 * t + 128
                    ]

        for j in range(4):
            lay(16 + 5 * j, acc_small, 5 + j, 5)
        lay(36, acc_small, 4, 5)
        lay(43, sums, 0, 3)
        lay(46, acc_small, 1, 3)
        lay(49, acc_small, 2, 1)
        lay(50, acc_small, 3, 1)
        for k in range(4):
            for piece in range(64):
                at = 32 * k + 16 * (piece % 2)
                tile, row = piece // 12, 192 * k + 16 * (piece % 12)
                if piece < 60:
                    value = acc_in[row : row + 16, 128 * tile : 128 * tile + 128].astype(bf16)
                else:
                    value = left[4 * k + piece - 60]
                bundle[piece // 2, at : at + 16, :] = value
            first, second = 192 * k, 192 * k + 128
            for h in range(HL):
                small[k, 2 * h : 2 * h + 1, :] = acc_dt[h : h + 1, first : first + 128]
                small[k, 2 * h + 1 : 2 * h + 2, 0:64] = acc_dt[h : h + 1, second : second + 64]
            small[k, 41:42, :] = acc_small[9:10, first : first + 128]
            small[k, 42:43, 0:64] = acc_small[9:10, second : second + 64]
        for r in range(32):
            if r < 16:
                value = jnp.concatenate([small[k, 4 * r : 4 * r + 4, :] for k in range(4)], axis=0)
            else:
                value = jnp.zeros((16, 128), f32)
            bundle[r, 128:144, :] = value.astype(bf16)


def assemble_kernel(
    me, parts, gain_in,
    grad_in, grad_out, grad_kernel, grad_bias, grad_gain_in, grad_gain_out, grad_skip, grad_dt,
    grad_log,
    wide, turned, shorts,
):
    g = me[0]
    for r in range(32):
        chunks = [parts[32 * k + r].astype(f32) for k in range(4)]
        pieces = [(0, r)]
        for n in (2 * r, 2 * r + 1):
            pieces.append((16 + 16 * (n % 2), 36 + n if n < 60 else n - 28))
        for at, piece in pieces:
            tile, row = piece // 12, 16 * (piece % 12)
            values = [chunk[at : at + 16] for chunk in chunks]
            if tile < 6:
                for k in range(4):
                    start = (tile // 3) * DI + k * XW + (tile % 3) * 128
                    grad_in[row : row + 16, start : start + 128] = values[k]
            else:
                start = 2 * DI + 128 * (tile - 6)
                grad_in[row : row + 16, start : start + 128] = (values[0] + values[1]) + (
                    values[2] + values[3]
                )
        for k in range(4):
            done = 0
            while done < 20:
                piece, inside = divmod(20 * k + done, 16)
                piece += 5 * r
                count = min(20 - done, 16 - inside)
                if piece < 144:
                    row, column = 16 * (piece % 24) + inside, 128 * (piece // 24)
                    grad_out[row : row + count, column : column + 128] = chunks[k][
                        48 + done : 48 + done + count
                    ]
                done += count
            if r < 16:
                shorts[k, 4 * r : 4 * r + 4, :] = chunks[k][68:72]

    turned[...] = jnp.zeros_like(turned)
    wide[...] = jnp.zeros_like(wide)
    gain = jnp.zeros((2, 128), f32)
    for k in range(4):
        rest = shorts[k]
        for h in range(HL):
            at = HL * k + h
            turned[at : at + 1, 0:128] = rest[2 * h : 2 * h + 1, :]
            turned[at : at + 1, 128:256] = rest[2 * h + 1 : 2 * h + 2, :]
        for j in range(5):
            for t in range(3):
                lanes = slice(k * XW + 128 * t, k * XW + 128 * t + 128)
                wide[j : j + 1, lanes] = rest[16 + 5 * j + t : 17 + 5 * j + t, :]
            for t in range(3, 5):
                lanes = slice(DI + 128 * (t - 3), DI + 128 * (t - 2))
                wide[j : j + 1, lanes] += rest[16 + 5 * j + t : 17 + 5 * j + t, :]
        gain = gain + rest[41:43, :]
    grad_in[:, DI + CW :] = turned[...].T[0:192, 0:NH]
    grad_gain_in[:, 0:128] = gain[0:1, :] / gain_in[:, 0:128]
    grad_gain_in[:, 128:192] = gain[1:2, 0:64] / gain_in[:, 128:192]
    for k in range(4):

        @pl.when(g == k)
        def _(k=k):
            grad_kernel[...] = wide[0:4, 448 * k : 448 * k + 448]
            grad_bias[...] = wide[4:5, 448 * k : 448 * k + 448]

    own = shorts[g]
    grad_gain_out[...] = jnp.concatenate([own[43 + t : 44 + t, :] for t in range(3)], axis=1).reshape(XW)
    lane_at = lax.broadcasted_iota(jnp.int32, (1, 128), 1)
    skips = jnp.zeros((1, 128), f32)
    for t in range(3):
        row = own[46 + t : 47 + t, :]
        first = jnp.sum(jnp.where(lane_at < HP, row, 0.0), axis=1, keepdims=True)
        second = jnp.sum(jnp.where(lane_at < HP, 0.0, row), axis=1, keepdims=True)
        skips = jnp.where(lane_at == 2 * t, first, skips)
        skips = jnp.where(lane_at == 2 * t + 1, second, skips)
    grad_skip[...] = skips[:, 0:HL]
    grad_dt[...] = own[49:50, 0:HL]
    grad_log[...] = own[50:51, 0:HL]


def whole(shape):
    zeros = (0,) * len(shape)
    return pl.BlockSpec(shape, lambda i: zeros)


def blocked(shape, place):
    zeros = (0,) * (len(shape) - 1)
    return pl.BlockSpec(shape, lambda i: (place(i),) + zeros)


scalar_spec = pl.BlockSpec(memory_space=pltpu.SMEM)
vmem_spec = pl.BlockSpec(memory_space=pltpu.VMEM)


def shape(dims, dtype):
    return jax.ShapeDtypeStruct(dims, dtype)


def call(body, name, micros, **kwargs):
    return pl.pallas_call(
        body,
        name=name,
        compiler_params=pltpu.CompilerParams(vmem_limit_bytes=vmem_bytes),
        cost_estimate=pl.CostEstimate(
            flops=int(micros * 1e9), bytes_accessed=1 << 20, transcendentals=0
        ),
        **kwargs,
    )


def among(value, d):
    return lax.ppermute(value, "group", [(i, i ^ d) for i in range(4)])


def local(
    tokens, segments, cotangent, gain_in, w_in, kernel, conv_bias, dt_bias, a_log, skip_gain,
    gain_out, w_out,
):
    reps = lax.axis_size("rep")
    g = lax.axis_index("group")
    me = g.astype(jnp.int32).reshape(1)
    tok = tokens.reshape(ROWS, D)
    cot = cotangent.reshape(ROWS, D)
    part = whole((ROWS, D))
    blocks = 4

    w0, w1, w2, w3a, w3b, both0 = call(
        columns_kernel,
        "columns",
        2,
        in_specs=[scalar_spec] + [vmem_spec] * 6,
        out_specs=[vmem_spec] * 6,
        out_shape=(shape((192, PW), bf16),) * 3
        + (shape((192, CUT), bf16), shape((192, PW - CUT), bf16), shape((ROWS + 16, D), bf16)),
        scratch_shapes=[pltpu.VMEM((16, D), f32), pltpu.VMEM((192, PW), bf16)],
    )(
        me, w_in, tok, kernel, conv_bias, gain_in,
        segments.reshape(1, ROWS),
    )

    def across(value, d):
        pairs = [(i * reps + r, (i ^ d) * reps + (r ^ 1)) for r in range(reps) for i in range(4)]
        return lax.ppermute(value, ("group", "rep"), pairs)

    w2 = across(w2, 2)
    both2 = among(both0, 2)
    w3b = across(w3b, 3)
    w3a = among(w3a, 3)
    both2, both0, cot_late, w1 = lax.optimization_barrier((both2, both0, cot, w1))
    w1 = among(w1, 1)
    both1 = among(both0, 1)
    both3 = among(both2, 1)
    c2 = among(cot_late, 2)
    c1 = among(cot_late, 1)
    c3 = among(cot_late, 3)
    length = blocks * ROWS
    spans = length // SPAN

    dtb = jnp.pad(dt_bias.astype(f32), (0, 128 - HL)).reshape(1, 128)
    rate = jnp.pad(-jnp.exp(a_log.astype(f32)), (0, 128 - HL)).reshape(1, 128)
    skip = jnp.repeat(skip_gain.astype(f32), HP).reshape(1, XW)
    gain_o = gain_out.astype(f32).reshape(1, XW)

    def up(i):
        return i

    by_owner_specs = [part, whole((2 * ROWS, D)), part]
    by_owner_shapes = tuple(shape((n * ROWS, D), bf16) for n in (1, 2, 1))

    def to_core(own, pair, over):
        got = among(pair, 1)
        other = (over.astype(f32) + got[ROWS:].astype(f32)).astype(bf16)
        return own, got[:ROWS], other

    def to_owner(own, got, other):
        return own, got, among(other, 2)

    w_full, normed, proj, v_rows, states, y_rows, pos, taps, gain_in_all = call(
        forward_kernel,
        "forward",
        15,
        grid=(blocks,),
        in_specs=[scalar_spec]
        + [whole((ROWS + 16, D))] * 4
        + [whole((192, PW))] * 3
        + [whole((192, CUT)), whole((192, PW - CUT))]
        + [whole((1, 128)), whole((1, 128)), whole((1, XW))],
        out_specs=[
            whole((D, PW)),
            blocked((ROWS, D), up),
            blocked((ROWS, PW), up),
            blocked((ROWS, CL), up),
            blocked((2, NS, XW), up),
            blocked((ROWS, XW), up),
            whole((8, 16, SPAN)),
            whole((8, CL)),
            whole((1, D)),
        ],
        out_shape=(
            shape((D, PW), bf16),
            shape((length, D), bf16),
            shape((length, PW), bf16),
            shape((length, CL), f32),
            shape((spans, NS, XW), f32),
            shape((length, XW), f32),
            shape((spans, 16, SPAN), f32),
            shape((8, CL), f32),
            shape((1, D), f32),
        ),
        scratch_shapes=[
            pltpu.VMEM((ROWS, D), bf16),
            pltpu.VMEM((NS, XW), f32),
            pltpu.VMEM((ROWS + 8, CL), f32),
            pltpu.VMEM((8, CW), f32),
            pltpu.VMEM((8, 128), f32),
        ],
    )(
        me, both0, both1, both2, both3, w0, w1, w2, w3a, w3b, dtb, rate, skip,
    )

    gate_spec = pl.BlockSpec((ROWS, XW), lambda i: (i, 0))
    dno, stats = call(
        sums_kernel,
        "sums",
        4,
        grid=(blocks,),
        in_specs=[scalar_spec]
        + [part] * 4
        + [gate_spec, blocked((ROWS, XW), up), whole((1, XW)), whole((XW, D))],
        out_specs=[blocked((ROWS, XW), up), blocked((1, 8, SPAN), up)],
        out_shape=(shape((length, XW), f32), shape((blocks, 8, SPAN), f32)),
        scratch_shapes=[pltpu.VMEM((ROWS, D), bf16)],
    )(me, cot, c1, c2, c3, proj, y_rows, gain_o, w_out)
    all_stats = [stats] + [among(stats, d) for d in range(1, 4)]

    o_parts = call(
        branch_kernel,
        "branch",
        3,
        grid=(blocks,),
        in_specs=[
            scalar_spec, gate_spec, blocked((ROWS, XW), up), whole((1, XW)), whole((XW, D)),
        ],
        out_specs=by_owner_specs,
        out_shape=by_owner_shapes,
    )(me, proj, y_rows, gain_o, w_out)
    o_parts, all_stats = lax.optimization_barrier((o_parts, all_stats))

    bundle1, left, d_gate, dy, sums = call(
        out_kernel,
        "out",
        6,
        grid=(blocks,),
        in_specs=[scalar_spec]
        + [part] * 4
        + [gate_spec, blocked((ROWS, XW), up), blocked((ROWS, XW), up)]
        + [blocked((1, 8, SPAN), up)] * 4
        + [whole((1, XW)), blocked((ROWS, D), up)],
        out_specs=[
            whole((32, 144, 128)), whole((16, 16, 128)), blocked((ROWS, XW), up), blocked((ROWS, XW), up), whole((8, XW)),
        ],
        out_shape=(
            shape((32, 144, 128), bf16), shape((16, 16, 128), bf16),
            shape((length, XW), bf16), shape((length, XW), f32),
            shape((8, XW), f32),
        ),
        scratch_shapes=[
            pltpu.VMEM((ROWS, D), bf16),
            pltpu.VMEM((XW, D), f32),
            pltpu.VMEM((D, XW), f32),
            pltpu.VMEM((8, XW), f32),
            pltpu.VMEM((ROWS, XW), bf16),
        ],
    )(me, cot, c1, c2, c3, proj, y_rows, dno, *all_stats, gain_o, normed)

    def spread(value):
        return lax.all_to_all(value, "rep", 0, 0, tiled=True)

    received1 = spread(bundle1)
    branches = to_core(*o_parts)
    dy, branches = lax.optimization_barrier((dy, branches))
    branches = to_owner(*branches)
    ones = jnp.asarray(np.arange(XW)[:, None] // HP == np.arange(128)[None, :], bf16)

    def back(i):
        return blocks - 1 - i

    bundle2, *n_parts = call(
        backward_kernel,
        "backward",
        26,
        grid=(blocks,),
        in_specs=[
            scalar_spec,
            whole((D, PW)),
            blocked((ROWS, D), back),
            blocked((ROWS, PW), back),
            blocked((ROWS, CL), back),
            blocked((2, NS, XW), back),
            blocked((ROWS, XW), back),
            blocked((ROWS, XW), back),
            blocked((2, 16, SPAN), back),
            whole((8, CL)), whole((1, 128)), whole((1, 128)), whole((1, XW)), whole((XW, 128)),
            whole((8, XW)),
            whole((16, 16, 128)),
        ],
        out_specs=[whole((32, 144, 128))] + by_owner_specs,
        out_shape=(shape((32, 144, 128), bf16),) + by_owner_shapes,
        scratch_shapes=[
            pltpu.VMEM((NS, XW), f32),
            pltpu.VMEM((ROWS + 8, CL), f32),
            pltpu.VMEM((D, CL), f32),
            pltpu.VMEM((8, D), f32),
            pltpu.VMEM((16, D), f32),
            pltpu.VMEM((ROWS, PW), bf16),
            pltpu.VMEM((4, 64, 128), f32),
        ],
    )(
        me, w_full, normed, proj, v_rows, states, dy, d_gate, pos, taps, dtb, rate, skip, ones,
        sums, left,
    )

    def total(received):
        return jnp.sum(received.astype(f32), axis=0).astype(bf16)

    bundle2, received1, branches = lax.optimization_barrier((bundle2, received1, branches))
    received2 = spread(bundle2)
    d_parts = to_core(*n_parts)
    reduced1 = total(received1)
    by_member = reduced1[64:].reshape(4, 20, 128)
    turns = [lax.dynamic_index_in_dim(by_member, g ^ d, 0, keepdims=False) for d in range(4)]
    turns = jnp.stack([turns[0]] + [among(turns[d], d) for d in range(1, 4)])
    outs = jnp.stack([lax.dynamic_index_in_dim(turns, g ^ k, 0, keepdims=False) for k in range(4)])
    first = reduced1[:64].reshape(4, 16, 128)
    reduced2, outs, first, d_parts = lax.optimization_barrier(
        (total(received2), outs, first, d_parts)
    )
    d_parts = to_owner(*d_parts)
    payload = jnp.concatenate(
        [
            first,
            reduced2[:128].reshape(4, 32, 128),
            outs,
            reduced2[128:].reshape(4, 4, 128),
        ],
        axis=1,
    )
    parts = lax.all_to_all(
        jnp.broadcast_to(payload[:, None], (4, reps, 72, 128)).reshape(4 * reps, 72, 128),
        ("group", "rep"), 0, 0, tiled=True,
    )

    x = tok.astype(f32)
    branch = sum(value.astype(f32) for value in branches)
    squares = sum(lax.dynamic_index_in_dim(v, g, 0, keepdims=False) for v in all_stats)
    rms_out = lax.rsqrt(squares[0:4:2].reshape(ROWS, 1) * (1.0 / DI) + epsilon)
    layer_out = (x + rms_out * branch).astype(bf16).reshape(tokens.shape)
    grads = call(
        assemble_kernel,
        "assemble",
        4,
        in_specs=[scalar_spec] + [vmem_spec] * 2,
        out_specs=[vmem_spec] * 9,
        out_shape=(
            shape((192, 3352), f32), shape((XW, D), f32), shape((4, 448), f32),
            shape((1, 448), f32), shape((1, 192), f32), shape((XW,), f32), shape((1, HL), f32),
            shape((1, HL), f32), shape((1, HL), f32),
        ),
        scratch_shapes=[
            pltpu.VMEM((8, CW), f32),
            pltpu.VMEM((128, 256), f32),
            pltpu.VMEM((4, 64, 128), f32),
        ],
    )(me, parts, gain_in.astype(f32).reshape(1, 192))
    grads, d_parts = lax.optimization_barrier((grads, d_parts))
    d_normed = sum(value.astype(f32) for value in d_parts)
    rms_in = lax.rsqrt(jnp.mean(x * x, axis=-1, keepdims=True) + epsilon)
    scaled = d_normed * gain_in_all
    grad_tokens = (
        cot.astype(f32)
        + rms_in * scaled
        - x * (rms_in * rms_in * rms_in * jnp.mean(x * scaled, axis=-1, keepdims=True))
    ).reshape(tokens.shape)
    grad_w_in, grad_w_out, grad_kernel, grad_bias, grad_gi, grad_go, grad_s, grad_d, grad_l = grads
    return (
        layer_out,
        grad_tokens,
        grad_gi.reshape(-1),
        grad_w_in,
        grad_kernel,
        grad_bias.reshape(-1),
        grad_d.reshape(-1),
        grad_l.reshape(-1),
        grad_s.reshape(-1),
        grad_go,
        grad_w_out,
    )


def solution(mesh):
    sequences = P("rep", "group", None)
    vector = P("group")
    matrix = P("group", None)
    return jax.shard_map(
        local,
        mesh=mesh,
        in_specs=(
            sequences, P("rep", "group"), sequences, vector, matrix, P(None, "group"),
            vector, vector, vector, vector, vector, matrix,
        ),
        out_specs=(
            sequences, sequences, vector, matrix, P(None, "group"), vector, vector, vector,
            vector, vector, matrix,
        ),
        check_vma=False,
    )
```
